32 devices in a mesh: gx: 4 (over z), gy: 4 (over y, core), gz: 2 (over x).
Axes of the slice: x: 2, y: 2, z: 4, core: 2. Of those that a mesh axis runs over, the one named last changes fastest.
Arguments:
- patch_state: float32 [4, 2, 32, 5, 1024], P('gx', 'gz', 'gy'), as said below
- coarse_boxes: float32 [8, 5, 4096], P(('gx', 'gz')), as said below
- new_owner: int32 [4, 2, 32, 1], P('gx', 'gz'), may hold values from 0 to 3; in each aligned block of 8 rows (0 to 7, 8 to 15, ..., all dimensions but the last counted through in order) at most 4 rows name the same one
- neighbors: int32 [4, 2, 32, 4], P('gx', 'gz'), may hold values from -1 to 31, as said below
- coarse_box: int32 [4, 2, 32, 4], P('gx', 'gz'), may hold values from 0 to 7
- coarse_start: int32 [4, 2, 32, 4], P('gx', 'gz'), may hold values from 0 to 3135
Outputs:
- advanced: float32 [4, 2, 64, 5, 1024], P('gx', 'gz', 'gy')
The draws below stay inside these ranges and needn't reach their ends.
Inputs may be any that keep to these rules, and one draw needn't show every extreme that they name: `new_owner`: no device hands more than 4 of its patches to one new owner. `neighbors`: a patch of the same group by its number before redistribution, or -1 where the side borders the coarse level. `patch_state`: density and pressure positive. `coarse_boxes`: density and pressure positive.
All inputs are finite; a program needn't handle non-finite values.
Results may differ from the reference program's by a relative error of at most 0.0003.
Values sent between devices are 32-bit elements; how exact they have to be, the bound alone decides.
No kernel may reach another device: no remote copies, remote signals or barrier semaphores. Data moves between devices by JAX's collectives and lax.ppermute only.
A program may use at most 64 MiB of HBM per device.

```python
import math
import jax
import jax.numpy as jnp
import numpy as np
from jax import lax

FIELDS = 5
PX = 32
BOX = 64
P_DEV = 8
CAP = 4
SLOTS = 16
NPATCH = 32
NBOX = 8
N_GX = 4
N_GY = 4
N_GZ = 2


def euler_cells(key, leading, cells, temper_top, motion, heated):
    keys = jax.random.split(key, 6)
    density = jnp.exp(jax.random.uniform(keys[0], leading + (cells,), jnp.float32, jnp.log(0.5), jnp.log(2.0)))
    temper = jnp.exp(jax.random.uniform(keys[1], leading + (1,), jnp.float32, 0.0, jnp.log(temper_top)))
    if heated:
        total = 1
        for extent in leading:
            total = total * extent
        hottest = jax.random.randint(keys[4], (), 0, total)
        boost = jnp.exp(jax.random.uniform(keys[5], (), jnp.float32, jnp.log(2.0), jnp.log(16.0)))
        marked = (jnp.arange(total, dtype=jnp.int32) == hottest).reshape(leading + (1,))
        temper = jnp.where(marked, temper_top * boost, temper)
    rough = jnp.exp(jax.random.uniform(keys[2], leading + (cells,), jnp.float32, jnp.log(0.7), jnp.log(1.4)))
    pressure = density * temper * rough
    velocity = motion * jnp.sqrt(temper)[..., None, :] * jnp.clip(jax.random.normal(keys[3], leading + (3, cells), jnp.float32), -3.0, 3.0)
    momentum = density[..., None, :] * velocity
    energy = pressure / 0.4 + 0.5 * density * jnp.sum(velocity * velocity, axis=-2)
    return jnp.concatenate([density[..., None, :], momentum, energy[..., None, :]], axis=-2)


def draw_patch_state(key, part):
    return euler_cells(key, (N_GX, N_GZ, NPATCH), PX * PX, 16.0, 0.5, True)


def draw_coarse_boxes(key, part):
    return euler_cells(key, (NBOX,), BOX * BOX, 16.0, 0.5, False)


def draw_neighbors(key, part):
    keys = jax.random.split(jax.random.fold_in(key, 17), 2)
    scores = jax.random.randint(keys[0], (N_GX, N_GZ, 4, NPATCH), 0, 1 << 20) * NPATCH + jnp.arange(NPATCH, dtype=jnp.int32)
    ids = jnp.swapaxes(jnp.argsort(scores, axis=-1).astype(jnp.int32), -1, -2)
    coarse_side = jax.random.randint(keys[1], (N_GX, N_GZ, NPATCH, 4), 0, 4) == 0
    forced = jnp.zeros((NPATCH, 4), jnp.bool_).at[0, 0].set(True).at[1, 0].set(True)
    coarse_side = (coarse_side | forced) & (ids != NPATCH - 1)
    return jnp.where(coarse_side, -1, ids)


def with_ends(entries, stream_key, smallest, high):
    shape = entries.shape
    place = [jax.random.randint(jax.random.fold_in(stream_key, axis), (), 0, shape[axis]) for axis in range(len(shape))]
    entries = entries.at[tuple(place)].set(smallest)
    longest = shape.index(max(shape))
    place[longest] = (place[longest] + 1) % shape[longest]
    return entries.at[tuple(place)].set(high)


def rank_bounds(amount, lean):
    portions = [(1 << 20) // math.isqrt(grade ** lean) + 1 for grade in range(1, amount + 1)]
    width = 1 + sum(portions) // (1 << 30)
    return np.cumsum(np.array([max(1, weight // width) for weight in portions]))


def skewed_ids(key, dims, amount, slope):
    listing = rank_bounds(amount, slope)
    ticket = jax.random.randint(jax.random.fold_in(key, 1), dims, 0, int(listing[amount - 1]))
    rank = jnp.searchsorted(jnp.asarray(listing, jnp.int32), ticket, side="right")
    return jax.random.permutation(jax.random.fold_in(key, 2), amount)[rank].astype(jnp.int32)


def routed_block(rng, own, number, rows, number_of, top, reach, skew):
    order = jax.random.permutation(rng, number_of)
    packed, ordinary = portions_of(number_of, rows * top, reach, skew, True), portions_of(number_of, rows * top, reach, skew, False)
    places = jnp.arange(number_of)

    def named(sizes, turn):
        used = int((sizes > 0).sum())
        fixed = max(1, used // 4)
        passed = fixed + (places - fixed + turn * (used - fixed)) % max(1, number_of - fixed)
        return jnp.zeros((number_of,), jnp.int32).at[order[jnp.where(places < fixed, places, passed)]].set(jnp.asarray(sizes, jnp.int32))

    sizes = jnp.where(number % 4 == 0, named(packed, number // 4), named(ordinary, number - number // 4 - 1))
    mixed = jax.random.permutation(jax.random.fold_in(own, 3), number_of)
    donor, taker = mixed[0:number_of // 2 * 2:2], mixed[1:number_of // 2 * 2:2]
    room = jnp.minimum(sizes[donor] - 1, reach - sizes[taker]) // 2
    room = jnp.where((donor == order[0]) | (taker == order[0]) | (sizes[taker] == 0), 0, jnp.maximum(room, 0))
    passed = jax.random.randint(jax.random.fold_in(own, 4), (number_of // 2,), 0, 1 << 20) % (room + 1)
    sizes = sizes.at[donor].add(-passed).at[taker].add(passed)
    items = jnp.searchsorted(jnp.cumsum(sizes), jnp.arange(rows * top), side="right").astype(jnp.int32)
    listing = items.reshape(top, rows).T
    listing = listing[jax.random.permutation(jax.random.fold_in(own, 1), rows)]
    turn = jax.random.randint(jax.random.fold_in(own, 2), (rows, 1), 0, top)
    return jnp.take_along_axis(listing, (jnp.arange(top)[None, :] + turn) % top, axis=1)


def portions_of(amount, total, most, skew, full):
    weights = [(1 << 20) // math.isqrt(grade ** skew) + 1 for grade in range(1, amount + 1)]
    largest = most if full else min(most, max(-(-total // amount), total * weights[0] // sum(weights)))
    least = 1 if total - largest >= amount - 1 else 0
    counts, spare = [largest] + [least] * (amount - 1), total - largest - least * (amount - 1)
    while spare > 0:
        movable = [i for i in range(1, amount) if counts[i] < largest] or [i for i in range(1, amount) if counts[i] < most]
        whole, budget = sum([weights[i] for i in movable]), spare
        for i in movable:
            addition = min(most - counts[i], max(1, budget * weights[i] // whole), spare)
            counts[i] = counts[i] + addition
            spare = spare - addition
    return np.array(counts)


def setup_inputs(seed: int = 0) -> dict:
    streams_of = jax.random.split(jax.random.key(seed), 7)
    patch_state = draw_patch_state(jax.random.fold_in(streams_of[6], 71), 0)
    coarse_boxes = draw_coarse_boxes(jax.random.fold_in(streams_of[6], 71), 0)
    new_owner_keys = jax.random.split(jax.random.fold_in(streams_of[2], 1), N_GX * N_GZ * NPATCH // P_DEV)
    new_owner_turns = jax.random.permutation(jax.random.fold_in(streams_of[2], 3), N_GX * N_GZ * NPATCH // P_DEV)
    new_owner = jax.vmap(lambda own, number: routed_block(jax.random.fold_in(streams_of[2], 2), own, number, P_DEV, N_GY, 1, CAP, 2))(new_owner_keys, new_owner_turns).reshape((N_GX, N_GZ, NPATCH, 1))
    neighbors = draw_neighbors(jax.random.fold_in(streams_of[6], 71), 0)
    coarse_box = with_ends(skewed_ids(streams_of[4], (N_GX, N_GZ, NPATCH, 4), NBOX, 2), jax.random.fold_in(streams_of[4], 3), 0, NBOX - 1).astype(jnp.int32)
    coarse_start = with_ends(jax.random.randint(streams_of[5], (N_GX, N_GZ, NPATCH, 4), 0, BOX * (BOX - PX // 2 + 1)), jax.random.fold_in(streams_of[5], 1), 0, (BOX * (BOX - PX // 2 + 1)) - 1).astype(jnp.int32)
    return {"patch_state": patch_state, "coarse_boxes": coarse_boxes, "new_owner": new_owner, "neighbors": neighbors, "coarse_box": coarse_box, "coarse_start": coarse_start}


heat_ratio = 1.4
courant = 0.3
OPPOSITE = (1, 0, 3, 2)

def primitive(current):
    density = current[..., 0, :]
    speed_x = current[..., 1, :] / density
    speed_y = current[..., 2, :] / density
    speed_z = current[..., 3, :] / density
    kinetic = 0.5 * density * (speed_x * speed_x + speed_y * speed_y + speed_z * speed_z)
    pressure = (heat_ratio - 1.0) * (current[..., 4, :] - kinetic)
    sound = jnp.sqrt(heat_ratio * pressure / density)
    return (speed_x, speed_y, pressure, sound)

def physical_flux(current, normal):
    speed_x, speed_y, pressure, sound = primitive(current)
    moving = speed_x if normal == 1 else speed_y
    carried = current * moving[..., None, :]
    extra = [jnp.zeros_like(pressure)] * 5
    extra[normal] = pressure
    extra[4] = pressure * moving
    return (carried + jnp.stack(extra, axis=-2), jnp.abs(moving) + sound)

def rusanov(left_cells, right_cells, normal):
    flux_left, wave_left = physical_flux(left_cells, normal)
    flux_right, wave_right = physical_flux(right_cells, normal)
    fastest = jnp.maximum(wave_left, wave_right)
    return 0.5 * (flux_left + flux_right) - 0.5 * fastest[..., None, :] * (right_cells - left_cells)

def tendency(current, ghost):
    position = jnp.arange(PX * PX, dtype=jnp.int32)
    col_index = position % PX
    row_index = position // PX
    repeats = (1,) * (ghost.ndim - 2) + (PX,)
    west = jnp.repeat(ghost[..., 0, :, :], PX, axis=-1)
    east = jnp.repeat(ghost[..., 1, :, :], PX, axis=-1)
    south = jnp.tile(ghost[..., 2, :, :], repeats)
    north = jnp.tile(ghost[..., 3, :, :], repeats)
    left_cells = jnp.where(col_index == 0, west, jnp.roll(current, 1, axis=-1))
    west_flux = rusanov(left_cells, current, 1)
    east_flux = jnp.where(col_index == PX - 1, rusanov(current, east, 1), jnp.roll(west_flux, -1, axis=-1))
    below = jnp.where(row_index == 0, south, jnp.roll(current, PX, axis=-1))
    south_flux = rusanov(below, current, 2)
    north_flux = jnp.where(row_index == PX - 1, rusanov(current, north, 2), jnp.roll(south_flux, -PX, axis=-1))
    return west_flux - east_flux + (south_flux - north_flux)

def edge_rows(current):
    grid = current.reshape(current.shape[:-1] + (PX, PX))
    return jnp.stack([grid[..., :, 0], grid[..., :, PX - 1], grid[..., 0, :], grid[..., PX - 1, :]], axis=-3)

def wave_top(current):
    speed_x, speed_y, pressure, sound = primitive(current)
    return jnp.maximum(jnp.abs(speed_x), jnp.abs(speed_y)) + sound

def coarse_strips(coarse_boxes, box_ids, starts):
    half = PX // 2
    stride = BOX - half + 1
    row_start = starts // stride * BOX + starts % stride
    cells = row_start[..., None] + jnp.arange(half, dtype=jnp.int32)
    fields = jnp.arange(FIELDS, dtype=jnp.int32)
    picked = coarse_boxes[box_ids[..., None, None], fields[:, None], cells[..., None, :]]
    return jnp.repeat(picked, 2, axis=-1)

def reference(patch_state, coarse_boxes, new_owner, neighbors, coarse_box, coarse_start):
    time_step = courant / jnp.max(wave_top(patch_state))
    numbers = jnp.arange(NPATCH, dtype=jnp.int32)
    source = numbers // P_DEV

    def group_step(inputs):
        current, neighbor_ids, box_ids, starts, owner_plan = inputs
        coarse = coarse_strips(coarse_boxes, box_ids, starts)
        fine_side = (neighbor_ids >= 0)[:, :, None, None]
        safe_ids = jnp.maximum(neighbor_ids, 0)

        def ghosts(values):
            picked = edge_rows(values)[safe_ids]
            facing = jnp.stack([picked[:, side, OPPOSITE[side]] for side in range(4)], axis=1)
            return jnp.where(fine_side, facing, coarse)
        section_one = current + time_step * tendency(current, ghosts(current))
        section_two = section_one + time_step * tendency(section_one, ghosts(section_one))
        stepped = 0.5 * current + 0.5 * section_two
        owner = owner_plan[:, 0]
        same = (owner[:, None] == owner[None, :]) & (source[:, None] == source[None, :]) & (numbers[:, None] > numbers[None, :])
        slot_rank = lax.optimization_barrier(jnp.sum(same.astype(jnp.int32), axis=1))
        target = owner * SLOTS + source * CAP + slot_rank
        placed = jnp.zeros((N_GY * SLOTS, FIELDS, PX * PX), jnp.float32)
        return placed.at[target].set(stepped)
    groups = N_GX * N_GZ
    flat = (patch_state.reshape((groups, NPATCH, FIELDS, PX * PX)), neighbors.reshape((groups, NPATCH, 4)), coarse_box.reshape((groups, NPATCH, 4)), coarse_start.reshape((groups, NPATCH, 4)), new_owner.reshape((groups, NPATCH, 1)))
    results = lax.map(group_step, flat)
    return results.reshape((N_GX, N_GZ, N_GY * SLOTS, FIELDS, PX * PX))
```

```python
import functools

import jax
import jax.numpy as jnp
from jax import lax
from jax.experimental import pallas as pl
from jax.experimental.pallas import tpu as pltpu
from jax.sharding import PartitionSpec as P

FIELDS = 5
PX = 32
BOX = 64
SUB = 8
LANE = 128
HALF = PX // 2
ROWS = FIELDS * SUB
STRIDE = BOX - HALF + 1
heat_ratio = 1.4
courant = 0.3
WEST, EAST, SOUTH, NORTH = range(4)


def primitive(u):
    inverse = 1.0 / u[0]
    vx, vy, vz = u[1] * inverse, u[2] * inverse, u[3] * inverse
    kinetic = 0.5 * (u[1] * vx + u[2] * vy + u[3] * vz)
    pressure = (heat_ratio - 1.0) * (u[4] - kinetic)
    sound = jnp.sqrt(heat_ratio * pressure * inverse)
    return vx, vy, pressure, sound


def half_flux(u, moving, pressure, sound, normal):
    half = 0.5 * moving
    flux = [u[f] * half for f in range(FIELDS)]
    flux[normal] = flux[normal] + 0.5 * pressure
    flux[4] = flux[4] + pressure * half
    return flux, 0.5 * (jnp.abs(moving) + sound)


def left_of(x):
    return pltpu.roll(x, 1, 1)


def right_of(x):
    return pltpu.roll(x, LANE - 1, 1)


def tendency(u, ghosts, masks):
    first_col, last_col, first_row, last_row, low_lanes, high_lanes, swap = masks

    def below(x):
        turned = pltpu.roll(x, PX, 1)
        return jnp.where(low_lanes, pltpu.roll(turned, 1, 0), turned)

    def above(x):
        turned = pltpu.roll(x, LANE - PX, 1)
        return jnp.where(high_lanes, pltpu.roll(turned, SUB - 1, 0), turned)

    vx, vy, pressure, sound = primitive(u)
    total = None
    for normal, moving, before, after, first, last in (
        (1, vx, left_of, right_of, first_col, last_col),
        (2, vy, below, above, first_row, last_row),
    ):
        flux, wave = half_flux(u, moving, pressure, sound, normal)
        wave_face = jnp.maximum(before(wave), wave)
        if normal == 1:
            beyond = [
                jnp.take_along_axis(
                    jnp.where(last_col, ghosts[WEST][f], ghosts[EAST][f]), swap, axis=1, mode="promise_in_bounds"
                )
                for f in range(FIELDS)
            ]
        else:
            beyond = [
                jnp.where(
                    first,
                    pltpu.roll(pltpu.roll(ghosts[SOUTH][f], PX, 1), 1, 0),
                    pltpu.roll(pltpu.roll(ghosts[NORTH][f], LANE - PX, 1), SUB - 1, 0),
                )
                for f in range(FIELDS)
            ]
        gx, gy, gp, gs = primitive(beyond)
        gflux, gwave = half_flux(beyond, gx if normal == 1 else gy, gp, gs, normal)
        gface = jnp.maximum(gwave, wave)
        part = []
        for f in range(FIELDS):
            inner = before(flux[f]) + flux[f] - wave_face * (u[f] - before(u[f]))
            inner = jnp.where(first, 0.0, inner)
            both = flux[f] + gflux[f]
            spread = gface * (u[f] - beyond[f])
            border = jnp.where(first, both - spread, jnp.where(last, -both - spread, 0.0))
            part.append(inner - after(inner) + border)
        total = part if total is None else [a + b for a, b in zip(total, part)]
    return total


def cell_masks():
    lane = lax.broadcasted_iota(jnp.int32, (SUB, LANE), 1)
    sub = lax.broadcasted_iota(jnp.int32, (SUB, LANE), 0)
    col = lane % PX
    low, high = lane < PX, lane >= LANE - PX
    return (
        col == 0,
        col == PX - 1,
        low & (sub == 0),
        high & (sub == SUB - 1),
        low,
        high,
        lane - col + (PX - 1 - col),
    )


def pack_kernel(count, tiles, rows, patch_ref, box_ref, state_ref, pay_ref, scr):
    top = None
    for p in range(count):
        for s in range(SUB):
            scr[p * 64 + s * SUB : p * 64 + s * SUB + FIELDS, :] = patch_ref[0, 0, p, :, s * LANE : (s + 1) * LANE]
        u = []
        for f in range(FIELDS):
            plane = scr[pl.ds(p * 64 + f, SUB, stride=SUB), :]
            state_ref[p * ROWS + f * SUB : p * ROWS + (f + 1) * SUB, :] = plane
            u.append(plane)
        vx, vy, pressure, sound = primitive(u)
        wave = jnp.maximum(jnp.abs(vx), jnp.abs(vy)) + sound
        top = wave if top is None else jnp.maximum(top, wave)
    start = lax.axis_index("gy") * (tiles * LANE)
    for t in range(tiles):
        lanes = pl.ds(pl.multiple_of(start + t * LANE, LANE), LANE)
        pay_ref[t * FIELDS : (t + 1) * FIELDS, :] = box_ref[0, :, lanes]
    pay_ref[rows - SUB : rows, :] = top


def strip_kernel(parts, rows, requests, at_ref, shift_ref, *refs):
    pay_refs, out_ref, scr = refs[:parts], refs[parts], refs[parts + 1]
    top = None
    for k in range(parts):
        scr[k * rows : (k + 1) * rows, :] = pay_refs[k][...]
        wave = pay_refs[k][rows - SUB : rows, :]
        top = wave if top is None else jnp.maximum(top, wave)
    scr[parts * rows : parts * rows + SUB, :] = jnp.zeros((SUB, LANE), jnp.float32)
    place = lax.broadcasted_iota(jnp.int32, (SUB, LANE), 1) // HALF
    for v in range(requests // SUB):
        acc = None
        for m in range(SUB):
            q = v * SUB + m
            turned = pltpu.roll(scr[pl.ds(at_ref[q], SUB), :], shift_ref[q], 1)
            acc = turned if acc is None else jnp.where(place == m, turned, acc)
        out_ref[v * FIELDS : (v + 1) * FIELDS, :] = acc[:FIELDS, :]
    strip_rows = requests // SUB * FIELDS
    out_ref[strip_rows : strip_rows + SUB, :] = top


def step_kernel(group, count, patches, slots, mix, around_ref, slot_ref, *refs):
    state_refs, strip_refs, out_ref = refs[:group], refs[group : 2 * group], refs[2 * group]
    cells, strips, scr = refs[2 * group + 1 :]
    me = lax.axis_index("gy")
    requests = 4 * patches
    strip_rows = requests // SUB * FIELDS
    for k in range(group):
        first = pl.multiple_of(mix(me, k, group) * (count * ROWS), SUB)
        cells[pl.ds(first, count * ROWS), :] = state_refs[k][...]
    total = strip_refs[0][:strip_rows, :]
    top = strip_refs[0][strip_rows:, :]
    for k in range(1, group):
        total = total + strip_refs[k][:strip_rows, :]
        top = jnp.maximum(top, strip_refs[k][strip_rows:, :])
    strips[...] = total
    time_step = courant / jnp.max(top)
    masks = cell_masks()
    lane = lax.broadcasted_iota(jnp.int32, (SUB, LANE), 1)
    sub = lax.broadcasted_iota(jnp.int32, (SUB, LANE), 0)
    along_col = 2 * sub + lane // (2 * PX)
    along_row = lane % PX // 2

    def coarse(v, carry):
        for m in range(SUB):
            q = v * SUB + m

            @pl.when(around_ref[q] < 0)
            def _():
                pick = HALF * m + (along_col if m % 4 < 2 else along_row)
                for f in range(FIELDS):
                    row = jnp.broadcast_to(strips[pl.ds(v * FIELDS + f, 1), :], (SUB, LANE))
                    wide = jnp.take_along_axis(row, pick, axis=1, mode="promise_in_bounds")
                    to = pl.multiple_of((2 * patches + q) * ROWS + f * SUB, SUB)
                    cells[pl.ds(to, SUB), :] = wide

        return carry

    lax.fori_loop(0, requests // SUB, coarse, 0)

    def planes(index):
        first = pl.multiple_of(index * ROWS, SUB)
        return [cells[pl.ds(first + f * SUB, SUB), :] for f in range(FIELDS)]

    def advance(p, base):
        u = planes(base + p)
        ghosts = []
        for side in range(4):
            near = around_ref[4 * p + side]
            ghosts.append(planes(jnp.where(near >= 0, base + near, 2 * patches + 4 * p + side)))
        change = tendency(u, ghosts, masks)
        return [u[f] + time_step * change[f] for f in range(FIELDS)]

    def first_section(i, carry):
        for half in range(2):
            p = i * 2 + half
            new = advance(p, 0)
            first = pl.multiple_of((patches + p) * ROWS, SUB)
            for f in range(FIELDS):
                cells[pl.ds(first + f * SUB, SUB), :] = new[f]
        return carry

    lax.fori_loop(0, patches // 2, first_section, 0)

    def second_section(j, carry):
        p = slot_ref[j]

        @pl.when(p >= 0)
        def _():
            new = advance(p, patches)
            old = planes(p)
            for f in range(FIELDS):
                scr[f * SUB : (f + 1) * SUB, :] = 0.5 * old[f] + 0.5 * new[f]
            for s in range(SUB):
                tile = scr[pl.ds(s, SUB, stride=SUB), :]
                out_ref[0, 0, j, :, s * LANE : (s + 1) * LANE] = tile[:FIELDS, :]

        @pl.when(p < 0)
        def _():
            out_ref[0, 0, j, :, :] = jnp.zeros((FIELDS, SUB * LANE), jnp.float32)

        return carry

    lax.fori_loop(0, slots, second_section, 0)


def power_of_two(n):
    return n & (n - 1) == 0


def mix(me, k, n):
    return me ^ k if power_of_two(n) else (me - k + n) % n


def exchange(x, axes, n):
    if power_of_two(n):
        perms = [[(i, i ^ k) for i in range(n)] for k in range(1, n)]
    else:
        perms = [[(i, (i + k) % n) for i in range(n)] for k in range(1, n)]
    return [x] + [lax.ppermute(x, axes, perm) for perm in perms]


def per_device(patch_state, coarse_boxes, new_owner, neighbors, coarse_box, coarse_start):
    count = patch_state.shape[2]
    group = lax.axis_size("gy")
    parts = lax.axis_size("gx") * lax.axis_size("gz")
    patches = count * group
    requests = 4 * patches
    capacity = max(2, 2 * count // group)
    slots = group * capacity
    tiles = BOX * BOX // LANE // group
    rows = -(-tiles * FIELDS // SUB) * SUB + SUB
    strip_rows = requests // SUB * FIELDS
    me = lax.axis_index("gy")
    part = lax.axis_index("gx") * lax.axis_size("gz") + lax.axis_index("gz")
    vmem = pl.BlockSpec(memory_space=pltpu.VMEM)
    smem = pl.BlockSpec(memory_space=pltpu.SMEM)
    f32 = jnp.float32

    state, payload = pl.pallas_call(
        functools.partial(pack_kernel, count, tiles, rows),
        out_shape=(
            jax.ShapeDtypeStruct((count * ROWS, LANE), f32),
            jax.ShapeDtypeStruct((rows, LANE), f32),
        ),
        in_specs=[vmem, vmem],
        out_specs=(vmem, vmem),
        scratch_shapes=[pltpu.VMEM((count * 64, LANE), f32)],
        name="pack",
    )(patch_state, coarse_boxes)

    payloads = exchange(payload, ("gx", "gz"), parts)
    states = exchange(state, "gy", group)

    order = jnp.arange(requests, dtype=jnp.int32)
    start = coarse_start.reshape(-1)
    row = start // STRIDE
    tile = row // 2
    offset = BOX * (row % 2) + start % STRIDE
    kth = mix(part, coarse_box.reshape(-1), parts)
    at = jnp.where(tile // tiles == me, kth * rows + tile % tiles * FIELDS, parts * rows)
    shift = (HALF * (order % SUB) - offset + LANE) % LANE
    around = neighbors.reshape(-1)

    owner = new_owner.reshape(-1)
    numbers = jnp.arange(patches, dtype=jnp.int32)
    source = numbers // count
    same = (
        (owner[:, None] == owner[None, :])
        & (source[:, None] == source[None, :])
        & (numbers[:, None] > numbers[None, :])
    )
    target = source * capacity + jnp.sum(same.astype(jnp.int32), axis=1)
    here = (owner == me)[None, :] & (target[None, :] == jnp.arange(slots, dtype=jnp.int32)[:, None])
    slot_patch = jnp.max(jnp.where(here, numbers[None, :], -1), axis=1)

    strip = pl.pallas_call(
        functools.partial(strip_kernel, parts, rows, requests),
        out_shape=jax.ShapeDtypeStruct((strip_rows + SUB, LANE), f32),
        in_specs=[smem, smem] + [vmem] * parts,
        out_specs=vmem,
        scratch_shapes=[pltpu.VMEM((parts * rows + SUB, LANE), f32)],
        name="strips",
    )(at, shift, *payloads)
    strips = exchange(strip, "gy", group)

    return pl.pallas_call(
        functools.partial(step_kernel, group, count, patches, slots, mix),
        out_shape=jax.ShapeDtypeStruct((1, 1, slots, FIELDS, SUB * LANE), f32),
        in_specs=[smem, smem] + [vmem] * (2 * group),
        out_specs=vmem,
        scratch_shapes=[
            pltpu.VMEM(((2 * patches + requests) * ROWS, LANE), f32),
            pltpu.VMEM((strip_rows, LANE), f32),
            pltpu.VMEM((64, LANE), f32),
        ],
        compiler_params=pltpu.CompilerParams(vmem_limit_bytes=48 * 1024 * 1024),
        name="step",
    )(around, slot_patch, *states, *strips)


def solution(mesh):
    in_specs = (
        P("gx", "gz", "gy", None, None),
        P(("gx", "gz"), None, None),
        P("gx", "gz", None, None),
        P("gx", "gz", None, None),
        P("gx", "gz", None, None),
        P("gx", "gz", None, None),
    )
    out_specs = P("gx", "gz", "gy", None, None)
    return jax.shard_map(
        per_device, mesh=mesh, in_specs=in_specs, out_specs=out_specs, check_vma=False
    )
```

```python
import functools

import jax
import jax.numpy as jnp
from jax import lax
from jax.experimental import pallas as pl
from jax.experimental.pallas import tpu as pltpu
from jax.sharding import PartitionSpec as P

FIELDS = 5
PX = 32
BOX = 64
SUB = 8
LANE = 128
HALF = PX // 2
STRIDE = BOX - HALF + 1
BOX_ROWS = BOX * BOX // LANE
ROWS = FIELDS * SUB
VX, PRESSURE, WAVE_X, VY, WAVE_Y = range(FIELDS, FIELDS + 5)
X_PLANES = WAVE_X + 1
PLANES = WAVE_Y + 1
FULL = PLANES * SUB
SIDE = X_PLANES * SUB
heat_ratio = 1.4
courant = 0.3
WEST, EAST, SOUTH, NORTH = range(4)
BATCH = 4


def power_of_two(n):
    return n & (n - 1) == 0


def masks_of(n):
    return [n >> (i + 1) for i in range(n.bit_length() - 1)]


def primitive(u):
    inverse = 1.0 / u[0]
    vx, vy, vz = u[1] * inverse, u[2] * inverse, u[3] * inverse
    kinetic = u[1] * (0.5 * vx) + u[2] * (0.5 * vy) + u[3] * (0.5 * vz)
    pressure = (heat_ratio - 1.0) * (u[4] - kinetic)
    sound = jnp.sqrt(heat_ratio * pressure * inverse)
    return vx, vy, pressure, sound


def with_primitives(u):
    vx, vy, pressure, sound = primitive(u)
    return u + [vx, pressure, 0.5 * (jnp.abs(vx) + sound), vy, 0.5 * (jnp.abs(vy) + sound)]


def half_flux(u, moving, pressure, normal):
    half = 0.5 * moving
    flux = [u[f] * half for f in range(FIELDS)]
    flux[normal] = flux[normal] + 0.5 * pressure
    flux[4] = flux[4] + pressure * half
    return flux


def lane_of():
    return lax.broadcasted_iota(jnp.int32, (SUB, LANE), 1)


def sub_of():
    return lax.broadcasted_iota(jnp.int32, (SUB, LANE), 0)


def take_lanes(x, lanes):
    return jnp.take_along_axis(x, lanes, axis=1, mode="promise_in_bounds")


def below(x, low_lanes):
    turned = pltpu.roll(x, PX, 1)
    return jnp.where(low_lanes, pltpu.roll(turned, 1, 0), turned)


def above(x, high_lanes):
    turned = pltpu.roll(x, LANE - PX, 1)
    return jnp.where(high_lanes, pltpu.roll(turned, SUB - 1, 0), turned)


def x_part(own, west, east):
    lane = lane_of()
    col = lane % PX
    first, last = col == 0, col == PX - 1
    swap = lane + (PX - 1) - 2 * col
    ghost = [take_lanes(jnp.where(last, w, e), swap) for w, e in zip(west, east)]
    u, wave = own[:FIELDS], own[WAVE_X]
    flux = half_flux(u, own[VX], own[PRESSURE], 1)
    gflux = half_flux(ghost[:FIELDS], ghost[VX], ghost[PRESSURE], 1)
    gwave = ghost[WAVE_X]
    face = jnp.maximum(jnp.where(first, gwave, pltpu.roll(wave, 1, 1)), wave)
    border = jnp.maximum(gwave, wave)
    part = []
    for f in range(FIELDS):
        left_u = jnp.where(first, ghost[f], pltpu.roll(u[f], 1, 1))
        left_flux = jnp.where(first, gflux[f], pltpu.roll(flux[f], 1, 1))
        west_flux = left_flux + flux[f] - face * (u[f] - left_u)
        east_flux = flux[f] + gflux[f] - border * (ghost[f] - u[f])
        part.append(west_flux - jnp.where(last, east_flux, pltpu.roll(west_flux, LANE - 1, 1)))
    return part


def y_border(row0, row31, south, north):
    lane, sub = lane_of(), sub_of()
    low = lane < LANE // 2
    cell = [jnp.where(low, a, b) for a, b in zip(row0, row31)]
    ghost = [take_lanes(jnp.where(low, n, s), lane ^ (LANE - PX)) for s, n in zip(south, north)]

    def flux(u, moving, pressure):
        half = 0.5 * moving
        return u * half + pressure * jnp.where(sub == 2, 0.5, jnp.where(sub == 4, half, 0.0))

    both = flux(*ghost[:3]) + flux(*cell[:3])
    spread = jnp.maximum(ghost[3], cell[3]) * (cell[0] - ghost[0])
    return both - jnp.where(low, spread, -spread)


def y_part(own, border):
    lane, sub = lane_of(), sub_of()
    low, high = lane < PX, lane >= LANE - PX
    first, last = low & (sub == 0), high & (sub == SUB - 1)
    u, wave = own[:FIELDS], own[WAVE_Y]
    flux = half_flux(u, own[VY], own[PRESSURE], 2)
    face = jnp.maximum(below(wave, low), wave)
    part = []
    for f in range(FIELDS):
        south_flux = below(flux[f], low) + flux[f] - face * (u[f] - below(u[f], low))
        edge = jnp.broadcast_to(border[f : f + 1, :], (SUB, LANE))
        south_flux = jnp.where(first, edge, south_flux)
        part.append(south_flux - jnp.where(last, edge, above(south_flux, high)))
    return part


def pack_kernel(
    count, tiles, rows, patches, mesh_sizes, patch_ref, box_ref, which_ref, start_ref, state_ref, pay_ref, meta_ref, scr
):
    n_gx, n_gz = mesh_sizes
    for f in range(FIELDS):
        for s in range(SUB):
            at = (f * SUB + s) * count
            scr[at : at + count, :] = patch_ref[0, 0, f, :, s * LANE : (s + 1) * LANE]
    top = None
    for p in range(count):
        u = []
        for f in range(FIELDS):
            plane = scr[pl.ds(f * SUB * count + p, SUB, stride=count), :]
            state_ref[p * ROWS + f * SUB : p * ROWS + (f + 1) * SUB, :] = plane
            u.append(plane)
        vx, vy, pressure, sound = primitive(u)
        wave = jnp.maximum(jnp.abs(vx), jnp.abs(vy)) + sound
        top = wave if top is None else jnp.maximum(top, wave)
    me = lax.axis_index("gy")
    for f in range(FIELDS):
        pay_ref[f * tiles : (f + 1) * tiles, :] = box_ref[pl.ds(f * BOX_ROWS + me * tiles, tiles), :]
    pay_ref[rows - SUB : rows, :] = top

    start = start_ref[0, 0]
    row = lax.shift_right_logical(start * 2675, 17)
    offset = BOX * (row & 1) + start - row * STRIDE
    tile = lax.shift_right_logical(row, 1)
    which = which_ref[0, 0]
    gz_bits = n_gz.bit_length() - 1
    place = place_of(lax.axis_index("gx"), lax.shift_right_logical(which, gz_bits), n_gx) + n_gx * place_of(
        lax.axis_index("gz"), which & (n_gz - 1), n_gz
    )
    near = tile - me * tiles
    mine = (near >= 0) & (near < tiles)
    patch = lax.broadcasted_iota(jnp.int32, start.shape, 1)
    meta_ref[0:4, 0:patches] = place * rows + jnp.where(mine, near, 0)
    meta_ref[4:8, 0:patches] = (HALF * (patch & (SUB - 1)) - offset) & (LANE - 1)
    meta_ref[8:12, 0:patches] = jnp.where(mine, patch & (SUB - 1), -1)


def place_of(me, other, n):
    if power_of_two(n):
        apart = me ^ other
        place = 0
        for i, mask in enumerate(masks_of(n)):
            place = place + jnp.where((apart & mask) != 0, 1 << i, 0)
        return place
    behind = me - other
    return jnp.where(behind < 0, behind + n, behind)


def strip_kernel(parts, rows, tiles, patches, meta_ref, pay_ref, out_ref):
    top = None
    for k in range(parts):
        wave = pay_ref[(k + 1) * rows - SUB : (k + 1) * rows, :]
        top = wave if top is None else jnp.maximum(top, wave)
    block = lane_of() // HALF
    lines = 4 * patches // SUB
    for v in range(lines):
        side, first = v * SUB // patches, v * SUB % patches
        acc = jnp.zeros((SUB, LANE), jnp.float32)
        for m in range(SUB):
            p = first + m
            at, shift, fills = meta_ref[side, p], meta_ref[4 + side, p], meta_ref[8 + side, p]
            strip = pay_ref[pl.ds(at, FIELDS, stride=tiles), :]
            strip = jnp.concatenate([strip, jnp.zeros((SUB - FIELDS, LANE), jnp.float32)], axis=0)
            acc = jnp.where(block == fills, pltpu.roll(strip, shift, 1), acc)
        out_ref[pl.ds(v, FIELDS, stride=lines), :] = acc[:FIELDS, :]
    out_ref[FIELDS * lines :, :] = top


def step_kernel(sources, count, patches, slots, around_ref, owner_ref, *refs):
    group = len(sources)
    state_refs, strip_ref, out_ref = refs[:group], refs[group], refs[group + 1]
    cells, cells_one, strips, placed, own_patch, own_slot = refs[group + 2 :]
    me = lax.axis_index("gy")
    lines = 4 * patches // SUB
    capacity = slots // group
    side_base = patches * FULL
    row_base = side_base + 2 * patches * SIDE

    held = jnp.int32(0)
    for i in range(BATCH):
        own_patch[slots + i] = 0
    for source in range(group):
        rank = jnp.int32(0)
        for i in range(count):
            hit = owner_ref[0, 0, 0, source * count + i] == me
            own_patch[held] = source * count + i
            own_slot[held] = source * capacity + rank
            step = jnp.where(hit, 1, 0)
            held, rank = held + step, rank + step

    def prepare(i, carry):
        made = []
        for k in range(group):
            u = [state_refs[k][pl.ds(pl.multiple_of(i * ROWS + f * SUB, SUB), SUB), :] for f in range(FIELDS)]
            made.append(with_primitives(u))
        for k in range(group):
            first = pl.multiple_of((sources[k](me) * count + i) * FULL, SUB)
            for q in range(PLANES):
                cells[pl.ds(first + q * SUB, SUB), :] = made[k][q]
        return carry

    lax.fori_loop(0, count, prepare, 0)

    for h in range(lines // SUB):
        u = [strip_ref[f * lines + h * SUB : f * lines + (h + 1) * SUB, :] for f in range(FIELDS)]
        planes = with_primitives(u)
        for q in range(PLANES):
            strips[q * lines + h * SUB : q * lines + (h + 1) * SUB, :] = planes[q]
    time_step = courant / jnp.max(strip_ref[FIELDS * lines :, :])
    lane, sub = lane_of(), sub_of()
    down = 2 * sub + lane // (2 * PX)
    along = HALF * sub + lane % PX // 2

    def wide(q, v, pick):
        row = jnp.broadcast_to(strips[pl.ds(q * lines + v, 1), :], (SUB, LANE))
        return take_lanes(row, pick)

    def coarse_sides(v, carry):
        for m in range(SUB):
            first = pl.multiple_of(side_base + (v * SUB + m) * SIDE, SUB)
            made = [wide(q, v, HALF * m + down) for q in range(X_PLANES)]
            for q in range(X_PLANES):
                cells[pl.ds(first + q * SUB, SUB), :] = made[q]
                cells_one[pl.ds(first + q * SUB, SUB), :] = made[q]
        return carry

    lax.fori_loop(0, lines // 2, coarse_sides, 0)

    def coarse_rows(v, carry):
        first = pl.multiple_of(row_base + v * FULL, SUB)
        made = [wide(q, lines // 2 + v, along) for q in range(PLANES)]
        for q in range(PLANES):
            cells[pl.ds(first + q * SUB, SUB), :] = made[q]
            cells_one[pl.ds(first + q * SUB, SUB), :] = made[q]
        return carry

    lax.fori_loop(0, lines // 2, coarse_rows, 0)

    def tendencies(ref, ps):
        loaded = []
        for p in ps:
            near = [around_ref[0, 0, side, p] for side in range(4)]
            first = p * FULL
            bases = [
                pl.multiple_of(
                    jnp.where(near[side] >= 0, near[side] * FULL, side_base + (side * patches + p) * SIDE), SUB
                )
                for side in (WEST, EAST)
            ]

            def facing(side, row):
                line = (side - SOUTH) * patches + p
                at_coarse = row_base + line // SUB * FULL + line % SUB
                return jnp.where(near[side] >= 0, near[side] * FULL + row, at_coarse)

            def rows_at(at):
                return [ref[pl.ds(at, SUB, stride=SUB), :]] + [
                    jnp.broadcast_to(ref[pl.ds(at + q * SUB, 1), :], (SUB, LANE)) for q in (VY, PRESSURE, WAVE_Y)
                ]

            own = [ref[pl.ds(pl.multiple_of(first + q * SUB, SUB), SUB), :] for q in range(PLANES)]
            west, east = [
                [ref[pl.ds(pl.multiple_of(base + q * SUB, SUB), SUB), :] for q in range(X_PLANES)] for base in bases
            ]
            border = [
                rows_at(at)
                for at in (first, first + SUB - 1, facing(SOUTH, SUB - 1), facing(NORTH, 0))
            ]
            loaded.append((own, west, east, border))
        out = []
        for own, west, east, border in loaded:
            across = x_part(own, west, east)
            along = y_part(own, y_border(*border))
            out.append((own, [a + b for a, b in zip(across, along)]))
        return out

    def first_section(i, carry):
        ps = [i * BATCH + b for b in range(BATCH)]
        made = []
        for own, change in tendencies(cells, ps):
            made.append(with_primitives([own[f] + time_step * change[f] for f in range(FIELDS)]))
        for p, planes in zip(ps, made):
            first = pl.multiple_of(p * FULL, SUB)
            for q in range(PLANES):
                cells_one[pl.ds(first + q * SUB, SUB), :] = planes[q]
        return carry

    lax.fori_loop(0, patches // BATCH, first_section, 0)

    placed[...] = jnp.zeros_like(placed)

    def second_section(i, carry):
        ps = [own_patch[i * BATCH + b] for b in range(BATCH)]
        ps = [jnp.where(i * BATCH + b < held, p, 0) for b, p in enumerate(ps)]
        made = []
        for p, (own, change) in zip(ps, tendencies(cells_one, ps)):
            first = pl.multiple_of(p * FULL, SUB)
            old = [cells[pl.ds(first + f * SUB, SUB), :] for f in range(FIELDS)]
            made.append([0.5 * old[f] + 0.5 * (own[f] + time_step * change[f]) for f in range(FIELDS)])
        for b in range(BATCH):
            slot = jnp.where(i * BATCH + b < held, own_slot[i * BATCH + b], slots)
            for f in range(FIELDS):
                at = (f * (slots // SUB + 1) + slot // SUB) * (SUB * SUB) + slot % SUB
                placed[pl.ds(at, SUB, stride=SUB), :] = made[b][f]
        return carry

    lax.fori_loop(0, (held + BATCH - 1) // BATCH, second_section, 0)
    for f in range(FIELDS):
        for t in range(slots // SUB):
            for s in range(SUB):
                at = ((f * (slots // SUB + 1) + t) * SUB + s) * SUB
                out_ref[0, 0, f, t * SUB : (t + 1) * SUB, s * LANE : (s + 1) * LANE] = placed[at : at + SUB, :]


def doubled(blocks, axis, n, join):
    if power_of_two(n):
        for mask in masks_of(n):
            blocks = join(blocks, lax.ppermute(blocks, axis, [(i, i ^ mask) for i in range(n)]))
        return blocks
    moved = [lax.ppermute(blocks, axis, [(i, (i + k) % n) for i in range(n)]) for k in range(1, n)]
    return functools.reduce(join, moved, blocks)


def per_device(patch_state, coarse_boxes, new_owner, neighbors, coarse_box, coarse_start):
    count = patch_state.shape[2]
    n_gx, n_gz, group = lax.axis_size("gx"), lax.axis_size("gz"), lax.axis_size("gy")
    parts = n_gx * n_gz
    patches = count * group
    lines = 4 * patches // SUB
    slots = group * max(2, 2 * count // group)
    tiles = BOX_ROWS // group
    rows = -(-tiles * FIELDS // SUB) * SUB + SUB
    vmem = pl.BlockSpec(memory_space=pltpu.VMEM)
    smem = pl.BlockSpec(memory_space=pltpu.SMEM)
    f32 = jnp.float32

    def sides_first(x):
        return jnp.swapaxes(x, 2, 3)

    state, payload, meta = pl.pallas_call(
        functools.partial(pack_kernel, count, tiles, rows, patches, (n_gx, n_gz)),
        out_shape=(
            jax.ShapeDtypeStruct((count * ROWS, LANE), f32),
            jax.ShapeDtypeStruct((rows, LANE), f32),
            jax.ShapeDtypeStruct((16, max(LANE, patches)), jnp.int32),
        ),
        in_specs=[vmem] * 4,
        out_specs=(vmem,) * 3,
        scratch_shapes=[pltpu.VMEM((FIELDS * SUB * count, LANE), f32)],
        name="pack",
    )(
        sides_first(patch_state),
        coarse_boxes.reshape(FIELDS * BOX_ROWS, LANE),
        sides_first(coarse_box),
        sides_first(coarse_start),
    )

    def beside(a, b):
        return jnp.concatenate([a, b], axis=0)

    payload = doubled(doubled(payload, "gx", n_gx, beside), "gz", n_gz, beside)

    states, sources = [state], [lambda me: me]
    for mask in masks_of(group):
        perm = [(i, i ^ mask) for i in range(group)]
        states = states + [lax.ppermute(x, "gy", perm) for x in states]
        sources = sources + [lambda me, f=f, mask=mask: f(me) ^ mask for f in sources]

    strip = pl.pallas_call(
        functools.partial(strip_kernel, parts, rows, tiles, patches),
        out_shape=jax.ShapeDtypeStruct((FIELDS * lines + SUB, LANE), f32),
        in_specs=[smem, vmem],
        out_specs=vmem,
        name="strips",
    )(meta, payload)

    def merge(a, b):
        row = lax.broadcasted_iota(jnp.int32, a.shape, 0)
        return jnp.where(row < FIELDS * lines, a + b, jnp.maximum(a, b))

    strip = doubled(strip, "gy", group, merge)

    place_rows = patches * FULL + 2 * patches * SIDE + lines // 2 * FULL
    out = pl.pallas_call(
        functools.partial(step_kernel, sources, count, patches, slots),
        out_shape=jax.ShapeDtypeStruct((1, 1, FIELDS, slots, SUB * LANE), f32),
        in_specs=[smem, smem] + [vmem] * (group + 1),
        out_specs=vmem,
        scratch_shapes=[
            pltpu.VMEM((place_rows, LANE), f32),
            pltpu.VMEM((place_rows, LANE), f32),
            pltpu.VMEM((PLANES * lines, LANE), f32),
            pltpu.VMEM((FIELDS * (slots // SUB + 1) * SUB * SUB, LANE), f32),
            pltpu.SMEM((slots + BATCH,), jnp.int32),
            pltpu.SMEM((slots + BATCH,), jnp.int32),
        ],
        compiler_params=pltpu.CompilerParams(vmem_limit_bytes=56 * 1024 * 1024),
        name="step",
    )(sides_first(neighbors), sides_first(new_owner), *states, strip)
    return sides_first(out)


def solution(mesh):
    in_specs = (
        P("gx", "gz", "gy", None, None),
        P(("gx", "gz"), None, None),
        P("gx", "gz", None, None),
        P("gx", "gz", None, None),
        P("gx", "gz", None, None),
        P("gx", "gz", None, None),
    )
    out_specs = P("gx", "gz", "gy", None, None)
    return jax.shard_map(
        per_device, mesh=mesh, in_specs=in_specs, out_specs=out_specs, check_vma=False
    )
```

```python
import functools

import jax
import jax.numpy as jnp
from jax import lax
from jax.experimental import pallas as pl
from jax.experimental.pallas import tpu as pltpu
from jax.sharding import PartitionSpec as P

FIELDS = 5
PX = 32
BOX = 64
SUB = 8
LANE = 128
HALF = PX // 2
STRIDE = BOX - HALF + 1
BOX_ROWS = BOX * BOX // LANE
ROWS = FIELDS * SUB
VX, PRESSURE, WAVE_X, VY, WAVE_Y = range(FIELDS, FIELDS + 5)
X_PLANES = WAVE_X + 1
PLANES = WAVE_Y + 1
FULL = PLANES * SUB
SIDE = X_PLANES * SUB
heat_ratio = 1.4
courant = 0.3
WEST, EAST, SOUTH, NORTH = range(4)
BATCH = 8


def power_of_two(n):
    return n & (n - 1) == 0


def masks_of(n):
    return [n >> (i + 1) for i in range(n.bit_length() - 1)]


def primitive(u):
    inverse = 1.0 / u[0]
    vx, vy, vz = u[1] * inverse, u[2] * inverse, u[3] * inverse
    kinetic = u[1] * (0.5 * vx) + u[2] * (0.5 * vy) + u[3] * (0.5 * vz)
    pressure = (heat_ratio - 1.0) * (u[4] - kinetic)
    sound = jnp.sqrt(heat_ratio * pressure * inverse)
    return vx, vy, pressure, sound


def with_primitives(u):
    vx, vy, pressure, sound = primitive(u)
    return u + [vx, pressure, 0.5 * (jnp.abs(vx) + sound), vy, 0.5 * (jnp.abs(vy) + sound)]


def half_flux(u, moving, pressure, normal):
    half = 0.5 * moving
    flux = [u[f] * half for f in range(FIELDS)]
    flux[normal] = flux[normal] + 0.5 * pressure
    flux[4] = flux[4] + pressure * half
    return flux


def lane_of():
    return lax.broadcasted_iota(jnp.int32, (SUB, LANE), 1)


def sub_of():
    return lax.broadcasted_iota(jnp.int32, (SUB, LANE), 0)


def take_lanes(x, lanes):
    return jnp.take_along_axis(x, lanes, axis=1, mode="promise_in_bounds")


def below(x, low_lanes):
    turned = pltpu.roll(x, PX, 1)
    return jnp.where(low_lanes, pltpu.roll(turned, 1, 0), turned)


def above(x, high_lanes):
    turned = pltpu.roll(x, LANE - PX, 1)
    return jnp.where(high_lanes, pltpu.roll(turned, SUB - 1, 0), turned)


def x_part(own, west, east):
    lane = lane_of()
    col = lane & (PX - 1)
    first, last = col == 0, col == PX - 1
    swap = lane + (PX - 1) - 2 * col
    ghost = [take_lanes(jnp.where(last, w, e), swap) for w, e in zip(west, east)]
    u, wave = own[:FIELDS], own[WAVE_X]
    flux = half_flux(u, own[VX], own[PRESSURE], 1)
    gflux = half_flux(ghost[:FIELDS], ghost[VX], ghost[PRESSURE], 1)
    gwave = ghost[WAVE_X]
    face = jnp.maximum(jnp.where(first, gwave, pltpu.roll(wave, 1, 1)), wave)
    border = jnp.maximum(gwave, wave)
    part = []
    for f in range(FIELDS):
        left_u = jnp.where(first, ghost[f], pltpu.roll(u[f], 1, 1))
        left_flux = jnp.where(first, gflux[f], pltpu.roll(flux[f], 1, 1))
        west_flux = left_flux + flux[f] - face * (u[f] - left_u)
        east_flux = flux[f] + gflux[f] - border * (ghost[f] - u[f])
        part.append(west_flux - jnp.where(last, east_flux, pltpu.roll(west_flux, LANE - 1, 1)))
    return part


def y_border(row0, row31, south, north):
    lane, sub = lane_of(), sub_of()
    low = lane < LANE // 2
    cell = [jnp.where(low, a, b) for a, b in zip(row0, row31)]
    ghost = [take_lanes(jnp.where(low, n, s), lane ^ (LANE - PX)) for s, n in zip(south, north)]

    def flux(u, moving, pressure):
        half = 0.5 * moving
        return u * half + pressure * jnp.where(sub == 2, 0.5, jnp.where(sub == 4, half, 0.0))

    both = flux(*ghost[:3]) + flux(*cell[:3])
    spread = jnp.maximum(ghost[3], cell[3]) * (cell[0] - ghost[0])
    return both - jnp.where(low, spread, -spread)


def y_part(own, border):
    lane, sub = lane_of(), sub_of()
    low, high = lane < PX, lane >= LANE - PX
    first, last = low & (sub == 0), high & (sub == SUB - 1)
    u, wave = own[:FIELDS], own[WAVE_Y]
    flux = half_flux(u, own[VY], own[PRESSURE], 2)
    face = jnp.maximum(below(wave, low), wave)
    part = []
    for f in range(FIELDS):
        south_flux = below(flux[f], low) + flux[f] - face * (u[f] - below(u[f], low))
        edge = jnp.broadcast_to(border[f : f + 1, :], (SUB, LANE))
        south_flux = jnp.where(first, edge, south_flux)
        part.append(south_flux - jnp.where(last, edge, above(south_flux, high)))
    return part


def pack_kernel(
    count, tiles, rows, patches, mesh_sizes, patch_ref, box_ref, which_ref, start_ref, state_ref, pay_ref, meta_ref, scr
):
    n_gx, n_gz = mesh_sizes
    for f in range(FIELDS):
        for s in range(SUB):
            at = (f * SUB + s) * count
            scr[at : at + count, :] = patch_ref[0, 0, f, :, s * LANE : (s + 1) * LANE]
    top = None
    for p in range(count):
        u = []
        for f in range(FIELDS):
            plane = scr[pl.ds(f * SUB * count + p, SUB, stride=count), :]
            state_ref[p * ROWS + f * SUB : p * ROWS + (f + 1) * SUB, :] = plane
            u.append(plane)
        vx, vy, pressure, sound = primitive(u)
        wave = jnp.maximum(jnp.abs(vx), jnp.abs(vy)) + sound
        top = wave if top is None else jnp.maximum(top, wave)
    me = lax.axis_index("gy")
    pieces = [box_ref[pl.ds(f * BOX_ROWS + me * tiles, tiles), :] for f in range(FIELDS)]
    for k in range(n_gx * n_gz):
        for f in range(FIELDS):
            at = k * rows + f * tiles
            pay_ref[at : at + tiles, :] = pieces[f]
        pay_ref[(k + 1) * rows - SUB : (k + 1) * rows, :] = top

    start = start_ref[0, 0]
    row = lax.shift_right_logical(start * 2675, 17)
    offset = BOX * (row & 1) + start - row * STRIDE
    tile = lax.shift_right_logical(row, 1)
    which = which_ref[0, 0]
    near = tile - me * tiles
    mine = (near >= 0) & (near < tiles)
    patch = lax.broadcasted_iota(jnp.int32, start.shape, 1)
    meta_ref[0:4, 0:patches] = which * rows + jnp.where(mine, near, 0)
    meta_ref[4:8, 0:patches] = (HALF * (patch & (SUB - 1)) - offset) & (LANE - 1)
    meta_ref[8:12, 0:patches] = jnp.where(mine, patch & (SUB - 1), -1)


def strip_kernel(parts, group, rows, tiles, patches, meta_ref, pay_ref, out_ref):
    top = None
    for k in range(parts):
        wave = pay_ref[(k + 1) * rows - SUB : (k + 1) * rows, :]
        top = wave if top is None else jnp.maximum(top, wave)
    block = lane_of() // HALF
    lines = 4 * patches // SUB
    total = FIELDS * lines + SUB
    for v in range(lines):
        side, first = v * SUB // patches, v * SUB % patches
        acc = jnp.zeros((SUB, LANE), jnp.float32)
        for m in range(SUB):
            p = first + m
            at, shift, fills = meta_ref[side, p], meta_ref[4 + side, p], meta_ref[8 + side, p]
            strip = pay_ref[pl.ds(at, FIELDS, stride=tiles), :]
            strip = jnp.concatenate([strip, jnp.zeros((SUB - FIELDS, LANE), jnp.float32)], axis=0)
            acc = jnp.where(block == fills, pltpu.roll(strip, shift, 1), acc)
        for k in range(group):
            out_ref[pl.ds(k * total + v, FIELDS, stride=lines), :] = acc[:FIELDS, :]
    for k in range(group):
        out_ref[(k + 1) * total - SUB : (k + 1) * total, :] = top


def step_kernel(sources, count, patches, slots, around_ref, owner_ref, *refs):
    group = len(sources)
    state_refs, strip_ref, out_ref = refs[:group], refs[group], refs[group + 1]
    cells, cells_one, strips, placed, own_patch, own_slot = refs[group + 2 :]
    me = lax.axis_index("gy")
    lines = 4 * patches // SUB
    capacity = slots // group
    side_base = patches * FULL
    row_base = side_base + 2 * patches * SIDE

    held = jnp.int32(0)
    for i in range(BATCH):
        own_patch[slots + i] = 0
    for source in range(group):
        rank = jnp.int32(0)
        for i in range(count):
            hit = owner_ref[0, 0, 0, source * count + i] == me
            own_patch[held] = source * count + i
            own_slot[held] = source * capacity + rank
            step = jnp.where(hit, 1, 0)
            held, rank = held + step, rank + step

    def prepare(k):
        for i in range(count):
            u = [state_refs[k][i * ROWS + f * SUB : i * ROWS + (f + 1) * SUB, :] for f in range(FIELDS)]
            first = pl.multiple_of((sources[k](me) * count + i) * FULL, SUB)
            for q, plane in enumerate(with_primitives(u)):
                cells[pl.ds(first + q * SUB, SUB), :] = plane

    for k in range(group):
        prepare(k)

    length = FIELDS * lines + SUB

    def joined(at, join):
        return functools.reduce(join, [strip_ref[k * length + at : k * length + at + SUB, :] for k in range(group)])

    for h in range(lines // SUB):
        u = [joined(f * lines + h * SUB, jnp.add) for f in range(FIELDS)]
        planes = with_primitives(u)
        for q in range(PLANES):
            strips[q * lines + h * SUB : q * lines + (h + 1) * SUB, :] = planes[q]
    time_step = courant / jnp.max(joined(FIELDS * lines, jnp.maximum))
    lane, sub = lane_of(), sub_of()
    down = 2 * sub + lane // (2 * PX)
    along = HALF * sub + (lane & (PX - 1)) // 2

    def wide(q, v, pick):
        row = jnp.broadcast_to(strips[pl.ds(q * lines + v, 1), :], (SUB, LANE))
        return take_lanes(row, pick)

    def coarse_sides(v, carry):
        for m in range(SUB):
            first = pl.multiple_of(side_base + (v * SUB + m) * SIDE, SUB)
            made = [wide(q, v, HALF * m + down) for q in range(X_PLANES)]
            for q in range(X_PLANES):
                cells[pl.ds(first + q * SUB, SUB), :] = made[q]
                cells_one[pl.ds(first + q * SUB, SUB), :] = made[q]
        return carry

    lax.fori_loop(0, lines // 2, coarse_sides, 0)

    def coarse_rows(v, carry):
        first = pl.multiple_of(row_base + v * FULL, SUB)
        made = [wide(q, lines // 2 + v, along) for q in range(PLANES)]
        for q in range(PLANES):
            cells[pl.ds(first + q * SUB, SUB), :] = made[q]
            cells_one[pl.ds(first + q * SUB, SUB), :] = made[q]
        return carry

    lax.fori_loop(0, lines // 2, coarse_rows, 0)

    def tendencies(ref, ps):
        loaded = []
        for p in ps:
            near = [around_ref[0, 0, side, p] for side in range(4)]
            first = p * FULL
            bases = [
                pl.multiple_of(
                    jnp.where(near[side] >= 0, near[side] * FULL, side_base + (side * patches + p) * SIDE), SUB
                )
                for side in (WEST, EAST)
            ]

            def facing(side, row):
                line = (side - SOUTH) * patches + p
                at_coarse = row_base + line // SUB * FULL + line % SUB
                return jnp.where(near[side] >= 0, near[side] * FULL + row, at_coarse)

            def rows_at(at):
                return [ref[pl.ds(at, SUB, stride=SUB), :]] + [
                    jnp.broadcast_to(ref[pl.ds(at + q * SUB, 1), :], (SUB, LANE)) for q in (VY, PRESSURE, WAVE_Y)
                ]

            own = [ref[pl.ds(pl.multiple_of(first + q * SUB, SUB), SUB), :] for q in range(PLANES)]
            west, east = [
                [ref[pl.ds(pl.multiple_of(base + q * SUB, SUB), SUB), :] for q in range(X_PLANES)] for base in bases
            ]
            border = [
                rows_at(at)
                for at in (first, first + SUB - 1, facing(SOUTH, SUB - 1), facing(NORTH, 0))
            ]
            loaded.append((own, west, east, border))
        out = []
        for own, west, east, border in loaded:
            across = x_part(own, west, east)
            along = y_part(own, y_border(*border))
            out.append((own, [a + b for a, b in zip(across, along)]))
        return out

    def first_section(i, carry):
        ps = [i * BATCH + b for b in range(BATCH)]
        made = []
        for own, change in tendencies(cells, ps):
            made.append(with_primitives([own[f] + time_step * change[f] for f in range(FIELDS)]))
        for p, planes in zip(ps, made):
            first = pl.multiple_of(p * FULL, SUB)
            for q in range(PLANES):
                cells_one[pl.ds(first + q * SUB, SUB), :] = planes[q]
        return carry

    lax.fori_loop(0, patches // BATCH, first_section, 0)

    placed[...] = jnp.zeros_like(placed)

    def second_section(i, carry):
        ps = [own_patch[i * BATCH + b] for b in range(BATCH)]
        ps = [jnp.where(i * BATCH + b < held, p, 0) for b, p in enumerate(ps)]
        made = []
        for p, (own, change) in zip(ps, tendencies(cells_one, ps)):
            first = pl.multiple_of(p * FULL, SUB)
            old = [cells[pl.ds(first + f * SUB, SUB), :] for f in range(FIELDS)]
            made.append([0.5 * old[f] + 0.5 * (own[f] + time_step * change[f]) for f in range(FIELDS)])
        for b in range(BATCH):
            slot = jnp.where(i * BATCH + b < held, own_slot[i * BATCH + b], slots)
            for f in range(FIELDS):
                at = (f * (slots // SUB + 1) + slot // SUB) * (SUB * SUB) + slot % SUB
                placed[pl.ds(at, SUB, stride=SUB), :] = made[b][f]
        return carry

    lax.fori_loop(0, (held + BATCH - 1) // BATCH, second_section, 0)
    for f in range(FIELDS):
        for t in range(slots // SUB):
            for s in range(SUB):
                at = ((f * (slots // SUB + 1) + t) * SUB + s) * SUB
                out_ref[0, 0, f, t * SUB : (t + 1) * SUB, s * LANE : (s + 1) * LANE] = placed[at : at + SUB, :]


def per_device(patch_state, coarse_boxes, new_owner, neighbors, coarse_box, coarse_start):
    count = patch_state.shape[2]
    n_gx, n_gz, group = lax.axis_size("gx"), lax.axis_size("gz"), lax.axis_size("gy")
    parts = n_gx * n_gz
    patches = count * group
    lines = 4 * patches // SUB
    slots = group * max(2, 2 * count // group)
    tiles = BOX_ROWS // group
    rows = -(-tiles * FIELDS // SUB) * SUB + SUB
    vmem = pl.BlockSpec(memory_space=pltpu.VMEM)
    smem = pl.BlockSpec(memory_space=pltpu.SMEM)
    f32 = jnp.float32

    def sides_first(x):
        return jnp.swapaxes(x, 2, 3)

    state, payload, meta = pl.pallas_call(
        functools.partial(pack_kernel, count, tiles, rows, patches, (n_gx, n_gz)),
        out_shape=(
            jax.ShapeDtypeStruct((count * ROWS, LANE), f32),
            jax.ShapeDtypeStruct((parts * rows, LANE), f32),
            jax.ShapeDtypeStruct((16, max(LANE, patches)), jnp.int32),
        ),
        in_specs=[vmem] * 4,
        out_specs=(vmem,) * 3,
        scratch_shapes=[pltpu.VMEM((FIELDS * SUB * count, LANE), f32)],
        name="pack",
    )(
        sides_first(patch_state),
        coarse_boxes.reshape(FIELDS * BOX_ROWS, LANE),
        sides_first(coarse_box),
        sides_first(coarse_start),
    )

    payload = lax.all_to_all(payload, ("gx", "gz"), split_axis=0, concat_axis=0, tiled=True)

    states, sources = [state], [lambda me: me]
    for mask in masks_of(group):
        perm = [(i, i ^ mask) for i in range(group)]
        states = states + [lax.ppermute(x, "gy", perm) for x in states]
        sources = sources + [lambda me, f=f, mask=mask: f(me) ^ mask for f in sources]

    strip = pl.pallas_call(
        functools.partial(strip_kernel, parts, group, rows, tiles, patches),
        out_shape=jax.ShapeDtypeStruct((group * (FIELDS * lines + SUB), LANE), f32),
        in_specs=[smem, vmem],
        out_specs=vmem,
        name="strips",
    )(meta, payload)

    strip = lax.all_to_all(strip, "gy", split_axis=0, concat_axis=0, tiled=True)

    place_rows = patches * FULL + 2 * patches * SIDE + lines // 2 * FULL
    out = pl.pallas_call(
        functools.partial(step_kernel, sources, count, patches, slots),
        out_shape=jax.ShapeDtypeStruct((1, 1, FIELDS, slots, SUB * LANE), f32),
        in_specs=[smem, smem] + [vmem] * (group + 1),
        out_specs=vmem,
        scratch_shapes=[
            pltpu.VMEM((place_rows, LANE), f32),
            pltpu.VMEM((place_rows, LANE), f32),
            pltpu.VMEM((PLANES * lines, LANE), f32),
            pltpu.VMEM((FIELDS * (slots // SUB + 1) * SUB * SUB, LANE), f32),
            pltpu.SMEM((slots + BATCH,), jnp.int32),
            pltpu.SMEM((slots + BATCH,), jnp.int32),
        ],
        compiler_params=pltpu.CompilerParams(vmem_limit_bytes=56 * 1024 * 1024),
        name="step",
    )(sides_first(neighbors), sides_first(new_owner), *states, strip)
    return sides_first(out)


def solution(mesh):
    in_specs = (
        P("gx", "gz", "gy", None, None),
        P(("gx", "gz"), None, None),
        P("gx", "gz", None, None),
        P("gx", "gz", None, None),
        P("gx", "gz", None, None),
        P("gx", "gz", None, None),
    )
    out_specs = P("gx", "gz", "gy", None, None)
    return jax.shard_map(
        per_device, mesh=mesh, in_specs=in_specs, out_specs=out_specs, check_vma=False
    )
```

```python
import functools

import jax
import jax.numpy as jnp
from jax import lax
from jax.experimental import pallas as pl
from jax.experimental.pallas import tpu as pltpu
from jax.sharding import PartitionSpec as P

FIELDS = 5
PX = 32
BOX = 64
SUB = 8
LANE = 128
HALF = PX // 2
STRIDE = BOX - HALF + 1
BOX_ROWS = BOX * BOX // LANE
ROWS = FIELDS * SUB
VX, PRESSURE, WAVE_X, VY, WAVE_Y = range(FIELDS, FIELDS + 5)
X_PLANES = WAVE_X + 1
PLANES = WAVE_Y + 1
FULL = PLANES * SUB
SIDE = X_PLANES * SUB
heat_ratio = 1.4
courant = 0.3
WEST, EAST, SOUTH, NORTH = range(4)
BATCH = 4


def masks_of(n):
    return [n >> (i + 1) for i in range(n.bit_length() - 1)]


def primitive(u):
    inverse = 1.0 / u[0]
    vx, vy, vz = u[1] * inverse, u[2] * inverse, u[3] * inverse
    kinetic = u[1] * (0.5 * vx) + u[2] * (0.5 * vy) + u[3] * (0.5 * vz)
    pressure = (heat_ratio - 1.0) * (u[4] - kinetic)
    sound = jnp.sqrt(heat_ratio * pressure * inverse)
    return vx, vy, pressure, sound


def with_primitives(u):
    vx, vy, pressure, sound = primitive(u)
    return u + [vx, pressure, 0.5 * (jnp.abs(vx) + sound), vy, 0.5 * (jnp.abs(vy) + sound)]


def half_flux(u, moving, pressure, normal):
    half = 0.5 * moving
    flux = [u[f] * half for f in range(FIELDS)]
    flux[normal] = flux[normal] + 0.5 * pressure
    flux[4] = flux[4] + pressure * half
    return flux


def lane_of():
    return lax.broadcasted_iota(jnp.int32, (SUB, LANE), 1)


def sub_of():
    return lax.broadcasted_iota(jnp.int32, (SUB, LANE), 0)


def take_lanes(x, lanes):
    return jnp.take_along_axis(x, lanes, axis=1, mode="promise_in_bounds")


def below(x, low_lanes):
    turned = pltpu.roll(x, PX, 1)
    return jnp.where(low_lanes, pltpu.roll(turned, 1, 0), turned)


def above(x, high_lanes):
    turned = pltpu.roll(x, LANE - PX, 1)
    return jnp.where(high_lanes, pltpu.roll(turned, SUB - 1, 0), turned)


def x_part(own, west, east):
    lane = lane_of()
    col = lane & (PX - 1)
    first, last = col == 0, col == PX - 1
    swap = lane + (PX - 1) - 2 * col
    ghost = [take_lanes(jnp.where(last, w, e), swap) for w, e in zip(west, east)]
    u, wave = own[:FIELDS], own[WAVE_X]
    flux = half_flux(u, own[VX], own[PRESSURE], 1)
    gflux = half_flux(ghost[:FIELDS], ghost[VX], ghost[PRESSURE], 1)
    gwave = ghost[WAVE_X]
    face = jnp.maximum(jnp.where(first, gwave, pltpu.roll(wave, 1, 1)), wave)
    border = jnp.maximum(gwave, wave)
    part = []
    for f in range(FIELDS):
        left_u = jnp.where(first, ghost[f], pltpu.roll(u[f], 1, 1))
        left_flux = jnp.where(first, gflux[f], pltpu.roll(flux[f], 1, 1))
        west_flux = left_flux + flux[f] - face * (u[f] - left_u)
        east_flux = flux[f] + gflux[f] - border * (ghost[f] - u[f])
        part.append(west_flux - jnp.where(last, east_flux, pltpu.roll(west_flux, LANE - 1, 1)))
    return part


def y_border(row0, row31, south, north):
    lane, sub = lane_of(), sub_of()
    low = lane < LANE // 2
    cell = [jnp.where(low, a, b) for a, b in zip(row0, row31)]
    ghost = [take_lanes(jnp.where(low, n, s), lane ^ (LANE - PX)) for s, n in zip(south, north)]

    def flux(u, moving, pressure):
        half = 0.5 * moving
        return u * half + pressure * jnp.where(sub == 2, 0.5, jnp.where(sub == 4, half, 0.0))

    both = flux(*ghost[:3]) + flux(*cell[:3])
    spread = jnp.maximum(ghost[3], cell[3]) * (cell[0] - ghost[0])
    return both - jnp.where(low, spread, -spread)


def y_part(own, border):
    lane, sub = lane_of(), sub_of()
    low, high = lane < PX, lane >= LANE - PX
    first, last = low & (sub == 0), high & (sub == SUB - 1)
    u, wave = own[:FIELDS], own[WAVE_Y]
    flux = half_flux(u, own[VY], own[PRESSURE], 2)
    face = jnp.maximum(below(wave, low), wave)
    part = []
    for f in range(FIELDS):
        south_flux = below(flux[f], low) + flux[f] - face * (u[f] - below(u[f], low))
        edge = jnp.broadcast_to(border[f : f + 1, :], (SUB, LANE))
        south_flux = jnp.where(first, edge, south_flux)
        part.append(south_flux - jnp.where(last, edge, above(south_flux, high)))
    return part


def top_speed(u):
    vx, vy, _, sound = primitive(u)
    return jnp.maximum(jnp.abs(vx), jnp.abs(vy)) + sound


def pack_kernel(parts, tiles, rows, patches, patch_ref, box_ref, which_ref, start_ref, pay_ref, meta_ref):
    me = lax.axis_index("gy")
    top = None
    for s in range(SUB):
        wave = top_speed([patch_ref[0, 0, f, :, s * LANE : (s + 1) * LANE] for f in range(FIELDS)])
        top = wave if top is None else jnp.maximum(top, wave)
    pieces = [box_ref[pl.ds(f * BOX_ROWS + me * tiles, tiles), :] for f in range(FIELDS)]
    for k in range(parts):
        for f in range(FIELDS):
            at = k * rows + f * tiles
            pay_ref[at : at + tiles, :] = pieces[f]
        pay_ref[(k + 1) * rows - SUB : (k + 1) * rows, :] = top

    start = start_ref[0, 0]
    row = lax.shift_right_logical(start * 2675, 17)
    offset = BOX * (row & 1) + start - row * STRIDE
    near = lax.shift_right_logical(row, 1) - me * tiles
    mine = (near >= 0) & (near < tiles)
    patch = lax.broadcasted_iota(jnp.int32, start.shape, 1)
    meta_ref[0:4, 0:patches] = which_ref[0, 0] * rows + jnp.where(mine, near, 0)
    meta_ref[4:8, 0:patches] = (HALF * (patch & (SUB - 1)) - offset) & (LANE - 1)
    meta_ref[8:12, 0:patches] = jnp.where(mine, patch & (SUB - 1), -1)


def strip_kernel(parts, rows, tiles, patches, meta_ref, pay_ref, out_ref):
    top = pay_ref[rows - SUB : rows, :]
    for k in range(1, parts):
        top = jnp.maximum(top, pay_ref[(k + 1) * rows - SUB : (k + 1) * rows, :])
    block = lane_of() // HALF
    lines = 4 * patches // SUB
    out_ref[FIELDS * lines :, :] = top

    def line(v, carry):
        side, first = v // (patches // SUB), v % (patches // SUB) * SUB
        acc = jnp.zeros((SUB, LANE), jnp.float32)
        for m in range(SUB):
            p = first + m
            at, shift, fills = meta_ref[side, p], meta_ref[4 + side, p], meta_ref[8 + side, p]
            strip = pay_ref[pl.ds(at, FIELDS, stride=tiles), :]
            strip = jnp.concatenate([strip, jnp.zeros((SUB - FIELDS, LANE), jnp.float32)], axis=0)
            acc = jnp.where(block == fills, pltpu.roll(strip, shift, 1), acc)
        out_ref[pl.ds(v, FIELDS, stride=lines), :] = acc[:FIELDS, :]
        return carry

    lax.fori_loop(0, lines, line, 0)


def step_kernel(sources, count, patches, slots, around_ref, owner_ref, *refs):
    group = len(sources)
    raw_refs, strip_refs, out_ref = refs[:group], refs[group : 2 * group], refs[2 * group]
    cells, states, strips, placed, items = refs[2 * group + 1 :]
    me = lax.axis_index("gy")
    lines = 4 * patches // SUB
    capacity = slots // group
    side_base = patches * FULL
    row_base = side_base + 2 * patches * SIDE

    for i in range(slots):
        items[patches + i] = -1

    def rank_source(source, carry):
        rank = jnp.int32(0)
        for i in range(count):
            p = source * count + i
            items[p] = p
            hit = owner_ref[0, 0, 0, p] == me
            items[patches + jnp.where(hit, source * capacity + rank, slots)] = p
            rank = rank + jnp.where(hit, 1, 0)
        return carry

    lax.fori_loop(0, group, rank_source, 0)

    def take_field(f, carry):
        for k in range(group):
            base = sources[k](me) * (count * ROWS) + f * SUB
            for s in range(SUB):
                states[pl.ds(base + s, count, stride=ROWS), :] = raw_refs[k][0, 0, f, :, s * LANE : (s + 1) * LANE]
        return carry

    lax.fori_loop(0, FIELDS, take_field, 0)

    def joined(at, join):
        return functools.reduce(join, [ref[at : at + SUB, :] for ref in strip_refs])

    for h in range(lines // SUB):
        u = [joined(f * lines + h * SUB, jnp.add) for f in range(FIELDS)]
        for q, plane in enumerate(with_primitives(u)):
            strips[q * lines + h * SUB : q * lines + (h + 1) * SUB, :] = plane
    time_step = courant / jnp.max(joined(FIELDS * lines, jnp.maximum))
    lane, sub = lane_of(), sub_of()
    down = 2 * sub + lane // (2 * PX)
    along = HALF * sub + (lane & (PX - 1)) // 2

    def wide(q, v, pick):
        return take_lanes(jnp.broadcast_to(strips[pl.ds(q * lines + v, 1), :], (SUB, LANE)), pick)

    def coarse_sides(r, carry):
        v = r // 2
        for m in range(SUB // 2):
            turn = r % 2 * (SUB // 2) + m
            first = pl.multiple_of(side_base + (v * SUB + turn) * SIDE, SUB)
            for q in range(X_PLANES):
                cells[pl.ds(first + q * SUB, SUB), :] = wide(q, v, HALF * turn + down)
        return carry

    lax.fori_loop(0, lines, coarse_sides, 0)

    def coarse_rows(v, carry):
        first = pl.multiple_of(row_base + v * FULL, SUB)
        for q in range(PLANES):
            cells[pl.ds(first + q * SUB, SUB), :] = wide(q, lines // 2 + v, along)
        return carry

    lax.fori_loop(0, lines // 2, coarse_rows, 0)

    def change_of(p):
        near = [around_ref[0, 0, side, p] for side in range(4)]
        first = pl.multiple_of(p * FULL, SUB)

        def beside(side):
            base = jnp.where(near[side] >= 0, near[side] * FULL, side_base + (side * patches + p) * SIDE)
            base = pl.multiple_of(base, SUB)
            return [cells[pl.ds(base + q * SUB, SUB), :] for q in range(X_PLANES)]

        def facing(side, row):
            line = (side - SOUTH) * patches + p
            at_coarse = row_base + line // SUB * FULL + line % SUB
            return jnp.where(near[side] >= 0, near[side] * FULL + row, at_coarse)

        def rows_at(at):
            return [cells[pl.ds(at, SUB, stride=SUB), :]] + [
                jnp.broadcast_to(cells[pl.ds(at + q * SUB, 1), :], (SUB, LANE)) for q in (VY, PRESSURE, WAVE_Y)
            ]

        own = [cells[pl.ds(first + q * SUB, SUB), :] for q in range(PLANES)]
        across = x_part(own, beside(WEST), beside(EAST))
        border = [rows_at(at) for at in (first, first + SUB - 1, facing(SOUTH, SUB - 1), facing(NORTH, 0))]
        along = y_part(own, y_border(*border))
        return own, [a + b for a, b in zip(across, along)]

    def section(stage, carry):
        start = stage * (patches * ROWS)

        def prepare(i, carry):
            for b in range(SUB):
                p = i * SUB + b
                first = pl.multiple_of(start + p * ROWS, SUB)
                u = [states[pl.ds(first + f * SUB, SUB), :] for f in range(FIELDS)]
                first = pl.multiple_of(p * FULL, SUB)
                for q, plane in enumerate(with_primitives(u)):
                    cells[pl.ds(first + q * SUB, SUB), :] = plane
            return carry

        lax.fori_loop(0, patches // SUB, prepare, 0)

        def advance(i, carry):
            made = []
            for b in range(BATCH):
                p = jnp.maximum(items[stage * patches + i * BATCH + b], 0)
                own, change = change_of(p)
                made.append([own[f] + time_step * change[f] for f in range(FIELDS)])
            for b in range(BATCH):
                first = pl.multiple_of(start + (patches + i * BATCH + b) * ROWS, SUB)
                for f in range(FIELDS):
                    states[pl.ds(first + f * SUB, SUB), :] = made[b][f]
            return carry

        lax.fori_loop(0, jnp.where(stage == 0, patches, slots) // BATCH, advance, 0)
        return carry

    lax.fori_loop(0, 2, section, 0)

    def finish(j, carry):
        p = items[patches + j]
        old = pl.multiple_of(jnp.maximum(p, 0) * ROWS, SUB)
        new = pl.multiple_of((2 * patches + j) * ROWS, SUB)
        for f in range(FIELDS):
            end = 0.5 * states[pl.ds(old + f * SUB, SUB), :] + 0.5 * states[pl.ds(new + f * SUB, SUB), :]
            at = (f * (slots // SUB) + j // SUB) * (SUB * SUB) + j % SUB
            placed[pl.ds(at, SUB, stride=SUB), :] = jnp.where(p >= 0, end, 0.0)
        return carry

    lax.fori_loop(0, slots, finish, 0)

    def write(f, carry):
        for t in range(slots // SUB):
            for s in range(SUB):
                at = pl.multiple_of(((f * (slots // SUB) + t) * SUB + s) * SUB, SUB)
                out_ref[0, 0, f, t * SUB : (t + 1) * SUB, s * LANE : (s + 1) * LANE] = placed[pl.ds(at, SUB), :]
        return carry

    lax.fori_loop(0, FIELDS, write, 0)


def limit(*row_counts):
    return pltpu.CompilerParams(vmem_limit_bytes=(sum(row_counts) * LANE * 4 * 5 // 4) + (1 << 20))


def per_device(patch_state, coarse_boxes, new_owner, neighbors, coarse_box, coarse_start):
    count = patch_state.shape[2]
    n_gx, n_gz, group = lax.axis_size("gx"), lax.axis_size("gz"), lax.axis_size("gy")
    parts = n_gx * n_gz
    patches = count * group
    lines = 4 * patches // SUB
    slots = group * max(2, 2 * count // group)
    tiles = BOX_ROWS // group
    rows = -(-tiles * FIELDS // SUB) * SUB + SUB
    strip_rows = FIELDS * lines + SUB
    vmem = pl.BlockSpec(memory_space=pltpu.VMEM)
    smem = pl.BlockSpec(memory_space=pltpu.SMEM)
    f32 = jnp.float32

    def sides_first(x):
        return jnp.swapaxes(x, 2, 3)

    def to_group(x):
        blocks = [x]
        for mask in masks_of(group):
            blocks = blocks + [lax.ppermute(b, "gy", [(i, i ^ mask) for i in range(group)]) for b in blocks]
        return blocks

    sources = [lambda me: me]
    for mask in masks_of(group):
        sources = sources + [lambda me, f=f, mask=mask: f(me) ^ mask for f in sources]

    raw = sides_first(patch_state)
    raws = to_group(raw)

    payload, meta = pl.pallas_call(
        functools.partial(pack_kernel, parts, tiles, rows, patches),
        out_shape=(
            jax.ShapeDtypeStruct((parts * rows, LANE), f32),
            jax.ShapeDtypeStruct((16, max(LANE, patches)), jnp.int32),
        ),
        in_specs=[vmem] * 4,
        out_specs=(vmem,) * 2,
        compiler_params=limit(parts * rows, count * ROWS, FIELDS * BOX_ROWS),
        name="pack",
    )(raw, coarse_boxes.reshape(FIELDS * BOX_ROWS, LANE), sides_first(coarse_box), sides_first(coarse_start))

    payload = lax.all_to_all(payload, ("gx", "gz"), split_axis=0, concat_axis=0, tiled=True)

    strip = pl.pallas_call(
        functools.partial(strip_kernel, parts, rows, tiles, patches),
        out_shape=jax.ShapeDtypeStruct((strip_rows, LANE), f32),
        in_specs=[smem, vmem],
        out_specs=vmem,
        compiler_params=limit(parts * rows, strip_rows),
        name="strips",
    )(meta, payload)
    strips = to_group(strip)

    scratch_rows = [
        patches * FULL + 2 * patches * SIDE + lines // 2 * FULL,
        (2 * patches + slots) * ROWS,
        PLANES * lines,
        FIELDS * slots * SUB,
    ]
    out = pl.pallas_call(
        functools.partial(step_kernel, sources, count, patches, slots),
        out_shape=jax.ShapeDtypeStruct((1, 1, FIELDS, slots, SUB * LANE), f32),
        in_specs=[smem, smem] + [vmem] * (2 * group),
        out_specs=vmem,
        scratch_shapes=[pltpu.VMEM((n, LANE), f32) for n in scratch_rows]
        + [pltpu.SMEM((patches + slots + 1,), jnp.int32)],
        compiler_params=limit(*scratch_rows, patches * ROWS, group * strip_rows, FIELDS * slots * SUB),
        name="step",
    )(sides_first(neighbors), sides_first(new_owner), *raws, *strips)
    return sides_first(out)


def solution(mesh):
    in_specs = (
        P("gx", "gz", "gy", None, None),
        P(("gx", "gz"), None, None),
        P("gx", "gz", None, None),
        P("gx", "gz", None, None),
        P("gx", "gz", None, None),
        P("gx", "gz", None, None),
    )
    out_specs = P("gx", "gz", "gy", None, None)
    return jax.shard_map(
        per_device, mesh=mesh, in_specs=in_specs, out_specs=out_specs, check_vma=False
    )
```

```python
import functools

import jax
import jax.numpy as jnp
from jax import lax
from jax.experimental import pallas as pl
from jax.experimental.pallas import tpu as pltpu
from jax.sharding import PartitionSpec as P

FIELDS = 5
PX = 32
BOX = 64
SUB = 8
LANE = 128
HALF = PX // 2
STRIDE = BOX - HALF + 1
BOX_ROWS = BOX * BOX // LANE
heat_ratio = 1.4
courant = 0.3
WEST, EAST, SOUTH, NORTH = range(4)
BLOCKS = LANE // PX
DEEP = PX // BLOCKS
SPAN = PX + 2 * SUB
PLANE = (DEEP + 2) * SPAN
FACES = PX + SUB
AUX = 2 * (FIELDS + 1)


def spot(row, column):
    return (row + 1) * SPAN + SUB + column


def masks_of(n):
    return [n >> (i + 1) for i in range(n.bit_length() - 1)]


def primitive(u):
    inverse = 1.0 / u[0]
    vx, vy, vz = u[1] * inverse, u[2] * inverse, u[3] * inverse
    kinetic = u[1] * (0.5 * vx) + u[2] * (0.5 * vy) + u[3] * (0.5 * vz)
    pressure = (heat_ratio - 1.0) * (u[4] - kinetic)
    sound = jnp.sqrt(heat_ratio * pressure * inverse)
    return vx, vy, pressure, sound


def half_flux(u, moving, pressure, sound, normal):
    half = 0.5 * moving
    flux = [u[f] * half for f in range(FIELDS)]
    flux[normal] = flux[normal] + 0.5 * pressure
    flux[4] = flux[4] + pressure * half
    return flux + [0.5 * (jnp.abs(moving) + sound)]


def face_flux(low_u, low_aux, u, aux):
    wave = jnp.maximum(low_aux[FIELDS], aux[FIELDS])
    return [low_aux[f] + aux[f] - wave * (u[f] - low_u[f]) for f in range(FIELDS)]


def lane_of():
    return lax.broadcasted_iota(jnp.int32, (SUB, LANE), 1)


def sub_of():
    return lax.broadcasted_iota(jnp.int32, (SUB, LANE), 0)


def take_lanes(x, lanes):
    return jnp.take_along_axis(x, lanes, axis=1, mode="promise_in_bounds")


def top_speed(u):
    vx, vy, _, sound = primitive(u)
    return jnp.maximum(jnp.abs(vx), jnp.abs(vy)) + sound


def pack_kernel(parts, tiles, rows, patches, patch_ref, box_ref, which_ref, start_ref, pay_ref, meta_ref):
    me = lax.axis_index("gy")
    top = None
    for s in range(SUB):
        wave = top_speed([patch_ref[0, 0, f, :, s * LANE : (s + 1) * LANE] for f in range(FIELDS)])
        top = wave if top is None else jnp.maximum(top, wave)
    pieces = [box_ref[pl.ds(f * BOX_ROWS + me * tiles, tiles), :] for f in range(FIELDS)]
    for k in range(parts):
        for f in range(FIELDS):
            at = k * rows + f * tiles
            pay_ref[at : at + tiles, :] = pieces[f]
        pay_ref[(k + 1) * rows - SUB : (k + 1) * rows, :] = top

    start = start_ref[0, 0]
    row = lax.shift_right_logical(start * 2675, 17)
    offset = BOX * (row & 1) + start - row * STRIDE
    near = lax.shift_right_logical(row, 1) - me * tiles
    mine = (near >= 0) & (near < tiles)
    patch = lax.broadcasted_iota(jnp.int32, start.shape, 1)
    meta_ref[0:4, 0:patches] = which_ref[0, 0] * rows + jnp.where(mine, near, 0)
    meta_ref[4:8, 0:patches] = (HALF * (patch & (SUB - 1)) - offset) & (LANE - 1)
    meta_ref[8:12, 0:patches] = jnp.where(mine, patch & (SUB - 1), -1)


def strip_kernel(parts, rows, tiles, patches, meta_ref, pay_ref, out_ref):
    top = pay_ref[rows - SUB : rows, :]
    for k in range(1, parts):
        top = jnp.maximum(top, pay_ref[(k + 1) * rows - SUB : (k + 1) * rows, :])
    block = lane_of() // HALF
    lines = 4 * patches // SUB
    out_ref[FIELDS * lines :, :] = top

    for v in range(lines):
        side, first = v // (patches // SUB), v % (patches // SUB) * SUB
        acc = jnp.zeros((SUB, LANE), jnp.float32)
        for m in range(SUB):
            p = first + m
            at, shift, fills = meta_ref[side, p], meta_ref[4 + side, p], meta_ref[8 + side, p]
            strip = pay_ref[pl.ds(at, FIELDS, stride=tiles), :]
            strip = jnp.concatenate([strip, jnp.zeros((SUB - FIELDS, LANE), jnp.float32)], axis=0)
            acc = jnp.where(block == fills, pltpu.roll(strip, shift, 1), acc)
        out_ref[pl.ds(v, FIELDS, stride=lines), :] = acc[:FIELDS, :]


def step_kernel(group, count, patches, slots, around_ref, owner_ref, *refs):
    raw_refs, strip_refs, out_ref = refs[:group], refs[group : 2 * group], refs[2 * group]
    first_u, second_u, aux_ref, dx_ref, strips, doubled, coarse_ref, table, slot_ref = refs[2 * group + 1 :]
    me = lax.axis_index("gy")
    lines = 4 * patches // SUB
    capacity = slots // group
    sets = patches // PX
    lane, sub = lane_of(), sub_of()
    block, in_block = lane // PX, lane & (PX - 1)
    turn = me * count

    for i in range(slots):
        slot_ref[i] = -1

    def rank_source(source, carry):
        rank = jnp.int32(0)
        for i in range(count):
            p = source * count + i
            hit = owner_ref[0, 0, 0, p] == me
            slot_ref[jnp.where(hit, source * capacity + rank, slots)] = p
            rank = rank + jnp.where(hit, 1, 0)
        return carry

    lax.fori_loop(0, group, rank_source, 0)

    def take_field(f, carry):
        for g in range(sets):
            base = (g * FIELDS + f) * PLANE
            for h in range(2):
                tiles = []
                for q in range(BLOCKS):
                    at = (q * 2 + h) * LANE
                    for k in range(PX // count):
                        tiles.append(raw_refs[g * (PX // count) + k][0, 0, f, :, at : at + LANE])
                cells = jnp.concatenate(tiles, axis=0).T
                for i in range(BLOCKS):
                    to = pl.multiple_of(base + spot(h * BLOCKS + i, 0), SUB)
                    first_u[pl.ds(to, PX), :] = cells[i * PX : (i + 1) * PX, :]
        return carry

    lax.fori_loop(0, FIELDS, take_field, 0)

    def joined(at, join):
        return functools.reduce(join, [ref[at : at + SUB, :] for ref in strip_refs])

    for at in range(0, FIELDS * lines, SUB):
        strips[at : at + SUB, :] = joined(at, jnp.add)
    time_step = courant / jnp.max(joined(FIELDS * lines, jnp.maximum))
    part = HALF * sub + (lane & (HALF - 1))
    for t in range(4 * patches // LANE):
        tiles = []
        for v in range(t * HALF, (t + 1) * HALF):
            tile = None
            for f in range(FIELDS):
                row = jnp.broadcast_to(strips[f * lines + v : f * lines + v + 1, :], (SUB, LANE))
                wide = take_lanes(row, part)
                tile = wide if tile is None else jnp.where(lane // HALF == f, wide, tile)
            tiles.append(tile)
        cells = jnp.concatenate(tiles, axis=0).T
        for n in range(FIELDS * 2):
            for twice in range(2):
                at = t * FIELDS * PX + n * HALF + twice
                doubled[pl.ds(at, SUB, stride=2), :] = cells[n * SUB : (n + 1) * SUB, :]

    table[0:4, 0:patches] = around_ref[0, 0]
    picks, origins, coarses = [], [], []
    for g in range(sets):
        patch = (g * PX + in_block) ^ turn
        for side in range(4):
            near = take_lanes(jnp.broadcast_to(table[side : side + 1, :], (SUB, LANE)), patch)
            place = jnp.maximum(near, 0) ^ turn
            pick, origin = place & (PX - 1), lax.shift_right_logical(place, 5)
            lacking = jnp.where(near < 0, 1, 0)
            if side in (WEST, EAST):
                pick = pick + PX * block
            else:
                edge, step = (0, -PX) if side == SOUTH else (BLOCKS - 1, PX)
                across = pick + (LANE - PX if side == SOUTH else 0)
                pick = jnp.where(block == edge, across, lane + step)
                origin = jnp.where(block == edge, origin, g)
                lacking = jnp.where(block == edge, lacking, 0)
            picks.append(pick)
            origins.append(origin)
            coarses.append(lacking)

    def coarse_field(f, carry):
        for g in range(sets):
            patch = (g * PX + in_block) ^ turn
            base = (g * FIELDS + f) * (10 * SUB)
            for side in range(4):
                t, shift = side * patches // LANE, side * patches % LANE
                pieces = [
                    take_lanes(
                        doubled[pl.ds(pl.multiple_of(t * FIELDS * PX + f * PX + SUB * i, SUB), SUB), :], patch + shift
                    )
                    for i in range(BLOCKS)
                ]
                if side in (WEST, EAST):
                    x = pieces[0]
                    for q in range(1, BLOCKS):
                        x = jnp.where(block == q, pieces[q], x)
                    coarse_ref[pl.ds(pl.multiple_of(base + side * SUB, SUB), SUB), :] = x
                else:
                    for i in range(BLOCKS):
                        to = base + (2 + (side - SOUTH) * BLOCKS + i) * SUB
                        coarse_ref[pl.ds(pl.multiple_of(to, SUB), SUB), :] = pieces[i]
        return carry

    lax.fori_loop(0, FIELDS, coarse_field, 0)

    def fill_ghosts(u_ref):
        def field(f, carry):
            bases = [pl.multiple_of((g * FIELDS + f) * PLANE, SUB) for g in range(sets)]

            def ghost(g, side, load, kept):
                x = None
                for o in range(sets):
                    moved = take_lanes(load(bases[o]), picks[4 * g + side])
                    x = moved if x is None else jnp.where(origins[4 * g + side] == o, moved, x)
                at = pl.multiple_of(((g * FIELDS + f) * 10 + kept) * SUB, SUB)
                return jnp.where(coarses[4 * g + side] != 0, coarse_ref[pl.ds(at, SUB), :], x)

            made = []
            for g in range(sets):
                for side, column, to in ((WEST, PX - 1, -1), (EAST, 0, PX)):
                    x = ghost(g, side, lambda b, c=column: u_ref[pl.ds(b + spot(0, c), DEEP, stride=SPAN), :], side)
                    made.append((pl.ds(bases[g] + spot(0, to), DEEP, stride=SPAN), x))
                for side, row, to in ((SOUTH, DEEP - 1, -1), (NORTH, 0, DEEP)):
                    for i in range(BLOCKS):
                        x = ghost(
                            g,
                            side,
                            lambda b, r=row, i=i: u_ref[pl.ds(b + spot(r, SUB * i), SUB), :],
                            2 + (side - SOUTH) * BLOCKS + i,
                        )
                        made.append((pl.ds(bases[g] + spot(to, SUB * i), SUB), x))
            for at, x in made:
                u_ref[at, :] = x
            return carry

        lax.fori_loop(0, FIELDS, field, 0)

    def halves(u_ref, g, rows, axes):
        u = [u_ref[rows((g * FIELDS + f) * PLANE), :] for f in range(FIELDS)]
        vx, vy, pressure, sound = primitive(u)
        for axis in axes:
            made = half_flux(u, (vx, vy)[axis], pressure, sound, axis + 1)
            for n, x in enumerate(made):
                aux_ref[rows((g * AUX + axis * (FIELDS + 1) + n) * PLANE), :] = x

    def section(u_ref, to_ref, last):
        fill_ghosts(u_ref)
        for g in range(sets):

            def cells(r, carry):
                for i in range(BLOCKS):
                    halves(u_ref, g, lambda b, i=i: pl.ds(pl.multiple_of(b + spot(r, SUB * i), SUB), SUB), (0, 1))
                return carry

            lax.fori_loop(0, DEEP, cells, 0)
            for r in (-1, DEEP):
                for i in range(BLOCKS):
                    halves(u_ref, g, lambda b, r=r, i=i: pl.ds(b + spot(r, SUB * i), SUB), (1,))
            for c in (-1, PX):
                halves(u_ref, g, lambda b, c=c: pl.ds(b + spot(0, c), DEEP, stride=SPAN), (0,))

        for g in range(sets):

            def load(at, axis):
                u = [u_ref[pl.ds((g * FIELDS + f) * PLANE + at, SUB), :] for f in range(FIELDS)]
                start = g * AUX + axis * (FIELDS + 1)
                return u, [aux_ref[pl.ds((start + n) * PLANE + at, SUB), :] for n in range(FIELDS + 1)]

            def across(r, carry):
                for i in range(BLOCKS + 1):
                    at = pl.multiple_of(spot(r, SUB * i), SUB)
                    faces = face_flux(*load(at - 1, 0), *load(at, 0))
                    for f in range(FIELDS):
                        to = pl.multiple_of((f * DEEP + r) * FACES + SUB * i, SUB)
                        dx_ref[pl.ds(to, SUB), :] = faces[f]
                return carry

            lax.fori_loop(0, DEEP, across, 0)

            def along(i, carry):
                low_u, low_aux = load(pl.multiple_of(spot(-1, SUB * i), SUB), 1)
                low_faces = None
                for r in range(DEEP + 1):
                    u, aux = load(pl.multiple_of(spot(r, SUB * i), SUB), 1)
                    faces = face_flux(low_u, low_aux, u, aux)
                    for f in range(FIELDS):
                        if r == 0:
                            continue
                        west = pl.multiple_of((f * DEEP + r - 1) * FACES + SUB * i, SUB)
                        change = dx_ref[pl.ds(west, SUB), :] - dx_ref[pl.ds(west + 1, SUB), :]
                        change = change + (low_faces[f] - faces[f])
                        new = low_u[f] + time_step * change
                        to = pl.ds(pl.multiple_of((g * FIELDS + f) * PLANE + spot(r - 1, SUB * i), SUB), SUB)
                        to_ref[to, :] = 0.5 * to_ref[to, :] + 0.5 * new if last else new
                    low_u, low_aux, low_faces = u, aux, faces
                return carry

            lax.fori_loop(0, BLOCKS, along, 0)

    section(first_u, second_u, False)
    section(second_u, first_u, True)

    held = jnp.full((SUB, LANE), -1, jnp.int32)
    for j in range(slots):
        held = jnp.where(in_block == j, slot_ref[j], held)
    place = jnp.maximum(held, 0) ^ turn
    pick, origin = PX * block + (place & (PX - 1)), lax.shift_right_logical(place, 5)

    def give_field(f, carry):
        for h in range(2):
            tiles = []
            for i in range(LANE // SUB):
                at = spot(h * BLOCKS + i // BLOCKS, SUB * (i % BLOCKS))
                x = None
                for g in range(sets):
                    from_set = pl.ds(pl.multiple_of((g * FIELDS + f) * PLANE + at, SUB), SUB)
                    moved = take_lanes(first_u[from_set, :], pick)
                    x = moved if x is None else jnp.where(origin == g, moved, x)
                tiles.append(jnp.where(held >= 0, x, 0.0))
            cells = jnp.concatenate(tiles, axis=0).T
            for q in range(BLOCKS):
                at = (q * 2 + h) * LANE
                out_ref[0, 0, f, :, at : at + LANE] = cells[q * PX : q * PX + slots, :]
        return carry

    lax.fori_loop(0, FIELDS, give_field, 0)


def limit(*row_counts):
    return pltpu.CompilerParams(vmem_limit_bytes=(sum(row_counts) * LANE * 4 * 5 // 4) + (1 << 20))


def per_device(patch_state, coarse_boxes, new_owner, neighbors, coarse_box, coarse_start):
    count = patch_state.shape[2]
    n_gx, n_gz, group = lax.axis_size("gx"), lax.axis_size("gz"), lax.axis_size("gy")
    parts = n_gx * n_gz
    patches = count * group
    lines = 4 * patches // SUB
    slots = group * max(2, 2 * count // group)
    tiles = BOX_ROWS // group
    rows = -(-tiles * FIELDS // SUB) * SUB + SUB
    strip_rows = FIELDS * lines + SUB
    vmem = pl.BlockSpec(memory_space=pltpu.VMEM)
    smem = pl.BlockSpec(memory_space=pltpu.SMEM)
    f32 = jnp.float32

    def sides_first(x):
        return jnp.swapaxes(x, 2, 3)

    def to_group(x):
        blocks = [x] + [None] * (group - 1)
        have = [0]
        for mask in masks_of(group):
            for k in have:
                blocks[k ^ mask] = lax.ppermute(blocks[k], "gy", [(i, i ^ mask) for i in range(group)])
            have = have + [k ^ mask for k in have]
        return blocks

    raw = sides_first(patch_state)
    raws = [raw] + [lax.ppermute(raw, "gy", [(i, i ^ k) for i in range(group)]) for k in range(1, group)]

    payload, meta = pl.pallas_call(
        functools.partial(pack_kernel, parts, tiles, rows, patches),
        out_shape=(
            jax.ShapeDtypeStruct((parts * rows, LANE), f32),
            jax.ShapeDtypeStruct((16, max(LANE, patches)), jnp.int32),
        ),
        in_specs=[vmem] * 4,
        out_specs=(vmem,) * 2,
        name="pack",
    )(raw, coarse_boxes.reshape(FIELDS * BOX_ROWS, LANE), sides_first(coarse_box), sides_first(coarse_start))

    payload = lax.all_to_all(payload, ("gx", "gz"), split_axis=0, concat_axis=0, tiled=True)

    strip = pl.pallas_call(
        functools.partial(strip_kernel, parts, rows, tiles, patches),
        out_shape=jax.ShapeDtypeStruct((strip_rows, LANE), f32),
        in_specs=[smem, vmem],
        out_specs=vmem,
        compiler_params=limit(parts * rows, strip_rows),
        name="strips",
    )(meta, payload)
    strips = to_group(strip)

    sets = patches // PX
    scratch_rows = [
        sets * FIELDS * PLANE,
        sets * FIELDS * PLANE,
        sets * AUX * PLANE,
        FIELDS * DEEP * FACES,
        FIELDS * lines,
        4 * patches // LANE * FIELDS * PX,
        sets * FIELDS * 10 * SUB,
    ]
    out = pl.pallas_call(
        functools.partial(step_kernel, group, count, patches, slots),
        out_shape=jax.ShapeDtypeStruct((1, 1, FIELDS, slots, SUB * LANE), f32),
        in_specs=[vmem, smem] + [vmem] * (2 * group),
        out_specs=vmem,
        scratch_shapes=[pltpu.VMEM((n, LANE), f32) for n in scratch_rows]
        + [pltpu.VMEM((SUB, LANE), jnp.int32), pltpu.SMEM((slots + 1,), jnp.int32)],
        compiler_params=limit(*scratch_rows, 2 * patches * FIELDS * SUB, group * strip_rows, FIELDS * slots * SUB),
        name="step",
    )(sides_first(neighbors), sides_first(new_owner), *raws, *strips)
    return sides_first(out)


def solution(mesh):
    in_specs = (
        P("gx", "gz", "gy", None, None),
        P(("gx", "gz"), None, None),
        P("gx", "gz", None, None),
        P("gx", "gz", None, None),
        P("gx", "gz", None, None),
        P("gx", "gz", None, None),
    )
    out_specs = P("gx", "gz", "gy", None, None)
    return jax.shard_map(
        per_device, mesh=mesh, in_specs=in_specs, out_specs=out_specs, check_vma=False
    )
```

```python
import functools

import jax
import jax.numpy as jnp
from jax import lax
from jax.experimental import pallas as pl
from jax.experimental.pallas import tpu as pltpu
from jax.sharding import PartitionSpec as P

FIELDS = 5
PX = 32
BOX = 64
SUB = 8
LANE = 128
HALF = PX // 2
STRIDE = BOX - HALF + 1
BOX_ROWS = BOX * BOX // LANE
heat_ratio = 1.4
courant = 0.3
WEST, EAST, SOUTH, NORTH = range(4)
BLOCKS = LANE // PX
DEEP = PX // BLOCKS
SPAN = PX + 2 * SUB
PLANE = (DEEP + 2) * SPAN
FACES = PX + SUB
AUX = 2 * (FIELDS + 1)


def spot(row, column):
    return (row + 1) * SPAN + SUB + column


def power_of_two(n):
    return n & (n - 1) == 0


def masks_of(n):
    return [n >> (i + 1) for i in range(n.bit_length() - 1)]


def primitive(u):
    inverse = 1.0 / u[0]
    vx, vy, vz = u[1] * inverse, u[2] * inverse, u[3] * inverse
    kinetic = u[1] * (0.5 * vx) + u[2] * (0.5 * vy) + u[3] * (0.5 * vz)
    pressure = (heat_ratio - 1.0) * (u[4] - kinetic)
    sound = jnp.sqrt(heat_ratio * pressure * inverse)
    return vx, vy, pressure, sound


def half_flux(u, moving, pressure, sound, normal):
    half = 0.5 * moving
    flux = [u[f] * half for f in range(FIELDS)]
    flux[normal] = flux[normal] + 0.5 * pressure
    flux[4] = flux[4] + pressure * half
    return flux + [0.5 * (jnp.abs(moving) + sound)]


def face_flux(low_u, low_aux, u, aux):
    wave = jnp.maximum(low_aux[FIELDS], aux[FIELDS])
    return [low_aux[f] + aux[f] - wave * (u[f] - low_u[f]) for f in range(FIELDS)]


def lane_of():
    return lax.broadcasted_iota(jnp.int32, (SUB, LANE), 1)


def sub_of():
    return lax.broadcasted_iota(jnp.int32, (SUB, LANE), 0)


def take_lanes(x, lanes):
    return jnp.take_along_axis(x, lanes, axis=1, mode="promise_in_bounds")


def top_speed(u):
    vx, vy, _, sound = primitive(u)
    return jnp.maximum(jnp.abs(vx), jnp.abs(vy)) + sound


def place_of(me, other, n):
    if power_of_two(n):
        return me ^ other
    behind = me - other
    return jnp.where(behind < 0, behind + n, behind)


def pack_kernel(tiles, rows, patches, mesh_sizes, patch_ref, box_ref, which_ref, start_ref, pay_ref, meta_ref):
    n_gx, n_gz = mesh_sizes
    me = lax.axis_index("gy")
    top = None
    for s in range(SUB):
        wave = top_speed([patch_ref[0, 0, f, :, s * LANE : (s + 1) * LANE] for f in range(FIELDS)])
        top = wave if top is None else jnp.maximum(top, wave)
    for f in range(FIELDS):
        pay_ref[f * tiles : (f + 1) * tiles, :] = box_ref[pl.ds(f * BOX_ROWS + me * tiles, tiles), :]
    pay_ref[rows - SUB : rows, :] = top

    start = start_ref[0, 0]
    row = lax.shift_right_logical(start * 2675, 17)
    offset = BOX * (row & 1) + start - row * STRIDE
    near = lax.shift_right_logical(row, 1) - me * tiles
    mine = (near >= 0) & (near < tiles)
    patch = lax.broadcasted_iota(jnp.int32, start.shape, 1)
    which = which_ref[0, 0]
    gz_bits = n_gz.bit_length() - 1
    place = place_of(lax.axis_index("gx"), lax.shift_right_logical(which, gz_bits), n_gx) + n_gx * place_of(
        lax.axis_index("gz"), which & (n_gz - 1), n_gz
    )
    meta_ref[0:4, 0:patches] = place * rows + jnp.where(mine, near, 0)
    meta_ref[4:8, 0:patches] = (HALF * (patch & (SUB - 1)) - offset) & (LANE - 1)
    meta_ref[8:12, 0:patches] = jnp.where(mine, patch & (SUB - 1), -1)


def strip_kernel(parts, rows, tiles, patches, meta_ref, pay_ref, out_ref):
    top = pay_ref[rows - SUB : rows, :]
    for k in range(1, parts):
        top = jnp.maximum(top, pay_ref[(k + 1) * rows - SUB : (k + 1) * rows, :])
    block = lane_of() // HALF
    lines = 4 * patches // SUB
    out_ref[FIELDS * lines :, :] = top

    for v in range(lines):
        side, first = v // (patches // SUB), v % (patches // SUB) * SUB
        acc = jnp.zeros((SUB, LANE), jnp.float32)
        for m in range(SUB):
            p = first + m
            at, shift, fills = meta_ref[side, p], meta_ref[4 + side, p], meta_ref[8 + side, p]
            strip = pay_ref[pl.ds(at, FIELDS, stride=tiles), :]
            strip = jnp.concatenate([strip, jnp.zeros((SUB - FIELDS, LANE), jnp.float32)], axis=0)
            acc = jnp.where(block == fills, pltpu.roll(strip, shift, 1), acc)
        out_ref[pl.ds(v, FIELDS, stride=lines), :] = acc[:FIELDS, :]


def step_kernel(group, count, patches, slots, around_ref, owner_ref, *refs):
    raw_refs, strip_refs, out_ref = refs[:group], refs[group : 2 * group], refs[2 * group]
    first_u, second_u, aux_ref, dx_ref, strips, doubled, coarse_ref, table, slot_ref = refs[2 * group + 1 :]
    me = lax.axis_index("gy")
    lines = 4 * patches // SUB
    capacity = slots // group
    sets = patches // PX
    lane, sub = lane_of(), sub_of()
    block, in_block = lane // PX, lane & (PX - 1)
    turn = me * count

    for i in range(slots):
        slot_ref[i] = -1

    def rank_source(source, carry):
        rank = jnp.int32(0)
        for i in range(count):
            p = source * count + i
            hit = owner_ref[0, 0, 0, p] == me
            slot_ref[jnp.where(hit, source * capacity + rank, slots)] = p
            rank = rank + jnp.where(hit, 1, 0)
        return carry

    lax.fori_loop(0, group, rank_source, 0)

    def take_field(f, carry):
        for g in range(sets):
            base = (g * FIELDS + f) * PLANE
            for h in range(2):
                tiles = []
                for q in range(BLOCKS):
                    at = (q * 2 + h) * LANE
                    for k in range(PX // count):
                        tiles.append(raw_refs[g * (PX // count) + k][0, 0, f, :, at : at + LANE])
                cells = jnp.concatenate(tiles, axis=0).T
                for i in range(BLOCKS):
                    to = pl.multiple_of(base + spot(h * BLOCKS + i, 0), SUB)
                    first_u[pl.ds(to, PX), :] = cells[i * PX : (i + 1) * PX, :]
        return carry

    lax.fori_loop(0, FIELDS, take_field, 0)

    def joined(at, join):
        return functools.reduce(join, [ref[at : at + SUB, :] for ref in strip_refs])

    for at in range(0, FIELDS * lines, SUB):
        strips[at : at + SUB, :] = joined(at, jnp.add)
    time_step = courant / jnp.max(joined(FIELDS * lines, jnp.maximum))
    part = HALF * sub + (lane & (HALF - 1))
    for t in range(4 * patches // LANE):
        tiles = []
        for v in range(t * HALF, (t + 1) * HALF):
            tile = None
            for f in range(FIELDS):
                row = jnp.broadcast_to(strips[f * lines + v : f * lines + v + 1, :], (SUB, LANE))
                wide = take_lanes(row, part)
                tile = wide if tile is None else jnp.where(lane // HALF == f, wide, tile)
            tiles.append(tile)
        cells = jnp.concatenate(tiles, axis=0).T
        for n in range(FIELDS * 2):
            for twice in range(2):
                at = t * FIELDS * PX + n * HALF + twice
                doubled[pl.ds(at, SUB, stride=2), :] = cells[n * SUB : (n + 1) * SUB, :]

    table[0:4, 0:patches] = around_ref[0, 0]
    picks, origins, coarses = [], [], []
    for g in range(sets):
        patch = (g * PX + in_block) ^ turn
        for side in range(4):
            near = take_lanes(jnp.broadcast_to(table[side : side + 1, :], (SUB, LANE)), patch)
            place = jnp.maximum(near, 0) ^ turn
            pick, origin = place & (PX - 1), lax.shift_right_logical(place, 5)
            lacking = jnp.where(near < 0, 1, 0)
            if side in (WEST, EAST):
                pick = pick + PX * block
            else:
                edge, step = (0, -PX) if side == SOUTH else (BLOCKS - 1, PX)
                across = pick + (LANE - PX if side == SOUTH else 0)
                pick = jnp.where(block == edge, across, lane + step)
                origin = jnp.where(block == edge, origin, g)
                lacking = jnp.where(block == edge, lacking, 0)
            picks.append(pick)
            origins.append(origin)
            coarses.append(lacking)

    def coarse_field(f, carry):
        for g in range(sets):
            patch = (g * PX + in_block) ^ turn
            base = (g * FIELDS + f) * (10 * SUB)
            for side in range(4):
                t, shift = side * patches // LANE, side * patches % LANE
                pieces = [
                    take_lanes(
                        doubled[pl.ds(pl.multiple_of(t * FIELDS * PX + f * PX + SUB * i, SUB), SUB), :], patch + shift
                    )
                    for i in range(BLOCKS)
                ]
                if side in (WEST, EAST):
                    x = pieces[0]
                    for q in range(1, BLOCKS):
                        x = jnp.where(block == q, pieces[q], x)
                    coarse_ref[pl.ds(pl.multiple_of(base + side * SUB, SUB), SUB), :] = x
                else:
                    for i in range(BLOCKS):
                        to = base + (2 + (side - SOUTH) * BLOCKS + i) * SUB
                        coarse_ref[pl.ds(pl.multiple_of(to, SUB), SUB), :] = pieces[i]
        return carry

    lax.fori_loop(0, FIELDS, coarse_field, 0)

    def fill_ghosts(u_ref):
        def field(f, carry):
            bases = [pl.multiple_of((g * FIELDS + f) * PLANE, SUB) for g in range(sets)]

            def ghost(g, side, load, kept):
                x = None
                for o in range(sets):
                    moved = take_lanes(load(bases[o]), picks[4 * g + side])
                    x = moved if x is None else jnp.where(origins[4 * g + side] == o, moved, x)
                at = pl.multiple_of(((g * FIELDS + f) * 10 + kept) * SUB, SUB)
                return jnp.where(coarses[4 * g + side] != 0, coarse_ref[pl.ds(at, SUB), :], x)

            made = []
            for g in range(sets):
                for side, column, to in ((WEST, PX - 1, -1), (EAST, 0, PX)):
                    x = ghost(g, side, lambda b, c=column: u_ref[pl.ds(b + spot(0, c), DEEP, stride=SPAN), :], side)
                    made.append((pl.ds(bases[g] + spot(0, to), DEEP, stride=SPAN), x))
                for side, row, to in ((SOUTH, DEEP - 1, -1), (NORTH, 0, DEEP)):
                    for i in range(BLOCKS):
                        x = ghost(
                            g,
                            side,
                            lambda b, r=row, i=i: u_ref[pl.ds(b + spot(r, SUB * i), SUB), :],
                            2 + (side - SOUTH) * BLOCKS + i,
                        )
                        made.append((pl.ds(bases[g] + spot(to, SUB * i), SUB), x))
            for at, x in made:
                u_ref[at, :] = x
            return carry

        lax.fori_loop(0, FIELDS, field, 0)

    def halves(u_ref, g, rows, axes):
        u = [u_ref[rows((g * FIELDS + f) * PLANE), :] for f in range(FIELDS)]
        vx, vy, pressure, sound = primitive(u)
        for axis in axes:
            made = half_flux(u, (vx, vy)[axis], pressure, sound, axis + 1)
            for n, x in enumerate(made):
                aux_ref[rows((g * AUX + axis * (FIELDS + 1) + n) * PLANE), :] = x

    def section(u_ref, to_ref, last):
        fill_ghosts(u_ref)
        for g in range(sets):

            def cells(r, carry):
                for i in range(BLOCKS):
                    halves(u_ref, g, lambda b, i=i: pl.ds(pl.multiple_of(b + spot(r, SUB * i), SUB), SUB), (0, 1))
                return carry

            lax.fori_loop(0, DEEP, cells, 0)
            for r in (-1, DEEP):
                for i in range(BLOCKS):
                    halves(u_ref, g, lambda b, r=r, i=i: pl.ds(b + spot(r, SUB * i), SUB), (1,))
            for c in (-1, PX):
                halves(u_ref, g, lambda b, c=c: pl.ds(b + spot(0, c), DEEP, stride=SPAN), (0,))

        for g in range(sets):

            def load(at, axis):
                u = [u_ref[pl.ds((g * FIELDS + f) * PLANE + at, SUB), :] for f in range(FIELDS)]
                start = g * AUX + axis * (FIELDS + 1)
                return u, [aux_ref[pl.ds((start + n) * PLANE + at, SUB), :] for n in range(FIELDS + 1)]

            def across(r, carry):
                for i in range(BLOCKS + 1):
                    at = pl.multiple_of(spot(r, SUB * i), SUB)
                    faces = face_flux(*load(at - 1, 0), *load(at, 0))
                    for f in range(FIELDS):
                        to = pl.multiple_of((f * DEEP + r) * FACES + SUB * i, SUB)
                        dx_ref[pl.ds(to, SUB), :] = faces[f]
                return carry

            lax.fori_loop(0, DEEP, across, 0)

            def along(i, carry):
                low_u, low_aux = load(pl.multiple_of(spot(-1, SUB * i), SUB), 1)
                low_faces = None
                for r in range(DEEP + 1):
                    u, aux = load(pl.multiple_of(spot(r, SUB * i), SUB), 1)
                    faces = face_flux(low_u, low_aux, u, aux)
                    for f in range(FIELDS):
                        if r == 0:
                            continue
                        west = pl.multiple_of((f * DEEP + r - 1) * FACES + SUB * i, SUB)
                        change = dx_ref[pl.ds(west, SUB), :] - dx_ref[pl.ds(west + 1, SUB), :]
                        change = change + (low_faces[f] - faces[f])
                        new = low_u[f] + time_step * change
                        to = pl.ds(pl.multiple_of((g * FIELDS + f) * PLANE + spot(r - 1, SUB * i), SUB), SUB)
                        to_ref[to, :] = 0.5 * to_ref[to, :] + 0.5 * new if last else new
                    low_u, low_aux, low_faces = u, aux, faces
                return carry

            lax.fori_loop(0, BLOCKS, along, 0)

    section(first_u, second_u, False)
    section(second_u, first_u, True)

    held = jnp.full((SUB, LANE), -1, jnp.int32)
    for j in range(slots):
        held = jnp.where(in_block == j, slot_ref[j], held)
    place = jnp.maximum(held, 0) ^ turn
    pick, origin = PX * block + (place & (PX - 1)), lax.shift_right_logical(place, 5)

    def give_field(f, carry):
        for h in range(2):
            tiles = []
            for i in range(LANE // SUB):
                at = spot(h * BLOCKS + i // BLOCKS, SUB * (i % BLOCKS))
                x = None
                for g in range(sets):
                    from_set = pl.ds(pl.multiple_of((g * FIELDS + f) * PLANE + at, SUB), SUB)
                    moved = take_lanes(first_u[from_set, :], pick)
                    x = moved if x is None else jnp.where(origin == g, moved, x)
                tiles.append(jnp.where(held >= 0, x, 0.0))
            cells = jnp.concatenate(tiles, axis=0).T
            for q in range(BLOCKS):
                at = (q * 2 + h) * LANE
                out_ref[0, 0, f, :, at : at + LANE] = cells[q * PX : q * PX + slots, :]
        return carry

    lax.fori_loop(0, FIELDS, give_field, 0)


def limit(*row_counts):
    return pltpu.CompilerParams(vmem_limit_bytes=(sum(row_counts) * LANE * 4 * 5 // 4) + (1 << 20))


def per_device(patch_state, coarse_boxes, new_owner, neighbors, coarse_box, coarse_start):
    count = patch_state.shape[2]
    n_gx, n_gz, group = lax.axis_size("gx"), lax.axis_size("gz"), lax.axis_size("gy")
    parts = n_gx * n_gz
    patches = count * group
    lines = 4 * patches // SUB
    slots = group * max(2, 2 * count // group)
    tiles = BOX_ROWS // group
    rows = -(-tiles * FIELDS // SUB) * SUB + SUB
    strip_rows = FIELDS * lines + SUB
    vmem = pl.BlockSpec(memory_space=pltpu.VMEM)
    smem = pl.BlockSpec(memory_space=pltpu.SMEM)
    f32 = jnp.float32

    def sides_first(x):
        return jnp.swapaxes(x, 2, 3)

    raw = sides_first(patch_state)
    payload, meta = pl.pallas_call(
        functools.partial(pack_kernel, tiles, rows, patches, (n_gx, n_gz)),
        out_shape=(pltpu.VMEM((rows, LANE), f32), jax.ShapeDtypeStruct((16, max(LANE, patches)), jnp.int32)),
        in_specs=[vmem] * 4,
        out_specs=(vmem,) * 2,
        name="pack",
    )(raw, coarse_boxes.reshape(FIELDS * BOX_ROWS, LANE), sides_first(coarse_box), sides_first(coarse_start))

    def gathered(x, axis, n):
        if power_of_two(n):
            perms = [[(i, i ^ k) for i in range(n)] for k in range(1, n)]
        else:
            perms = [[(i, (i + k) % n) for i in range(n)] for k in range(1, n)]
        return jnp.concatenate([x] + [lax.ppermute(x, axis, perm) for perm in perms], axis=0)

    payload = gathered(gathered(payload, "gx", n_gx), "gz", n_gz)

    strip = pl.pallas_call(
        functools.partial(strip_kernel, parts, rows, tiles, patches),
        out_shape=pltpu.VMEM((strip_rows, LANE), f32),
        in_specs=[smem, vmem],
        out_specs=vmem,
        compiler_params=limit(parts * rows, strip_rows),
        name="strips",
    )(meta, payload)

    def to_group(x, after=None):
        blocks, have = [x] + [None] * (group - 1), [0]
        masks = masks_of(group)
        for mask in masks:
            perm = [(i, i ^ mask) for i in range(group)]
            for k in have:
                block = blocks[k]
                if after is not None and mask == masks[-1] and k:
                    block, _ = lax.optimization_barrier((block, after))
                blocks[k ^ mask] = lax.ppermute(block, "gy", perm)
            have = have + [k ^ mask for k in have]
        return blocks

    raws = to_group(raw, strip)
    strips = to_group(strip)

    sets = patches // PX
    scratch_rows = [
        sets * FIELDS * PLANE,
        sets * FIELDS * PLANE,
        sets * AUX * PLANE,
        FIELDS * DEEP * FACES,
        FIELDS * lines,
        4 * patches // LANE * FIELDS * PX,
        sets * FIELDS * 10 * SUB,
    ]
    out = pl.pallas_call(
        functools.partial(step_kernel, group, count, patches, slots),
        out_shape=jax.ShapeDtypeStruct((1, 1, FIELDS, slots, SUB * LANE), f32),
        in_specs=[vmem, smem] + [vmem] * (2 * group),
        out_specs=vmem,
        scratch_shapes=[pltpu.VMEM((n, LANE), f32) for n in scratch_rows]
        + [pltpu.VMEM((SUB, LANE), jnp.int32), pltpu.SMEM((slots + 1,), jnp.int32)],
        compiler_params=limit(*scratch_rows, 2 * patches * FIELDS * SUB, group * strip_rows, FIELDS * slots * SUB),
        name="step",
    )(sides_first(neighbors), sides_first(new_owner), *raws, *strips)
    return sides_first(out)


def solution(mesh):
    in_specs = (
        P("gx", "gz", "gy", None, None),
        P(("gx", "gz"), None, None),
        P("gx", "gz", None, None),
        P("gx", "gz", None, None),
        P("gx", "gz", None, None),
        P("gx", "gz", None, None),
    )
    out_specs = P("gx", "gz", "gy", None, None)
    return jax.shard_map(
        per_device, mesh=mesh, in_specs=in_specs, out_specs=out_specs, check_vma=False
    )
```

```python
import functools

import jax
import jax.numpy as jnp
from jax import lax
from jax.experimental import pallas as pl
from jax.experimental.pallas import tpu as pltpu
from jax.sharding import PartitionSpec as P

FIELDS = 5
PX = 32
BOX = 64
SUB = 8
LANE = 128
HALF = PX // 2
STRIDE = BOX - HALF + 1
BOX_ROWS = BOX * BOX // LANE
heat_ratio = 1.4
courant = 0.3
WEST, EAST, SOUTH, NORTH = range(4)
BLOCKS = LANE // PX
DEEP = PX // BLOCKS
SPAN = PX + 2 * SUB
PLANE = (DEEP + 2) * SPAN
FACES = PX + SUB
AUX = 2 * (FIELDS + 1)


def spot(row, column):
    return (row + 1) * SPAN + SUB + column


def power_of_two(n):
    return n & (n - 1) == 0


def masks_of(n):
    return [n >> (i + 1) for i in range(n.bit_length() - 1)]


def primitive(u):
    inverse = 1.0 / u[0]
    vx, vy, vz = u[1] * inverse, u[2] * inverse, u[3] * inverse
    kinetic = u[1] * (0.5 * vx) + u[2] * (0.5 * vy) + u[3] * (0.5 * vz)
    pressure = (heat_ratio - 1.0) * (u[4] - kinetic)
    sound = jnp.sqrt(heat_ratio * pressure * inverse)
    return vx, vy, pressure, sound


def half_flux(u, moving, pressure, sound, normal):
    half = 0.5 * moving
    flux = [u[f] * half for f in range(FIELDS)]
    flux[normal] = flux[normal] + 0.5 * pressure
    flux[4] = flux[4] + pressure * half
    return flux + [0.5 * (jnp.abs(moving) + sound)]


def face_flux(low_u, low_aux, u, aux):
    wave = jnp.maximum(low_aux[FIELDS], aux[FIELDS])
    return [low_aux[f] + aux[f] - wave * (u[f] - low_u[f]) for f in range(FIELDS)]


def lane_of():
    return lax.broadcasted_iota(jnp.int32, (SUB, LANE), 1)


def sub_of():
    return lax.broadcasted_iota(jnp.int32, (SUB, LANE), 0)


def take_lanes(x, lanes):
    return jnp.take_along_axis(x, lanes, axis=1, mode="promise_in_bounds")


def top_speed(u):
    vx, vy, _, sound = primitive(u)
    return jnp.maximum(jnp.abs(vx), jnp.abs(vy)) + sound


def place_of(me, other, n):
    if power_of_two(n):
        return me ^ other
    behind = me - other
    return jnp.where(behind < 0, behind + n, behind)


def pack_kernel(tiles, rows, patches, mesh_sizes, patch_ref, box_ref, which_ref, start_ref, pay_ref, meta_ref):
    n_gx, n_gz = mesh_sizes
    me = lax.axis_index("gy")
    top = None
    for s in range(SUB):
        wave = top_speed([patch_ref[0, 0, f, :, s * LANE : (s + 1) * LANE] for f in range(FIELDS)])
        top = wave if top is None else jnp.maximum(top, wave)
    for f in range(FIELDS):
        pay_ref[f * tiles : (f + 1) * tiles, :] = box_ref[pl.ds(f * BOX_ROWS + me * tiles, tiles), :]
    pay_ref[rows - SUB : rows, :] = top

    start = start_ref[0, 0]
    row = lax.shift_right_logical(start * 2675, 17)
    offset = BOX * (row & 1) + start - row * STRIDE
    near = lax.shift_right_logical(row, 1) - me * tiles
    mine = (near >= 0) & (near < tiles)
    patch = lax.broadcasted_iota(jnp.int32, start.shape, 1)
    which = which_ref[0, 0]
    gz_bits = n_gz.bit_length() - 1
    place = place_of(lax.axis_index("gx"), lax.shift_right_logical(which, gz_bits), n_gx) + n_gx * place_of(
        lax.axis_index("gz"), which & (n_gz - 1), n_gz
    )
    meta_ref[0:4, 0:patches] = place * rows + jnp.where(mine, near, 0)
    meta_ref[4:8, 0:patches] = (HALF * (patch & (SUB - 1)) - offset) & (LANE - 1)
    meta_ref[8:12, 0:patches] = jnp.where(mine, patch & (SUB - 1), -1)


def strip_kernel(parts, rows, tiles, patches, meta_ref, pay_ref, out_ref):
    top = pay_ref[rows - SUB : rows, :]
    for k in range(1, parts):
        top = jnp.maximum(top, pay_ref[(k + 1) * rows - SUB : (k + 1) * rows, :])
    block = lane_of() // HALF
    lines = 4 * patches // SUB
    out_ref[FIELDS * lines :, :] = top

    for v in range(lines):
        side, first = v // (patches // SUB), v % (patches // SUB) * SUB
        acc = jnp.zeros((SUB, LANE), jnp.float32)
        for m in range(SUB):
            p = first + m
            at, shift, fills = meta_ref[side, p], meta_ref[4 + side, p], meta_ref[8 + side, p]
            strip = pay_ref[pl.ds(at, FIELDS, stride=tiles), :]
            strip = jnp.concatenate([strip, jnp.zeros((SUB - FIELDS, LANE), jnp.float32)], axis=0)
            acc = jnp.where(block == fills, pltpu.roll(strip, shift, 1), acc)
        out_ref[pl.ds(v, FIELDS, stride=lines), :] = acc[:FIELDS, :]


def lanes_at(lanes_ref, g, side, kind):
    at = ((g * 4 + side) * 3 + kind) * SUB
    return lanes_ref[at : at + SUB, :]


def held_at(lanes_ref, sets):
    return lanes_ref[sets * 4 * 3 * SUB : (sets * 4 * 3 + 1) * SUB, :]


def fill_ghosts(u_ref, lanes_ref, coarse_ref, sets):
    for f in range(FIELDS):
        for g in range(sets):

            def ghost(side, at, kept):
                x = None
                for o in range(sets):
                    start = (o * FIELDS + f) * PLANE + at
                    edge = pl.ds(start, DEEP, stride=SPAN) if side in (WEST, EAST) else pl.ds(start, SUB)
                    moved = take_lanes(u_ref[edge, :], lanes_at(lanes_ref, g, side, 0))
                    x = moved if x is None else jnp.where(lanes_at(lanes_ref, g, side, 1) == o, moved, x)
                if coarse_ref is None:
                    return x
                start = ((g * FIELDS + f) * 10 + kept) * SUB
                return jnp.where(lanes_at(lanes_ref, g, side, 2) != 0, coarse_ref[start : start + SUB, :], x)

            base = (g * FIELDS + f) * PLANE
            for side, column, to in ((WEST, PX - 1, -1), (EAST, 0, PX)):
                u_ref[pl.ds(base + spot(0, to), DEEP, stride=SPAN), :] = ghost(side, spot(0, column), side)
            for side, row, to in ((SOUTH, DEEP - 1, -1), (NORTH, 0, DEEP)):
                for i in range(BLOCKS):
                    kept = 2 + (side - SOUTH) * BLOCKS + i
                    u_ref[pl.ds(base + spot(to, SUB * i), SUB), :] = ghost(side, spot(row, SUB * i), kept)


def halves_of(u, axis):
    vx, vy, pressure, sound = primitive(u)
    return half_flux(u, (vx, vy)[axis], pressure, sound, axis + 1)


def fill_halves(u_ref, aux_ref, sets):
    def fill(g, rows, axes):
        u = [u_ref[rows((g * FIELDS + f) * PLANE), :] for f in range(FIELDS)]
        vx, vy, pressure, sound = primitive(u)
        for axis in axes:
            for n, x in enumerate(half_flux(u, (vx, vy)[axis], pressure, sound, axis + 1)):
                aux_ref[rows((g * AUX + axis * (FIELDS + 1) + n) * PLANE), :] = x

    for g in range(sets):

        def cells(r, carry):
            for half in range(2):
                for i in range(BLOCKS):
                    at = spot(2 * r + half, SUB * i)
                    fill(g, lambda b, at=at: pl.ds(pl.multiple_of(b + at, SUB), SUB), (0, 1))
            return carry

        lax.fori_loop(0, DEEP // 2, cells, 0)
        for r in (-1, DEEP):
            for i in range(BLOCKS):
                fill(g, lambda b, at=spot(r, SUB * i): pl.ds(b + at, SUB), (1,))
        for c in (-1, PX):
            fill(g, lambda b, at=spot(0, c): pl.ds(b + at, DEEP, stride=SPAN), (0,))


def load_cells(u_ref, aux_ref, g, axis, rows):
    u = [u_ref[rows((g * FIELDS + f) * PLANE), :] for f in range(FIELDS)]
    start = g * AUX + axis * (FIELDS + 1)
    return u, [aux_ref[rows((start + n) * PLANE), :] for n in range(FIELDS + 1)]


def at_row(at):
    return lambda b: pl.ds(b + at, SUB)


def fill_x_faces(u_ref, aux_ref, dx_ref, g, base):
    def across(r, carry):
        for half in range(2):
            row = 2 * r + half
            for i in range(BLOCKS + 1):
                at = pl.multiple_of(spot(row, SUB * i), SUB)
                low = load_cells(u_ref, aux_ref, g, 0, at_row(at - 1))
                faces = face_flux(*low, *load_cells(u_ref, aux_ref, g, 0, at_row(at)))
                for f in range(FIELDS):
                    to = pl.multiple_of(base + (f * DEEP + row) * FACES + SUB * i, SUB)
                    dx_ref[pl.ds(to, SUB), :] = faces[f]
        return carry

    lax.fori_loop(0, DEEP // 2, across, 0)


def x_change(dx_ref, base, f, row, i):
    west = pl.multiple_of(base + (f * DEEP + row) * FACES + SUB * i, SUB)
    return dx_ref[pl.ds(west, SUB), :] - dx_ref[pl.ds(west + 1, SUB), :]


def prepare_kernel(group, count, patches, slots, around_ref, owner_ref, *refs):
    raw_refs = refs[:group]
    u_ref, edge_ref, dx_ref, dy_ref, lanes_ref, aux_ref, table, slot_ref = refs[group:]
    me = lax.axis_index("gy")
    capacity = slots // group
    sets = patches // PX
    lane = lane_of()
    block, in_block = lane // PX, lane & (PX - 1)
    turn = me * count

    for f in range(FIELDS):
        for g in range(sets):
            for h in range(2):
                tiles = []
                for q in range(BLOCKS):
                    at = (q * 2 + h) * LANE
                    for k in range(PX // count):
                        tiles.append(raw_refs[g * (PX // count) + k][0, 0, f, :, at : at + LANE])
                cells = jnp.concatenate(tiles, axis=0).T
                for i in range(BLOCKS):
                    to = (g * FIELDS + f) * PLANE + spot(h * BLOCKS + i, 0)
                    u_ref[to : to + PX, :] = cells[i * PX : (i + 1) * PX, :]

    for i in range(slots):
        slot_ref[i] = -1

    def rank_source(source, carry):
        rank = jnp.int32(0)
        for i in range(count):
            p = source * count + i
            hit = owner_ref[0, 0, 0, p] == me
            slot_ref[jnp.where(hit, source * capacity + rank, slots)] = p
            rank = rank + jnp.where(hit, 1, 0)
        return carry

    lax.fori_loop(0, group, rank_source, 0)
    held = jnp.full((SUB, LANE), -1, jnp.int32)
    for j in range(slots):
        held = jnp.where(in_block == j, slot_ref[j], held)
    lanes_ref[sets * 4 * 3 * SUB :, :] = held

    table[0:4, 0:patches] = around_ref[0, 0]
    for g in range(sets):
        patch = (g * PX + in_block) ^ turn
        for side in range(4):
            near = take_lanes(jnp.broadcast_to(table[side : side + 1, :], (SUB, LANE)), patch)
            place = jnp.maximum(near, 0) ^ turn
            pick, origin = place & (PX - 1), lax.shift_right_logical(place, 5)
            lacking = jnp.where(near < 0, 1, 0)
            if side in (WEST, EAST):
                pick = pick + PX * block
            else:
                edge, step = (0, -PX) if side == SOUTH else (BLOCKS - 1, PX)
                across = pick + (LANE - PX if side == SOUTH else 0)
                pick = jnp.where(block == edge, across, lane + step)
                origin = jnp.where(block == edge, origin, g)
                lacking = jnp.where(block == edge, lacking, 0)
            for kind, x in enumerate((pick, origin, lacking)):
                at = ((g * 4 + side) * 3 + kind) * SUB
                lanes_ref[at : at + SUB, :] = x

    fill_ghosts(u_ref, lanes_ref, None, sets)
    fill_halves(u_ref, aux_ref, sets)
    for g in range(sets):
        fill_x_faces(u_ref, aux_ref, dx_ref, g, g * FIELDS * DEEP * FACES)

        def along(i, carry):
            low = load_cells(u_ref, aux_ref, g, 1, at_row(pl.multiple_of(spot(-1, SUB * i), SUB)))
            for r in range(DEEP + 1):
                cell = load_cells(u_ref, aux_ref, g, 1, at_row(pl.multiple_of(spot(r, SUB * i), SUB)))
                for f, face in enumerate(face_flux(*low, *cell)):
                    to = pl.multiple_of(((g * FIELDS + f) * (DEEP + 1) + r) * PX + SUB * i, SUB)
                    dy_ref[pl.ds(to, SUB), :] = face
                low = cell
            return carry

        lax.fori_loop(0, BLOCKS, along, 0)
        for side in range(4):
            for i, rows in enumerate(edge_rows(side)):
                for n in range(FIELDS + 1):
                    start = g * AUX + (0 if side in (WEST, EAST) else FIELDS + 1) + n
                    to = edge_place(g, side, i, n)
                    edge_ref[to : to + SUB, :] = aux_ref[rows(start * PLANE), :]


def edge_rows(side):
    if side in (WEST, EAST):
        at = spot(0, 0 if side == WEST else PX - 1)
        return [lambda b: pl.ds(b + at, DEEP, stride=SPAN)]
    return [at_row(spot(0 if side == SOUTH else DEEP - 1, SUB * i)) for i in range(BLOCKS)]


def edge_place(g, side, i, n):
    kept = side if side in (WEST, EAST) else 2 + (side - SOUTH) * BLOCKS + i
    return ((g * 10 + kept) * (FIELDS + 1) + n) * SUB


def step_kernel(group, count, patches, slots, *refs):
    u_ref, edge_ref, dx_ref, dy_ref, lanes_ref = refs[:5]
    strip_refs, out_ref = refs[5 : 5 + group], refs[5 + group]
    next_u, next_aux, next_dx, strips, doubled, coarse_ref, border_ref = refs[6 + group :]
    lines = 4 * patches // SUB
    sets = patches // PX
    lane, sub = lane_of(), sub_of()
    block, in_block = lane // PX, lane & (PX - 1)
    turn = lax.axis_index("gy") * count

    def joined(at, join):
        return functools.reduce(join, [ref[at : at + SUB, :] for ref in strip_refs])

    for at in range(0, FIELDS * lines, SUB):
        strips[at : at + SUB, :] = joined(at, jnp.add)
    time_step = courant / jnp.max(joined(FIELDS * lines, jnp.maximum))
    part = HALF * sub + (lane & (HALF - 1))
    for t in range(4 * patches // LANE):
        tiles = []
        for v in range(t * HALF, (t + 1) * HALF):
            tile = None
            for f in range(FIELDS):
                row = jnp.broadcast_to(strips[f * lines + v : f * lines + v + 1, :], (SUB, LANE))
                wide = take_lanes(row, part)
                tile = wide if tile is None else jnp.where(lane // HALF == f, wide, tile)
            tiles.append(tile)
        cells = jnp.concatenate(tiles, axis=0).T
        for n in range(FIELDS * 2):
            for twice in range(2):
                at = t * FIELDS * PX + n * HALF + twice
                doubled[pl.ds(at, SUB, stride=2), :] = cells[n * SUB : (n + 1) * SUB, :]

    for g in range(sets):
        patch = (g * PX + in_block) ^ turn
        for side in range(4):
            t, shift = side * patches // LANE, side * patches % LANE
            for f in range(FIELDS):
                pieces = []
                for i in range(BLOCKS):
                    at = t * FIELDS * PX + f * PX + SUB * i
                    pieces.append(take_lanes(doubled[at : at + SUB, :], patch + shift))
                base = (g * FIELDS + f) * 10
                if side in (WEST, EAST):
                    x = pieces[0]
                    for q in range(1, BLOCKS):
                        x = jnp.where(block == q, pieces[q], x)
                    coarse_ref[(base + side) * SUB : (base + side + 1) * SUB, :] = x
                else:
                    for i in range(BLOCKS):
                        at = (base + 2 + (side - SOUTH) * BLOCKS + i) * SUB
                        coarse_ref[at : at + SUB, :] = pieces[i]

    size = FIELDS * DEEP * FACES
    for g in range(sets):
        for at in range(0, size, SUB):
            next_dx[g * size + at : g * size + at + SUB, :] = dx_ref[g * size + at : g * size + at + SUB, :]

        def coarse_cells(kept, axis):
            at = [((g * FIELDS + f) * 10 + kept) * SUB for f in range(FIELDS)]
            u = [coarse_ref[a : a + SUB, :] for a in at]
            return u, halves_of(u, axis)

        def own_cells(side, i):
            rows = edge_rows(side)[i]
            places = [edge_place(g, side, i, n) for n in range(FIELDS + 1)]
            u = [u_ref[rows((g * FIELDS + f) * PLANE), :] for f in range(FIELDS)]
            return u, [edge_ref[at : at + SUB, :] for at in places]

        for side, face in ((WEST, 0), (EAST, PX)):
            beyond, own = coarse_cells(side, 0), own_cells(side, 0)
            faces = face_flux(*beyond, *own) if side == WEST else face_flux(*own, *beyond)
            lacking = lanes_at(lanes_ref, g, side, 2) != 0
            for f in range(FIELDS):
                rows = pl.ds(g * size + f * DEEP * FACES + face, DEEP, stride=FACES)
                next_dx[rows, :] = jnp.where(lacking, faces[f], dx_ref[rows, :])
        for side, face in ((SOUTH, 0), (NORTH, DEEP)):
            lacking = lanes_at(lanes_ref, g, side, 2) != 0
            for i in range(BLOCKS):
                kept = (side - SOUTH) * BLOCKS + i
                beyond, own = coarse_cells(2 + kept, 1), own_cells(side, i)
                faces = face_flux(*beyond, *own) if side == SOUTH else face_flux(*own, *beyond)
                for f in range(FIELDS):
                    fine = ((g * FIELDS + f) * (DEEP + 1) + face) * PX + SUB * i
                    to = ((g * FIELDS + f) * 8 + kept) * SUB
                    border_ref[to : to + SUB, :] = jnp.where(lacking, faces[f], dy_ref[fine : fine + SUB, :])

        def update(f, carry):
            for i in range(BLOCKS):
                for r in range(DEEP):
                    faces = []
                    for n in (r, r + 1):
                        if n in (0, DEEP):
                            at = ((g * FIELDS + f) * 8 + (BLOCKS if n else 0) + i) * SUB
                            faces.append(border_ref[pl.ds(pl.multiple_of(at, SUB), SUB), :])
                        else:
                            at = ((g * FIELDS + f) * (DEEP + 1) + n) * PX + SUB * i
                            faces.append(dy_ref[pl.ds(pl.multiple_of(at, SUB), SUB), :])
                    change = x_change(next_dx, g * size, f, r, i) + (faces[0] - faces[1])
                    at = pl.ds(pl.multiple_of((g * FIELDS + f) * PLANE + spot(r, SUB * i), SUB), SUB)
                    next_u[at, :] = u_ref[at, :] + time_step * change
            return carry

        lax.fori_loop(0, FIELDS, update, 0)

    fill_ghosts(next_u, lanes_ref, coarse_ref, sets)
    fill_halves(next_u, next_aux, sets)
    for g in range(sets):
        fill_x_faces(next_u, next_aux, next_dx, g, g * size)

        def along(half, carry):
            for i in (2 * half, 2 * half + 1):
                low = load_cells(next_u, next_aux, g, 1, at_row(pl.multiple_of(spot(-1, SUB * i), SUB)))
                low_faces = None
                for r in range(DEEP + 1):
                    cell = load_cells(next_u, next_aux, g, 1, at_row(pl.multiple_of(spot(r, SUB * i), SUB)))
                    faces = face_flux(*low, *cell)
                    for f in range(FIELDS):
                        if r == 0:
                            continue
                        change = x_change(next_dx, g * size, f, r - 1, i) + (low_faces[f] - faces[f])
                        new = low[0][f] + time_step * change
                        at = pl.ds(pl.multiple_of((g * FIELDS + f) * PLANE + spot(r - 1, SUB * i), SUB), SUB)
                        next_u[at, :] = 0.5 * u_ref[at, :] + 0.5 * new
                    low, low_faces = cell, faces
            return carry

        lax.fori_loop(0, BLOCKS // 2, along, 0)

    held = held_at(lanes_ref, sets)
    place = jnp.maximum(held, 0) ^ turn
    pick, origin = PX * block + (place & (PX - 1)), lax.shift_right_logical(place, 5)
    for f in range(FIELDS):
        for h in range(2):
            tiles = []
            for i in range(LANE // SUB):
                at = spot(h * BLOCKS + i // BLOCKS, SUB * (i % BLOCKS))
                x = None
                for g in range(sets):
                    start = (g * FIELDS + f) * PLANE + at
                    moved = take_lanes(next_u[start : start + SUB, :], pick)
                    x = moved if x is None else jnp.where(origin == g, moved, x)
                tiles.append(jnp.where(held >= 0, x, 0.0))
            cells = jnp.concatenate(tiles, axis=0).T
            for q in range(BLOCKS):
                at = (q * 2 + h) * LANE
                out_ref[0, 0, f, :, at : at + LANE] = cells[q * PX : q * PX + slots, :]


def limit(*row_counts):
    return pltpu.CompilerParams(vmem_limit_bytes=(sum(row_counts) * LANE * 4 * 5 // 4) + (1 << 20))


def per_device(patch_state, coarse_boxes, new_owner, neighbors, coarse_box, coarse_start):
    count = patch_state.shape[2]
    n_gx, n_gz, group = lax.axis_size("gx"), lax.axis_size("gz"), lax.axis_size("gy")
    parts = n_gx * n_gz
    patches = count * group
    lines = 4 * patches // SUB
    slots = group * max(2, 2 * count // group)
    tiles = BOX_ROWS // group
    rows = -(-tiles * FIELDS // SUB) * SUB + SUB
    strip_rows = FIELDS * lines + SUB
    vmem = pl.BlockSpec(memory_space=pltpu.VMEM)
    smem = pl.BlockSpec(memory_space=pltpu.SMEM)
    f32 = jnp.float32

    def sides_first(x):
        return jnp.swapaxes(x, 2, 3)

    raw = sides_first(patch_state)
    payload, meta = pl.pallas_call(
        functools.partial(pack_kernel, tiles, rows, patches, (n_gx, n_gz)),
        out_shape=(pltpu.VMEM((rows, LANE), f32), jax.ShapeDtypeStruct((16, max(LANE, patches)), jnp.int32)),
        in_specs=[vmem] * 4,
        out_specs=(vmem,) * 2,
        name="pack",
    )(raw, coarse_boxes.reshape(FIELDS * BOX_ROWS, LANE), sides_first(coarse_box), sides_first(coarse_start))

    def gathered(x, axis, n):
        if power_of_two(n):
            perms = [[(i, i ^ k) for i in range(n)] for k in range(1, n)]
        else:
            perms = [[(i, (i + k) % n) for i in range(n)] for k in range(1, n)]
        return jnp.concatenate([x] + [lax.ppermute(x, axis, perm) for perm in perms], axis=0)

    payload = gathered(gathered(payload, "gx", n_gx), "gz", n_gz)

    strip = pl.pallas_call(
        functools.partial(strip_kernel, parts, rows, tiles, patches),
        out_shape=pltpu.VMEM((strip_rows, LANE), f32),
        in_specs=[smem, vmem],
        out_specs=vmem,
        compiler_params=limit(parts * rows, strip_rows),
        name="strips",
    )(meta, payload)

    def to_group(x, after=None):
        blocks, have = [x] + [None] * (group - 1), [0]
        masks = masks_of(group)
        for mask in masks:
            perm = [(i, i ^ mask) for i in range(group)]
            for k in have:
                block = blocks[k]
                if after is not None and mask == masks[-1] and k:
                    block, _ = lax.optimization_barrier((block, after))
                blocks[k ^ mask] = lax.ppermute(block, "gy", perm)
            have = have + [k ^ mask for k in have]
        return blocks

    raws = to_group(raw, strip)

    sets = patches // PX
    made_rows = [
        sets * FIELDS * PLANE,
        sets * 10 * (FIELDS + 1) * SUB,
        sets * FIELDS * DEEP * FACES,
        sets * FIELDS * (DEEP + 1) * PX,
    ]
    lane_rows = (sets * 4 * 3 + 1) * SUB
    made = pl.pallas_call(
        functools.partial(prepare_kernel, group, count, patches, slots),
        out_shape=[pltpu.VMEM((n, LANE), f32) for n in made_rows] + [pltpu.VMEM((lane_rows, LANE), jnp.int32)],
        in_specs=[vmem, smem] + [vmem] * group,
        out_specs=[vmem] * 5,
        scratch_shapes=[
            pltpu.VMEM((sets * AUX * PLANE, LANE), f32),
            pltpu.VMEM((SUB, LANE), jnp.int32),
            pltpu.SMEM((slots + 1,), jnp.int32),
        ],
        compiler_params=limit(*made_rows, sets * AUX * PLANE, lane_rows, patches * FIELDS * SUB),
        cost_estimate=pl.CostEstimate(flops=patches * 1024 * 300, bytes_accessed=patches * 40000, transcendentals=0),
        name="prepare",
    )(sides_first(neighbors), sides_first(new_owner), *raws)

    strips = to_group(strip, made[4])
    scratch_rows = [sets * FIELDS * PLANE, sets * AUX * PLANE, sets * FIELDS * DEEP * FACES] + [
        FIELDS * lines,
        4 * patches // LANE * FIELDS * PX,
        sets * FIELDS * 10 * SUB,
        sets * FIELDS * 8 * SUB,
    ]
    out = pl.pallas_call(
        functools.partial(step_kernel, group, count, patches, slots),
        out_shape=jax.ShapeDtypeStruct((1, 1, FIELDS, slots, SUB * LANE), f32),
        in_specs=[vmem] * (5 + group),
        out_specs=vmem,
        scratch_shapes=[pltpu.VMEM((n, LANE), f32) for n in scratch_rows],
        compiler_params=limit(*scratch_rows, *made_rows, lane_rows, group * strip_rows, FIELDS * slots * SUB),
        name="step",
    )(*made, *strips)
    return sides_first(out)


def solution(mesh):
    in_specs = (
        P("gx", "gz", "gy", None, None),
        P(("gx", "gz"), None, None),
        P("gx", "gz", None, None),
        P("gx", "gz", None, None),
        P("gx", "gz", None, None),
        P("gx", "gz", None, None),
    )
    out_specs = P("gx", "gz", "gy", None, None)
    return jax.shard_map(
        per_device, mesh=mesh, in_specs=in_specs, out_specs=out_specs, check_vma=False
    )
```

```python
import functools

import jax
import jax.numpy as jnp
from jax import lax
from jax.experimental import pallas as pl
from jax.experimental.pallas import tpu as pltpu
from jax.sharding import PartitionSpec as P

FIELDS = 5
PX = 32
BOX = 64
SUB = 8
LANE = 128
HALF = PX // 2
STRIDE = BOX - HALF + 1
BOX_ROWS = BOX * BOX // LANE
heat_ratio = 1.4
courant = 0.3
WEST, EAST, SOUTH, NORTH = range(4)
BLOCKS = LANE // PX
DEEP = PX // BLOCKS
SPAN = PX + 2 * SUB
PLANE = (DEEP + 2) * SPAN
FACES = PX + SUB
AUX = 2 * (FIELDS + 1)


def spot(row, column):
    return (row + 1) * SPAN + SUB + column


def power_of_two(n):
    return n & (n - 1) == 0


def masks_of(n):
    return [n >> (i + 1) for i in range(n.bit_length() - 1)]


def primitive(u):
    inverse = 1.0 / u[0]
    vx, vy, vz = u[1] * inverse, u[2] * inverse, u[3] * inverse
    kinetic = u[1] * (0.5 * vx) + u[2] * (0.5 * vy) + u[3] * (0.5 * vz)
    pressure = (heat_ratio - 1.0) * (u[4] - kinetic)
    sound = jnp.sqrt(heat_ratio * pressure * inverse)
    return vx, vy, pressure, sound


def half_flux(u, moving, pressure, sound, normal):
    half = 0.5 * moving
    flux = [u[f] * half for f in range(FIELDS)]
    flux[normal] = flux[normal] + 0.5 * pressure
    flux[4] = flux[4] + pressure * half
    return flux + [0.5 * (jnp.abs(moving) + sound)]


def face_flux(low_u, low_aux, u, aux):
    wave = jnp.maximum(low_aux[FIELDS], aux[FIELDS])
    return [low_aux[f] + aux[f] - wave * (u[f] - low_u[f]) for f in range(FIELDS)]


def lane_of():
    return lax.broadcasted_iota(jnp.int32, (SUB, LANE), 1)


def sub_of():
    return lax.broadcasted_iota(jnp.int32, (SUB, LANE), 0)


def take_lanes(x, lanes):
    return jnp.take_along_axis(x, lanes, axis=1, mode="promise_in_bounds")


def top_speed(u):
    vx, vy, _, sound = primitive(u)
    return jnp.maximum(jnp.abs(vx), jnp.abs(vy)) + sound


def make_lanes(group, count, patches, slots, around_ref, owner_ref, lanes_ref, table, slot_ref):
    me = lax.axis_index("gy")
    capacity = slots // group
    sets = patches // PX
    lane = lane_of()
    block, in_block = lane // PX, lane & (PX - 1)
    turn = me * count

    for i in range(slots):
        slot_ref[i] = -1

    def rank_source(source, carry):
        rank = jnp.int32(0)
        for i in range(count):
            p = source * count + i
            hit = owner_ref[0, 0, 0, p] == me
            slot_ref[jnp.where(hit, source * capacity + rank, slots)] = p
            rank = rank + jnp.where(hit, 1, 0)
        return carry

    lax.fori_loop(0, group, rank_source, 0)
    held = jnp.full((SUB, LANE), -1, jnp.int32)
    for j in range(slots):
        held = jnp.where(in_block == j, slot_ref[j], held)
    lanes_ref[sets * 4 * 3 * SUB :, :] = held

    table[0:4, 0:patches] = around_ref[0, 0]
    for g in range(sets):
        patch = (g * PX + in_block) ^ turn
        for side in range(4):
            near = take_lanes(jnp.broadcast_to(table[side : side + 1, :], (SUB, LANE)), patch)
            place = jnp.maximum(near, 0) ^ turn
            pick, origin = place & (PX - 1), lax.shift_right_logical(place, 5)
            lacking = jnp.where(near < 0, 1, 0)
            if side in (WEST, EAST):
                pick = pick + PX * block
            else:
                edge, step = (0, -PX) if side == SOUTH else (BLOCKS - 1, PX)
                across = pick + (LANE - PX if side == SOUTH else 0)
                pick = jnp.where(block == edge, across, lane + step)
                origin = jnp.where(block == edge, origin, g)
                lacking = jnp.where(block == edge, lacking, 0)
            for kind, x in enumerate((pick, origin, lacking)):
                at = ((g * 4 + side) * 3 + kind) * SUB
                lanes_ref[at : at + SUB, :] = x


def place_of(me, other, n):
    if power_of_two(n):
        return me ^ other
    behind = me - other
    return jnp.where(behind < 0, behind + n, behind)


def pack_kernel(tiles, rows, group, count, patches, slots, mesh_sizes, *refs):
    owner_ref, around_ref, which_ref, start_ref, patch_ref, box_ref = refs[:6]
    pay_ref, raw_ref, meta_ref, lanes_ref, table, slot_ref = refs[6:]
    n_gx, n_gz = mesh_sizes
    raw_ref[...] = patch_ref[...]
    me = lax.axis_index("gy")
    top = None
    for s in range(SUB):
        wave = top_speed([patch_ref[0, 0, f, :, s * LANE : (s + 1) * LANE] for f in range(FIELDS)])
        top = wave if top is None else jnp.maximum(top, wave)
    for f in range(FIELDS):
        pay_ref[f * tiles : (f + 1) * tiles, :] = box_ref[pl.ds(f * BOX_ROWS + me * tiles, tiles), :]
    pay_ref[rows - SUB : rows, :] = top

    start = start_ref[0, 0]
    row = lax.shift_right_logical(start * 2675, 17)
    offset = BOX * (row & 1) + start - row * STRIDE
    near = lax.shift_right_logical(row, 1) - me * tiles
    mine = (near >= 0) & (near < tiles)
    patch = lax.broadcasted_iota(jnp.int32, start.shape, 1)
    which = which_ref[0, 0]
    gz_bits = n_gz.bit_length() - 1
    place = place_of(lax.axis_index("gx"), lax.shift_right_logical(which, gz_bits), n_gx) + n_gx * place_of(
        lax.axis_index("gz"), which & (n_gz - 1), n_gz
    )
    meta_ref[0:4, 0:patches] = place * rows + jnp.where(mine, near, 0)
    meta_ref[4:8, 0:patches] = (HALF * (patch & (SUB - 1)) - offset) & (LANE - 1)
    meta_ref[8:12, 0:patches] = jnp.where(mine, patch & (SUB - 1), -1)
    make_lanes(group, count, patches, slots, around_ref, owner_ref, lanes_ref, table, slot_ref)


def strip_kernel(parts, rows, tiles, patches, meta_ref, pay_ref, out_ref):
    top = pay_ref[rows - SUB : rows, :]
    for k in range(1, parts):
        top = jnp.maximum(top, pay_ref[(k + 1) * rows - SUB : (k + 1) * rows, :])
    block = lane_of() // HALF
    lines = 4 * patches // SUB
    out_ref[FIELDS * lines :, :] = top

    for v in range(lines):
        side, first = v // (patches // SUB), v % (patches // SUB) * SUB
        acc = jnp.zeros((SUB, LANE), jnp.float32)
        for m in range(SUB):
            p = first + m
            at, shift, fills = meta_ref[side, p], meta_ref[4 + side, p], meta_ref[8 + side, p]
            strip = pay_ref[pl.ds(at, FIELDS, stride=tiles), :]
            strip = jnp.concatenate([strip, jnp.zeros((SUB - FIELDS, LANE), jnp.float32)], axis=0)
            acc = jnp.where(block == fills, pltpu.roll(strip, shift, 1), acc)
        out_ref[pl.ds(v, FIELDS, stride=lines), :] = acc[:FIELDS, :]


def lanes_at(lanes_ref, g, side, kind):
    at = ((g * 4 + side) * 3 + kind) * SUB
    return lanes_ref[at : at + SUB, :]


def held_at(lanes_ref, sets):
    return lanes_ref[sets * 4 * 3 * SUB : (sets * 4 * 3 + 1) * SUB, :]


def fill_ghosts(u_ref, lanes_ref, coarse_ref, sets):
    for f in range(FIELDS):
        for g in range(sets):

            def ghost(side, at, kept):
                x = None
                for o in range(sets):
                    start = (o * FIELDS + f) * PLANE + at
                    edge = pl.ds(start, DEEP, stride=SPAN) if side in (WEST, EAST) else pl.ds(start, SUB)
                    moved = take_lanes(u_ref[edge, :], lanes_at(lanes_ref, g, side, 0))
                    x = moved if x is None else jnp.where(lanes_at(lanes_ref, g, side, 1) == o, moved, x)
                if coarse_ref is None:
                    return x
                start = ((g * FIELDS + f) * 10 + kept) * SUB
                return jnp.where(lanes_at(lanes_ref, g, side, 2) != 0, coarse_ref[start : start + SUB, :], x)

            base = (g * FIELDS + f) * PLANE
            for side, column, to in ((WEST, PX - 1, -1), (EAST, 0, PX)):
                u_ref[pl.ds(base + spot(0, to), DEEP, stride=SPAN), :] = ghost(side, spot(0, column), side)
            for side, row, to in ((SOUTH, DEEP - 1, -1), (NORTH, 0, DEEP)):
                for i in range(BLOCKS):
                    kept = 2 + (side - SOUTH) * BLOCKS + i
                    u_ref[pl.ds(base + spot(to, SUB * i), SUB), :] = ghost(side, spot(row, SUB * i), kept)


def halves_of(u, axis):
    vx, vy, pressure, sound = primitive(u)
    return half_flux(u, (vx, vy)[axis], pressure, sound, axis + 1)


def fill_halves(u_ref, aux_ref, sets):
    def fill(g, rows, axes):
        u = [u_ref[rows((g * FIELDS + f) * PLANE), :] for f in range(FIELDS)]
        vx, vy, pressure, sound = primitive(u)
        for axis in axes:
            for n, x in enumerate(half_flux(u, (vx, vy)[axis], pressure, sound, axis + 1)):
                aux_ref[rows((g * AUX + axis * (FIELDS + 1) + n) * PLANE), :] = x

    for g in range(sets):

        def cells(r, carry):
            for half in range(2):
                for i in range(BLOCKS):
                    at = spot(2 * r + half, SUB * i)
                    fill(g, lambda b, at=at: pl.ds(pl.multiple_of(b + at, SUB), SUB), (0, 1))
            return carry

        lax.fori_loop(0, DEEP // 2, cells, 0)
        for r in (-1, DEEP):
            for i in range(BLOCKS):
                fill(g, lambda b, at=spot(r, SUB * i): pl.ds(b + at, SUB), (1,))
        for c in (-1, PX):
            fill(g, lambda b, at=spot(0, c): pl.ds(b + at, DEEP, stride=SPAN), (0,))


def load_cells(u_ref, aux_ref, g, axis, rows):
    u = [u_ref[rows((g * FIELDS + f) * PLANE), :] for f in range(FIELDS)]
    start = g * AUX + axis * (FIELDS + 1)
    return u, [aux_ref[rows((start + n) * PLANE), :] for n in range(FIELDS + 1)]


def at_row(at):
    return lambda b: pl.ds(b + at, SUB)


def fill_x_faces(u_ref, aux_ref, dx_ref, g, base):
    def across(r, carry):
        for half in range(2):
            row = 2 * r + half
            for i in range(BLOCKS + 1):
                at = pl.multiple_of(spot(row, SUB * i), SUB)
                low = load_cells(u_ref, aux_ref, g, 0, at_row(at - 1))
                faces = face_flux(*low, *load_cells(u_ref, aux_ref, g, 0, at_row(at)))
                for f in range(FIELDS):
                    to = pl.multiple_of(base + (f * DEEP + row) * FACES + SUB * i, SUB)
                    dx_ref[pl.ds(to, SUB), :] = faces[f]
        return carry

    lax.fori_loop(0, DEEP // 2, across, 0)


def x_change(dx_ref, base, f, row, i):
    west = pl.multiple_of(base + (f * DEEP + row) * FACES + SUB * i, SUB)
    return dx_ref[pl.ds(west, SUB), :] - dx_ref[pl.ds(west + 1, SUB), :]


def prepare_kernel(group, count, patches, lanes_ref, *refs):
    raw_refs = refs[:group]
    u_ref, edge_ref, dx_ref, dy_ref, aux_ref = refs[group:]
    sets = patches // PX

    for f in range(FIELDS):
        for g in range(sets):
            for h in range(2):
                tiles = []
                for q in range(BLOCKS):
                    at = (q * 2 + h) * LANE
                    for k in range(PX // count):
                        tiles.append(raw_refs[g * (PX // count) + k][0, 0, f, :, at : at + LANE])
                cells = jnp.concatenate(tiles, axis=0).T
                for i in range(BLOCKS):
                    to = (g * FIELDS + f) * PLANE + spot(h * BLOCKS + i, 0)
                    u_ref[to : to + PX, :] = cells[i * PX : (i + 1) * PX, :]

    fill_ghosts(u_ref, lanes_ref, None, sets)
    fill_halves(u_ref, aux_ref, sets)
    for g in range(sets):
        fill_x_faces(u_ref, aux_ref, dx_ref, g, g * FIELDS * DEEP * FACES)

        def along(i, carry):
            low = load_cells(u_ref, aux_ref, g, 1, at_row(pl.multiple_of(spot(-1, SUB * i), SUB)))
            for r in range(DEEP + 1):
                cell = load_cells(u_ref, aux_ref, g, 1, at_row(pl.multiple_of(spot(r, SUB * i), SUB)))
                for f, face in enumerate(face_flux(*low, *cell)):
                    to = pl.multiple_of(((g * FIELDS + f) * (DEEP + 1) + r) * PX + SUB * i, SUB)
                    dy_ref[pl.ds(to, SUB), :] = face
                low = cell
            return carry

        lax.fori_loop(0, BLOCKS, along, 0)
        for side in range(4):
            for i, rows in enumerate(edge_rows(side)):
                for n in range(FIELDS + 1):
                    start = g * AUX + (0 if side in (WEST, EAST) else FIELDS + 1) + n
                    to = edge_place(g, side, i, n)
                    edge_ref[to : to + SUB, :] = aux_ref[rows(start * PLANE), :]


def edge_rows(side):
    if side in (WEST, EAST):
        at = spot(0, 0 if side == WEST else PX - 1)
        return [lambda b: pl.ds(b + at, DEEP, stride=SPAN)]
    return [at_row(spot(0 if side == SOUTH else DEEP - 1, SUB * i)) for i in range(BLOCKS)]


def edge_place(g, side, i, n):
    kept = side if side in (WEST, EAST) else 2 + (side - SOUTH) * BLOCKS + i
    return ((g * 10 + kept) * (FIELDS + 1) + n) * SUB


def step_kernel(group, count, patches, slots, *refs):
    u_ref, edge_ref, dx_ref, dy_ref, lanes_ref = refs[:5]
    strip_refs, out_ref = refs[5 : 5 + group], refs[5 + group]
    next_u, next_aux, next_dx, strips, doubled, coarse_ref, border_ref = refs[6 + group :]
    lines = 4 * patches // SUB
    sets = patches // PX
    lane, sub = lane_of(), sub_of()
    block, in_block = lane // PX, lane & (PX - 1)
    turn = lax.axis_index("gy") * count

    def joined(at, join):
        return functools.reduce(join, [ref[at : at + SUB, :] for ref in strip_refs])

    for at in range(0, FIELDS * lines, SUB):
        strips[at : at + SUB, :] = joined(at, jnp.add)
    time_step = courant / jnp.max(joined(FIELDS * lines, jnp.maximum))
    part = HALF * sub + (lane & (HALF - 1))
    for t in range(4 * patches // LANE):
        tiles = []
        for v in range(t * HALF, (t + 1) * HALF):
            tile = None
            for f in range(FIELDS):
                row = jnp.broadcast_to(strips[f * lines + v : f * lines + v + 1, :], (SUB, LANE))
                wide = take_lanes(row, part)
                tile = wide if tile is None else jnp.where(lane // HALF == f, wide, tile)
            tiles.append(tile)
        cells = jnp.concatenate(tiles, axis=0).T
        for n in range(FIELDS * 2):
            for twice in range(2):
                at = t * FIELDS * PX + n * HALF + twice
                doubled[pl.ds(at, SUB, stride=2), :] = cells[n * SUB : (n + 1) * SUB, :]

    for g in range(sets):
        patch = (g * PX + in_block) ^ turn
        for side in range(4):
            t, shift = side * patches // LANE, side * patches % LANE
            for f in range(FIELDS):
                pieces = []
                for i in range(BLOCKS):
                    at = t * FIELDS * PX + f * PX + SUB * i
                    pieces.append(take_lanes(doubled[at : at + SUB, :], patch + shift))
                base = (g * FIELDS + f) * 10
                if side in (WEST, EAST):
                    x = pieces[0]
                    for q in range(1, BLOCKS):
                        x = jnp.where(block == q, pieces[q], x)
                    coarse_ref[(base + side) * SUB : (base + side + 1) * SUB, :] = x
                else:
                    for i in range(BLOCKS):
                        at = (base + 2 + (side - SOUTH) * BLOCKS + i) * SUB
                        coarse_ref[at : at + SUB, :] = pieces[i]

    size = FIELDS * DEEP * FACES
    for g in range(sets):
        for at in range(0, size, SUB):
            next_dx[g * size + at : g * size + at + SUB, :] = dx_ref[g * size + at : g * size + at + SUB, :]

        def coarse_cells(kept, axis):
            at = [((g * FIELDS + f) * 10 + kept) * SUB for f in range(FIELDS)]
            u = [coarse_ref[a : a + SUB, :] for a in at]
            return u, halves_of(u, axis)

        def own_cells(side, i):
            rows = edge_rows(side)[i]
            places = [edge_place(g, side, i, n) for n in range(FIELDS + 1)]
            u = [u_ref[rows((g * FIELDS + f) * PLANE), :] for f in range(FIELDS)]
            return u, [edge_ref[at : at + SUB, :] for at in places]

        for side, face in ((WEST, 0), (EAST, PX)):
            beyond, own = coarse_cells(side, 0), own_cells(side, 0)
            faces = face_flux(*beyond, *own) if side == WEST else face_flux(*own, *beyond)
            lacking = lanes_at(lanes_ref, g, side, 2) != 0
            for f in range(FIELDS):
                rows = pl.ds(g * size + f * DEEP * FACES + face, DEEP, stride=FACES)
                next_dx[rows, :] = jnp.where(lacking, faces[f], dx_ref[rows, :])
        for side, face in ((SOUTH, 0), (NORTH, DEEP)):
            lacking = lanes_at(lanes_ref, g, side, 2) != 0
            for i in range(BLOCKS):
                kept = (side - SOUTH) * BLOCKS + i
                beyond, own = coarse_cells(2 + kept, 1), own_cells(side, i)
                faces = face_flux(*beyond, *own) if side == SOUTH else face_flux(*own, *beyond)
                for f in range(FIELDS):
                    fine = ((g * FIELDS + f) * (DEEP + 1) + face) * PX + SUB * i
                    to = ((g * FIELDS + f) * 8 + kept) * SUB
                    border_ref[to : to + SUB, :] = jnp.where(lacking, faces[f], dy_ref[fine : fine + SUB, :])

        def update(f, carry):
            for i in range(BLOCKS):
                for r in range(DEEP):
                    faces = []
                    for n in (r, r + 1):
                        if n in (0, DEEP):
                            at = ((g * FIELDS + f) * 8 + (BLOCKS if n else 0) + i) * SUB
                            faces.append(border_ref[pl.ds(pl.multiple_of(at, SUB), SUB), :])
                        else:
                            at = ((g * FIELDS + f) * (DEEP + 1) + n) * PX + SUB * i
                            faces.append(dy_ref[pl.ds(pl.multiple_of(at, SUB), SUB), :])
                    change = x_change(next_dx, g * size, f, r, i) + (faces[0] - faces[1])
                    at = pl.ds(pl.multiple_of((g * FIELDS + f) * PLANE + spot(r, SUB * i), SUB), SUB)
                    next_u[at, :] = u_ref[at, :] + time_step * change
            return carry

        lax.fori_loop(0, FIELDS, update, 0)

    fill_ghosts(next_u, lanes_ref, coarse_ref, sets)
    fill_halves(next_u, next_aux, sets)
    for g in range(sets):
        fill_x_faces(next_u, next_aux, next_dx, g, g * size)

        def along(half, carry):
            for i in (2 * half, 2 * half + 1):
                low = load_cells(next_u, next_aux, g, 1, at_row(pl.multiple_of(spot(-1, SUB * i), SUB)))
                low_faces = None
                for r in range(DEEP + 1):
                    cell = load_cells(next_u, next_aux, g, 1, at_row(pl.multiple_of(spot(r, SUB * i), SUB)))
                    faces = face_flux(*low, *cell)
                    for f in range(FIELDS):
                        if r == 0:
                            continue
                        change = x_change(next_dx, g * size, f, r - 1, i) + (low_faces[f] - faces[f])
                        new = low[0][f] + time_step * change
                        at = pl.ds(pl.multiple_of((g * FIELDS + f) * PLANE + spot(r - 1, SUB * i), SUB), SUB)
                        next_u[at, :] = 0.5 * u_ref[at, :] + 0.5 * new
                    low, low_faces = cell, faces
            return carry

        lax.fori_loop(0, BLOCKS // 2, along, 0)

    held = held_at(lanes_ref, sets)
    place = jnp.maximum(held, 0) ^ turn
    pick, origin = PX * block + (place & (PX - 1)), lax.shift_right_logical(place, 5)
    for f in range(FIELDS):
        for h in range(2):
            tiles = []
            for i in range(LANE // SUB):
                at = spot(h * BLOCKS + i // BLOCKS, SUB * (i % BLOCKS))
                x = None
                for g in range(sets):
                    start = (g * FIELDS + f) * PLANE + at
                    moved = take_lanes(next_u[start : start + SUB, :], pick)
                    x = moved if x is None else jnp.where(origin == g, moved, x)
                tiles.append(jnp.where(held >= 0, x, 0.0))
            cells = jnp.concatenate(tiles, axis=0).T
            for q in range(BLOCKS):
                at = (q * 2 + h) * LANE
                out_ref[0, 0, f, :, at : at + LANE] = cells[q * PX : q * PX + slots, :]


def limit(*row_counts):
    return pltpu.CompilerParams(vmem_limit_bytes=(sum(row_counts) * LANE * 4 * 5 // 4) + (1 << 20))


def per_device(patch_state, coarse_boxes, new_owner, neighbors, coarse_box, coarse_start):
    count = patch_state.shape[2]
    n_gx, n_gz, group = lax.axis_size("gx"), lax.axis_size("gz"), lax.axis_size("gy")
    parts = n_gx * n_gz
    patches = count * group
    lines = 4 * patches // SUB
    slots = group * max(2, 2 * count // group)
    tiles = BOX_ROWS // group
    rows = -(-tiles * FIELDS // SUB) * SUB + SUB
    strip_rows = FIELDS * lines + SUB
    vmem = pl.BlockSpec(memory_space=pltpu.VMEM)
    smem = pl.BlockSpec(memory_space=pltpu.SMEM)
    f32 = jnp.float32

    def sides_first(x):
        return jnp.swapaxes(x, 2, 3)

    sets = patches // PX
    payload, raw, meta, lanes = pl.pallas_call(
        functools.partial(pack_kernel, tiles, rows, group, count, patches, slots, (n_gx, n_gz)),
        out_shape=(
            pltpu.VMEM((rows, LANE), f32),
            pltpu.VMEM((1, 1, FIELDS, count, SUB * LANE), f32),
            pltpu.VMEM((16, max(LANE, patches)), jnp.int32),
            pltpu.VMEM(((sets * 4 * 3 + 1) * SUB, LANE), jnp.int32),
        ),
        in_specs=[smem] + [vmem] * 5,
        out_specs=(vmem,) * 4,
        scratch_shapes=[pltpu.VMEM((SUB, LANE), jnp.int32), pltpu.SMEM((slots + 1,), jnp.int32)],
        name="pack",
    )(
        sides_first(new_owner),
        sides_first(neighbors),
        sides_first(coarse_box),
        sides_first(coarse_start),
        sides_first(patch_state),
        coarse_boxes.reshape(FIELDS * BOX_ROWS, LANE),
    )

    def gathered(x, axis, n):
        if power_of_two(n):
            perms = [[(i, i ^ k) for i in range(n)] for k in range(1, n)]
        else:
            perms = [[(i, (i + k) % n) for i in range(n)] for k in range(1, n)]
        return jnp.concatenate([x] + [lax.ppermute(x, axis, perm) for perm in perms], axis=0)

    payload = gathered(gathered(payload, "gx", n_gx), "gz", n_gz)

    strip = pl.pallas_call(
        functools.partial(strip_kernel, parts, rows, tiles, patches),
        out_shape=pltpu.VMEM((strip_rows, LANE), f32),
        in_specs=[smem, vmem],
        out_specs=vmem,
        compiler_params=limit(parts * rows, strip_rows),
        name="strips",
    )(meta, payload)

    def to_group(x, after=None):
        blocks, have = [x] + [None] * (group - 1), [0]
        masks = masks_of(group)
        for mask in masks:
            perm = [(i, i ^ mask) for i in range(group)]
            for k in have:
                block = blocks[k]
                if after is not None and mask == masks[-1] and k:
                    block, _ = lax.optimization_barrier((block, after))
                blocks[k ^ mask] = lax.ppermute(block, "gy", perm)
            have = have + [k ^ mask for k in have]
        return blocks

    raws = to_group(raw, strip)

    made_rows = [
        sets * FIELDS * PLANE,
        sets * 10 * (FIELDS + 1) * SUB,
        sets * FIELDS * DEEP * FACES,
        sets * FIELDS * (DEEP + 1) * PX,
    ]
    made = pl.pallas_call(
        functools.partial(prepare_kernel, group, count, patches),
        out_shape=[pltpu.VMEM((n, LANE), f32) for n in made_rows],
        in_specs=[vmem] * (1 + group),
        out_specs=[vmem] * 4,
        scratch_shapes=[pltpu.VMEM((sets * AUX * PLANE, LANE), f32)],
        compiler_params=limit(*made_rows, sets * AUX * PLANE, lanes.shape[0], patches * FIELDS * SUB),
        cost_estimate=pl.CostEstimate(flops=patches * 1024 * 300, bytes_accessed=patches * 40000, transcendentals=0),
        name="prepare",
    )(lanes, *raws)

    strips = to_group(strip, made[0])
    scratch_rows = [sets * FIELDS * PLANE, sets * AUX * PLANE, sets * FIELDS * DEEP * FACES] + [
        FIELDS * lines,
        4 * patches // LANE * FIELDS * PX,
        sets * FIELDS * 10 * SUB,
        sets * FIELDS * 8 * SUB,
    ]
    out = pl.pallas_call(
        functools.partial(step_kernel, group, count, patches, slots),
        out_shape=jax.ShapeDtypeStruct((1, 1, FIELDS, slots, SUB * LANE), f32),
        in_specs=[vmem] * (5 + group),
        out_specs=vmem,
        scratch_shapes=[pltpu.VMEM((n, LANE), f32) for n in scratch_rows],
        compiler_params=limit(*scratch_rows, *made_rows, lanes.shape[0], group * strip_rows, FIELDS * slots * SUB),
        name="step",
    )(*made, lanes, *strips)
    return sides_first(out)


def solution(mesh):
    in_specs = (
        P("gx", "gz", "gy", None, None),
        P(("gx", "gz"), None, None),
        P("gx", "gz", None, None),
        P("gx", "gz", None, None),
        P("gx", "gz", None, None),
        P("gx", "gz", None, None),
    )
    out_specs = P("gx", "gz", "gy", None, None)
    return jax.shard_map(
        per_device, mesh=mesh, in_specs=in_specs, out_specs=out_specs, check_vma=False
    )
```

```python
import functools

import jax
import jax.numpy as jnp
from jax import lax
from jax.experimental import pallas as pl
from jax.experimental.pallas import tpu as pltpu
from jax.sharding import PartitionSpec as P

FIELDS = 5
PX = 32
BOX = 64
SUB = 8
LANE = 128
HALF = PX // 2
STRIDE = BOX - HALF + 1
BOX_ROWS = BOX * BOX // LANE
heat_ratio = 1.4
courant = 0.3
WEST, EAST, SOUTH, NORTH = range(4)
BLOCKS = LANE // PX
DEEP = PX // BLOCKS
SPAN = PX + 2 * SUB
PLANE = (DEEP + 2) * SPAN
FACES = PX + SUB
AUX = 2 * (FIELDS + 1)


def spot(row, column):
    return (row + 1) * SPAN + SUB + column


def power_of_two(n):
    return n & (n - 1) == 0


def masks_of(n):
    return [n >> (i + 1) for i in range(n.bit_length() - 1)]


def primitive(u):
    inverse = 1.0 / u[0]
    vx, vy, vz = u[1] * inverse, u[2] * inverse, u[3] * inverse
    kinetic = u[1] * (0.5 * vx) + u[2] * (0.5 * vy) + u[3] * (0.5 * vz)
    pressure = (heat_ratio - 1.0) * (u[4] - kinetic)
    sound = jnp.sqrt(heat_ratio * pressure * inverse)
    return vx, vy, pressure, sound


def half_flux(u, moving, pressure, sound, normal):
    half = 0.5 * moving
    flux = [u[f] * half for f in range(FIELDS)]
    flux[normal] = flux[normal] + 0.5 * pressure
    flux[4] = flux[4] + pressure * half
    return flux + [0.5 * (jnp.abs(moving) + sound)]


def face_flux(low_u, low_aux, u, aux):
    wave = jnp.maximum(low_aux[FIELDS], aux[FIELDS])
    return [low_aux[f] + aux[f] - wave * (u[f] - low_u[f]) for f in range(FIELDS)]


def lane_of():
    return lax.broadcasted_iota(jnp.int32, (SUB, LANE), 1)


def sub_of():
    return lax.broadcasted_iota(jnp.int32, (SUB, LANE), 0)


def take_lanes(x, lanes):
    return jnp.take_along_axis(x, lanes, axis=1, mode="promise_in_bounds")


def top_speed(u):
    vx, vy, _, sound = primitive(u)
    return jnp.maximum(jnp.abs(vx), jnp.abs(vy)) + sound


def make_lanes(group, count, patches, slots, around_ref, owner_ref, lanes_ref, table, slot_ref):
    me = lax.axis_index("gy")
    capacity = slots // group
    sets = patches // PX
    lane = lane_of()
    block, in_block = lane // PX, lane & (PX - 1)
    turn = me * count

    for i in range(slots):
        slot_ref[i] = -1

    def rank_source(source, carry):
        rank = jnp.int32(0)
        for i in range(count):
            p = source * count + i
            hit = owner_ref[0, 0, 0, p] == me
            slot_ref[jnp.where(hit, source * capacity + rank, slots)] = p
            rank = rank + jnp.where(hit, 1, 0)
        return carry

    lax.fori_loop(0, group, rank_source, 0)
    held = jnp.full((SUB, LANE), -1, jnp.int32)
    for j in range(slots):
        held = jnp.where(in_block == j, slot_ref[j], held)
    lanes_ref[sets * 4 * 3 * SUB :, :] = held

    table[0:4, 0:patches] = around_ref[0, 0]
    for g in range(sets):
        patch = (g * PX + in_block) ^ turn
        for side in range(4):
            near = take_lanes(jnp.broadcast_to(table[side : side + 1, :], (SUB, LANE)), patch)
            place = jnp.maximum(near, 0) ^ turn
            pick, origin = place & (PX - 1), lax.shift_right_logical(place, 5)
            lacking = jnp.where(near < 0, 1, 0)
            if side in (WEST, EAST):
                pick = pick + PX * block
            else:
                edge, step = (0, -PX) if side == SOUTH else (BLOCKS - 1, PX)
                across = pick + (LANE - PX if side == SOUTH else 0)
                pick = jnp.where(block == edge, across, lane + step)
                origin = jnp.where(block == edge, origin, g)
                lacking = jnp.where(block == edge, lacking, 0)
            for kind, x in enumerate((pick, origin, lacking)):
                at = ((g * 4 + side) * 3 + kind) * SUB
                lanes_ref[at : at + SUB, :] = x


def place_of(me, other, n):
    if power_of_two(n):
        return me ^ other
    behind = me - other
    return jnp.where(behind < 0, behind + n, behind)


def pack_kernel(tiles, rows, group, count, patches, slots, mesh_sizes, *refs):
    owner_ref, around_ref, which_ref, start_ref, patch_ref, box_ref = refs[:6]
    n_gx, n_gz = mesh_sizes
    pay_ref, raw_ref, lanes_ref = refs[6:9]
    cut_refs, (table, slot_ref) = refs[9 : 9 + n_gz], refs[9 + n_gz :]
    raw_ref[...] = patch_ref[...]
    me = lax.axis_index("gy")
    top = None
    for s in range(SUB):
        wave = top_speed([patch_ref[0, 0, f, :, s * LANE : (s + 1) * LANE] for f in range(FIELDS)])
        top = wave if top is None else jnp.maximum(top, wave)
    for f in range(FIELDS):
        pay_ref[f * tiles : (f + 1) * tiles, :] = box_ref[pl.ds(f * BOX_ROWS + me * tiles, tiles), :]
    pay_ref[rows - SUB : rows, :] = top

    start, which = start_ref[0, 0], which_ref[0, 0]
    row = lax.shift_right_logical(start * 2675, 17)
    offset = BOX * (row & 1) + start - row * STRIDE
    near = lax.shift_right_logical(row, 1) - me * tiles
    place = place_of(lax.axis_index("gx"), lax.shift_right_logical(which, n_gz.bit_length() - 1), n_gx)
    apart = (which & (n_gz - 1)) ^ lax.axis_index("gz")
    patch = lax.broadcasted_iota(jnp.int32, start.shape, 1)
    for k in range(n_gz):
        mine = (near >= 0) & (near < tiles) & (apart == k)
        cut_refs[k][0:4, 0:patches] = jnp.where(mine, place * rows + near, n_gx * rows)
        cut_refs[k][4:8, 0:patches] = (HALF * (patch & (SUB - 1)) - offset) & (LANE - 1)
    make_lanes(group, count, patches, slots, around_ref, owner_ref, lanes_ref, table, slot_ref)


def strip_kernel(parts, groups, rows, tiles, patches, *refs):
    cut_refs, pay_ref, out_refs = refs[:groups], refs[groups], refs[groups + 1 :]
    top = pay_ref[rows - SUB : rows, :]
    for k in range(1, parts):
        top = jnp.maximum(top, pay_ref[(k + 1) * rows - SUB : (k + 1) * rows, :])
    block = lane_of() // HALF
    lines = 4 * patches // SUB
    for cut_ref, out_ref in zip(cut_refs, out_refs):
        out_ref[FIELDS * lines :, :] = top
        for v in range(lines):
            side, first = v // (patches // SUB), v % (patches // SUB) * SUB
            acc = None
            for m in range(SUB):
                strip = pay_ref[pl.ds(cut_ref[side, first + m], SUB, stride=tiles), :]
                strip = pltpu.roll(strip, cut_ref[4 + side, first + m], 1)
                acc = strip if acc is None else jnp.where(block == m, strip, acc)
            out_ref[pl.ds(v, FIELDS, stride=lines), :] = acc[:FIELDS, :]


def lanes_at(lanes_ref, g, side, kind):
    at = ((g * 4 + side) * 3 + kind) * SUB
    return lanes_ref[at : at + SUB, :]


def held_at(lanes_ref, sets):
    return lanes_ref[sets * 4 * 3 * SUB : (sets * 4 * 3 + 1) * SUB, :]


def fill_ghosts(u_ref, lanes_ref, coarse_ref, sets):
    for f in range(FIELDS):
        for g in range(sets):

            def ghost(side, at, kept):
                x = None
                for o in range(sets):
                    start = (o * FIELDS + f) * PLANE + at
                    edge = pl.ds(start, DEEP, stride=SPAN) if side in (WEST, EAST) else pl.ds(start, SUB)
                    moved = take_lanes(u_ref[edge, :], lanes_at(lanes_ref, g, side, 0))
                    x = moved if x is None else jnp.where(lanes_at(lanes_ref, g, side, 1) == o, moved, x)
                if coarse_ref is None:
                    return x
                start = ((g * FIELDS + f) * 10 + kept) * SUB
                return jnp.where(lanes_at(lanes_ref, g, side, 2) != 0, coarse_ref[start : start + SUB, :], x)

            base = (g * FIELDS + f) * PLANE
            for side, column, to in ((WEST, PX - 1, -1), (EAST, 0, PX)):
                u_ref[pl.ds(base + spot(0, to), DEEP, stride=SPAN), :] = ghost(side, spot(0, column), side)
            for side, row, to in ((SOUTH, DEEP - 1, -1), (NORTH, 0, DEEP)):
                for i in range(BLOCKS):
                    kept = 2 + (side - SOUTH) * BLOCKS + i
                    u_ref[pl.ds(base + spot(to, SUB * i), SUB), :] = ghost(side, spot(row, SUB * i), kept)


def halves_of(u, axis):
    vx, vy, pressure, sound = primitive(u)
    return half_flux(u, (vx, vy)[axis], pressure, sound, axis + 1)


def fill_halves(u_ref, aux_ref, sets):
    def fill(g, rows, axes):
        u = [u_ref[rows((g * FIELDS + f) * PLANE), :] for f in range(FIELDS)]
        vx, vy, pressure, sound = primitive(u)
        for axis in axes:
            for n, x in enumerate(half_flux(u, (vx, vy)[axis], pressure, sound, axis + 1)):
                aux_ref[rows((g * AUX + axis * (FIELDS + 1) + n) * PLANE), :] = x

    for g in range(sets):

        def cells(r, carry):
            for half in range(2):
                for i in range(BLOCKS):
                    at = spot(2 * r + half, SUB * i)
                    fill(g, lambda b, at=at: pl.ds(pl.multiple_of(b + at, SUB), SUB), (0, 1))
            return carry

        lax.fori_loop(0, DEEP // 2, cells, 0)
        for r in (-1, DEEP):
            for i in range(BLOCKS):
                fill(g, lambda b, at=spot(r, SUB * i): pl.ds(b + at, SUB), (1,))
        for c in (-1, PX):
            fill(g, lambda b, at=spot(0, c): pl.ds(b + at, DEEP, stride=SPAN), (0,))


def load_cells(u_ref, aux_ref, g, axis, rows):
    u = [u_ref[rows((g * FIELDS + f) * PLANE), :] for f in range(FIELDS)]
    start = g * AUX + axis * (FIELDS + 1)
    return u, [aux_ref[rows((start + n) * PLANE), :] for n in range(FIELDS + 1)]


def at_row(at):
    return lambda b: pl.ds(b + at, SUB)


def fill_x_faces(u_ref, aux_ref, dx_ref, g, base):
    def across(r, carry):
        for half in range(2):
            row = 2 * r + half
            for i in range(BLOCKS + 1):
                at = pl.multiple_of(spot(row, SUB * i), SUB)
                low = load_cells(u_ref, aux_ref, g, 0, at_row(at - 1))
                faces = face_flux(*low, *load_cells(u_ref, aux_ref, g, 0, at_row(at)))
                for f in range(FIELDS):
                    to = pl.multiple_of(base + (f * DEEP + row) * FACES + SUB * i, SUB)
                    dx_ref[pl.ds(to, SUB), :] = faces[f]
        return carry

    lax.fori_loop(0, DEEP // 2, across, 0)


def x_change(dx_ref, base, f, row, i):
    west = pl.multiple_of(base + (f * DEEP + row) * FACES + SUB * i, SUB)
    return dx_ref[pl.ds(west, SUB), :] - dx_ref[pl.ds(west + 1, SUB), :]


def prepare_kernel(group, count, patches, lanes_ref, *refs):
    raw_refs = refs[:group]
    u_ref, edge_ref, dx_ref, dy_ref, aux_ref = refs[group:]
    sets = patches // PX

    for f in range(FIELDS):
        for g in range(sets):
            for h in range(2):
                tiles = []
                for q in range(BLOCKS):
                    at = (q * 2 + h) * LANE
                    for k in range(PX // count):
                        tiles.append(raw_refs[g * (PX // count) + k][0, 0, f, :, at : at + LANE])
                cells = jnp.concatenate(tiles, axis=0).T
                for i in range(BLOCKS):
                    to = (g * FIELDS + f) * PLANE + spot(h * BLOCKS + i, 0)
                    u_ref[to : to + PX, :] = cells[i * PX : (i + 1) * PX, :]

    fill_ghosts(u_ref, lanes_ref, None, sets)
    fill_halves(u_ref, aux_ref, sets)
    for g in range(sets):
        fill_x_faces(u_ref, aux_ref, dx_ref, g, g * FIELDS * DEEP * FACES)

        def along(i, carry):
            low = load_cells(u_ref, aux_ref, g, 1, at_row(pl.multiple_of(spot(-1, SUB * i), SUB)))
            for r in range(DEEP + 1):
                cell = load_cells(u_ref, aux_ref, g, 1, at_row(pl.multiple_of(spot(r, SUB * i), SUB)))
                for f, face in enumerate(face_flux(*low, *cell)):
                    to = pl.multiple_of(((g * FIELDS + f) * (DEEP + 1) + r) * PX + SUB * i, SUB)
                    dy_ref[pl.ds(to, SUB), :] = face
                low = cell
            return carry

        lax.fori_loop(0, BLOCKS, along, 0)
        for side in range(4):
            for i, rows in enumerate(edge_rows(side)):
                for n in range(FIELDS + 1):
                    start = g * AUX + (0 if side in (WEST, EAST) else FIELDS + 1) + n
                    to = edge_place(g, side, i, n)
                    edge_ref[to : to + SUB, :] = aux_ref[rows(start * PLANE), :]


def edge_rows(side):
    if side in (WEST, EAST):
        at = spot(0, 0 if side == WEST else PX - 1)
        return [lambda b: pl.ds(b + at, DEEP, stride=SPAN)]
    return [at_row(spot(0 if side == SOUTH else DEEP - 1, SUB * i)) for i in range(BLOCKS)]


def edge_place(g, side, i, n):
    kept = side if side in (WEST, EAST) else 2 + (side - SOUTH) * BLOCKS + i
    return ((g * 10 + kept) * (FIELDS + 1) + n) * SUB


def step_kernel(count, patches, slots, *refs):
    u_ref, edge_ref, dx_ref, dy_ref, lanes_ref = refs[:5]
    strip_refs, out_ref = refs[5:7], refs[7]
    next_u, next_aux, next_dx, strips, doubled, coarse_ref, border_ref = refs[8:]
    lines = 4 * patches // SUB
    sets = patches // PX
    lane, sub = lane_of(), sub_of()
    block, in_block = lane // PX, lane & (PX - 1)
    turn = lax.axis_index("gy") * count

    def joined(at, join):
        return functools.reduce(join, [ref[at : at + SUB, :] for ref in strip_refs])

    for at in range(0, FIELDS * lines, SUB):
        strips[at : at + SUB, :] = joined(at, jnp.add)
    time_step = courant / jnp.max(joined(FIELDS * lines, jnp.maximum))
    part = HALF * sub + (lane & (HALF - 1))
    for t in range(4 * patches // LANE):
        tiles = []
        for v in range(t * HALF, (t + 1) * HALF):
            tile = None
            for f in range(FIELDS):
                row = jnp.broadcast_to(strips[f * lines + v : f * lines + v + 1, :], (SUB, LANE))
                wide = take_lanes(row, part)
                tile = wide if tile is None else jnp.where(lane // HALF == f, wide, tile)
            tiles.append(tile)
        cells = jnp.concatenate(tiles, axis=0).T
        for n in range(FIELDS * 2):
            for twice in range(2):
                at = t * FIELDS * PX + n * HALF + twice
                doubled[pl.ds(at, SUB, stride=2), :] = cells[n * SUB : (n + 1) * SUB, :]

    for g in range(sets):
        patch = (g * PX + in_block) ^ turn
        for side in range(4):
            t, shift = side * patches // LANE, side * patches % LANE
            for f in range(FIELDS):
                pieces = []
                for i in range(BLOCKS):
                    at = t * FIELDS * PX + f * PX + SUB * i
                    pieces.append(take_lanes(doubled[at : at + SUB, :], patch + shift))
                base = (g * FIELDS + f) * 10
                if side in (WEST, EAST):
                    x = pieces[0]
                    for q in range(1, BLOCKS):
                        x = jnp.where(block == q, pieces[q], x)
                    coarse_ref[(base + side) * SUB : (base + side + 1) * SUB, :] = x
                else:
                    for i in range(BLOCKS):
                        at = (base + 2 + (side - SOUTH) * BLOCKS + i) * SUB
                        coarse_ref[at : at + SUB, :] = pieces[i]

    size = FIELDS * DEEP * FACES
    for g in range(sets):
        for at in range(0, size, SUB):
            next_dx[g * size + at : g * size + at + SUB, :] = dx_ref[g * size + at : g * size + at + SUB, :]

        def coarse_cells(kept, axis):
            at = [((g * FIELDS + f) * 10 + kept) * SUB for f in range(FIELDS)]
            u = [coarse_ref[a : a + SUB, :] for a in at]
            return u, halves_of(u, axis)

        def own_cells(side, i):
            rows = edge_rows(side)[i]
            places = [edge_place(g, side, i, n) for n in range(FIELDS + 1)]
            u = [u_ref[rows((g * FIELDS + f) * PLANE), :] for f in range(FIELDS)]
            return u, [edge_ref[at : at + SUB, :] for at in places]

        for side, face in ((WEST, 0), (EAST, PX)):
            beyond, own = coarse_cells(side, 0), own_cells(side, 0)
            faces = face_flux(*beyond, *own) if side == WEST else face_flux(*own, *beyond)
            lacking = lanes_at(lanes_ref, g, side, 2) != 0
            for f in range(FIELDS):
                rows = pl.ds(g * size + f * DEEP * FACES + face, DEEP, stride=FACES)
                next_dx[rows, :] = jnp.where(lacking, faces[f], dx_ref[rows, :])
        for side, face in ((SOUTH, 0), (NORTH, DEEP)):
            lacking = lanes_at(lanes_ref, g, side, 2) != 0
            for i in range(BLOCKS):
                kept = (side - SOUTH) * BLOCKS + i
                beyond, own = coarse_cells(2 + kept, 1), own_cells(side, i)
                faces = face_flux(*beyond, *own) if side == SOUTH else face_flux(*own, *beyond)
                for f in range(FIELDS):
                    fine = ((g * FIELDS + f) * (DEEP + 1) + face) * PX + SUB * i
                    to = ((g * FIELDS + f) * 8 + kept) * SUB
                    border_ref[to : to + SUB, :] = jnp.where(lacking, faces[f], dy_ref[fine : fine + SUB, :])

        def update(f, carry):
            for i in range(BLOCKS):
                for r in range(DEEP):
                    faces = []
                    for n in (r, r + 1):
                        if n in (0, DEEP):
                            at = ((g * FIELDS + f) * 8 + (BLOCKS if n else 0) + i) * SUB
                            faces.append(border_ref[pl.ds(pl.multiple_of(at, SUB), SUB), :])
                        else:
                            at = ((g * FIELDS + f) * (DEEP + 1) + n) * PX + SUB * i
                            faces.append(dy_ref[pl.ds(pl.multiple_of(at, SUB), SUB), :])
                    change = x_change(next_dx, g * size, f, r, i) + (faces[0] - faces[1])
                    at = pl.ds(pl.multiple_of((g * FIELDS + f) * PLANE + spot(r, SUB * i), SUB), SUB)
                    next_u[at, :] = u_ref[at, :] + time_step * change
            return carry

        lax.fori_loop(0, FIELDS, update, 0)

    fill_ghosts(next_u, lanes_ref, coarse_ref, sets)
    fill_halves(next_u, next_aux, sets)
    for g in range(sets):
        fill_x_faces(next_u, next_aux, next_dx, g, g * size)

        def along(half, carry):
            for i in (2 * half, 2 * half + 1):
                low = load_cells(next_u, next_aux, g, 1, at_row(pl.multiple_of(spot(-1, SUB * i), SUB)))
                low_faces = None
                for r in range(DEEP + 1):
                    cell = load_cells(next_u, next_aux, g, 1, at_row(pl.multiple_of(spot(r, SUB * i), SUB)))
                    faces = face_flux(*low, *cell)
                    for f in range(FIELDS):
                        if r == 0:
                            continue
                        change = x_change(next_dx, g * size, f, r - 1, i) + (low_faces[f] - faces[f])
                        new = low[0][f] + time_step * change
                        at = pl.ds(pl.multiple_of((g * FIELDS + f) * PLANE + spot(r - 1, SUB * i), SUB), SUB)
                        next_u[at, :] = 0.5 * u_ref[at, :] + 0.5 * new
                    low, low_faces = cell, faces
            return carry

        lax.fori_loop(0, BLOCKS // 2, along, 0)

    held = held_at(lanes_ref, sets)
    place = jnp.maximum(held, 0) ^ turn
    pick, origin = PX * block + (place & (PX - 1)), lax.shift_right_logical(place, 5)
    for f in range(FIELDS):
        for h in range(2):
            tiles = []
            for i in range(LANE // SUB):
                at = spot(h * BLOCKS + i // BLOCKS, SUB * (i % BLOCKS))
                x = None
                for g in range(sets):
                    start = (g * FIELDS + f) * PLANE + at
                    moved = take_lanes(next_u[start : start + SUB, :], pick)
                    x = moved if x is None else jnp.where(origin == g, moved, x)
                tiles.append(jnp.where(held >= 0, x, 0.0))
            cells = jnp.concatenate(tiles, axis=0).T
            for q in range(BLOCKS):
                at = (q * 2 + h) * LANE
                out_ref[0, 0, f, :, at : at + LANE] = cells[q * PX : q * PX + slots, :]


def limit(*row_counts):
    return pltpu.CompilerParams(vmem_limit_bytes=(sum(row_counts) * LANE * 4 * 5 // 4) + (1 << 20))


def per_device(patch_state, coarse_boxes, new_owner, neighbors, coarse_box, coarse_start):
    count = patch_state.shape[2]
    n_gx, n_gz, group = lax.axis_size("gx"), lax.axis_size("gz"), lax.axis_size("gy")
    parts = n_gx * n_gz
    patches = count * group
    lines = 4 * patches // SUB
    slots = group * max(2, 2 * count // group)
    tiles = BOX_ROWS // group
    rows = -(-tiles * FIELDS // SUB) * SUB + SUB
    strip_rows = FIELDS * lines + SUB
    vmem = pl.BlockSpec(memory_space=pltpu.VMEM)
    smem = pl.BlockSpec(memory_space=pltpu.SMEM)
    f32 = jnp.float32

    def sides_first(x):
        return jnp.swapaxes(x, 2, 3)

    sets = patches // PX
    payload, raw, lanes, *cuts = pl.pallas_call(
        functools.partial(pack_kernel, tiles, rows, group, count, patches, slots, (n_gx, n_gz)),
        out_shape=(
            pltpu.VMEM((rows, LANE), f32),
            pltpu.VMEM((1, 1, FIELDS, count, SUB * LANE), f32),
            pltpu.VMEM(((sets * 4 * 3 + 1) * SUB, LANE), jnp.int32),
        )
        + (pltpu.VMEM((SUB, max(LANE, patches)), jnp.int32),) * n_gz,
        in_specs=[smem] + [vmem] * 5,
        out_specs=(vmem,) * (3 + n_gz),
        scratch_shapes=[pltpu.VMEM((SUB, LANE), jnp.int32), pltpu.SMEM((slots + 1,), jnp.int32)],
        name="pack",
    )(
        sides_first(new_owner),
        sides_first(neighbors),
        sides_first(coarse_box),
        sides_first(coarse_start),
        sides_first(patch_state),
        coarse_boxes.reshape(FIELDS * BOX_ROWS, LANE),
    )

    if power_of_two(n_gx):
        perms = [[(i, i ^ k) for i in range(n_gx)] for k in range(1, n_gx)]
    else:
        perms = [[(i, (i + k) % n_gx) for i in range(n_gx)] for k in range(1, n_gx)]
    boxes = [payload] + [lax.ppermute(payload, "gx", perm) for perm in perms]
    boxes = jnp.concatenate(boxes + [jnp.zeros((SUB * tiles, LANE), f32)], axis=0)
    cuts = cuts[:1] + [lax.ppermute(cuts[k], "gz", [(i, i ^ k) for i in range(n_gz)]) for k in range(1, n_gz)]

    strips = pl.pallas_call(
        functools.partial(strip_kernel, n_gx, n_gz, rows, tiles, patches),
        out_shape=[pltpu.VMEM((strip_rows, LANE), f32)] * n_gz,
        in_specs=[smem] * n_gz + [vmem],
        out_specs=[vmem] * n_gz,
        compiler_params=limit(n_gx * rows + SUB * tiles, n_gz * strip_rows),
        name="strips",
    )(*cuts, boxes)

    def to_group(x, after=None):
        blocks, have = [x] + [None] * (group - 1), [0]
        masks = masks_of(group)
        for mask in masks:
            perm = [(i, i ^ mask) for i in range(group)]
            for k in have:
                block = blocks[k]
                if after is not None and mask == masks[-1] and k:
                    block, _ = lax.optimization_barrier((block, after))
                blocks[k ^ mask] = lax.ppermute(block, "gy", perm)
            have = have + [k ^ mask for k in have]
        return blocks

    raws = to_group(raw, strips[0])

    shares = [strips[0]]
    for k in range(1, n_gz * group):
        if k // n_gz % 2 == 0:
            perm = [(i, i ^ k) for i in range(n_gz * group)]
            shares.append(lax.ppermute(strips[k % n_gz], ("gy", "gz"), perm))

    made_rows = [
        sets * FIELDS * PLANE,
        sets * 10 * (FIELDS + 1) * SUB,
        sets * FIELDS * DEEP * FACES,
        sets * FIELDS * (DEEP + 1) * PX,
    ]
    made = pl.pallas_call(
        functools.partial(prepare_kernel, group, count, patches),
        out_shape=[pltpu.VMEM((n, LANE), f32) for n in made_rows],
        in_specs=[vmem] * (1 + group),
        out_specs=[vmem] * 4,
        scratch_shapes=[pltpu.VMEM((sets * AUX * PLANE, LANE), f32)],
        compiler_params=limit(*made_rows, sets * AUX * PLANE, lanes.shape[0], patches * FIELDS * SUB),
        cost_estimate=pl.CostEstimate(flops=patches * 1024 * 300, bytes_accessed=patches * 40000, transcendentals=0),
        name="prepare",
    )(lanes, *raws)

    shares = lax.optimization_barrier(shares + [made[0]])[:-1]
    row = lax.broadcasted_iota(jnp.int32, (strip_rows, LANE), 0)
    joined = jnp.where(row < FIELDS * lines, functools.reduce(jnp.add, shares), functools.reduce(jnp.maximum, shares))

    strips = [joined, lax.ppermute(joined, "gy", [(i, i ^ 1) for i in range(group)])]
    scratch_rows = [sets * FIELDS * PLANE, sets * AUX * PLANE, sets * FIELDS * DEEP * FACES] + [
        FIELDS * lines,
        4 * patches // LANE * FIELDS * PX,
        sets * FIELDS * 10 * SUB,
        sets * FIELDS * 8 * SUB,
    ]
    out = pl.pallas_call(
        functools.partial(step_kernel, count, patches, slots),
        out_shape=jax.ShapeDtypeStruct((1, 1, FIELDS, slots, SUB * LANE), f32),
        in_specs=[vmem] * 7,
        out_specs=vmem,
        scratch_shapes=[pltpu.VMEM((n, LANE), f32) for n in scratch_rows],
        compiler_params=limit(*scratch_rows, *made_rows, lanes.shape[0], 2 * strip_rows, FIELDS * slots * SUB),
        name="step",
    )(*made, lanes, *strips)
    return sides_first(out)


def solution(mesh):
    in_specs = (
        P("gx", "gz", "gy", None, None),
        P(("gx", "gz"), None, None),
        P("gx", "gz", None, None),
        P("gx", "gz", None, None),
        P("gx", "gz", None, None),
        P("gx", "gz", None, None),
    )
    out_specs = P("gx", "gz", "gy", None, None)
    return jax.shard_map(
        per_device, mesh=mesh, in_specs=in_specs, out_specs=out_specs, check_vma=False
    )
```

```python
import functools

import jax
import jax.numpy as jnp
from jax import lax
from jax.experimental import pallas as pl
from jax.experimental.pallas import tpu as pltpu
from jax.sharding import PartitionSpec as P

FIELDS = 5
PX = 32
BOX = 64
SUB = 8
LANE = 128
HALF = PX // 2
STRIDE = BOX - HALF + 1
BOX_ROWS = BOX * BOX // LANE
heat_ratio = 1.4
courant = 0.3
WEST, EAST, SOUTH, NORTH = range(4)
BLOCKS = LANE // PX
DEEP = PX // BLOCKS
SPAN = PX + 2 * SUB
PLANE = (DEEP + 2) * SPAN
FACES = PX + SUB
AUX = 2 * (FIELDS + 1)


def spot(row, column):
    return (row + 1) * SPAN + SUB + column


def power_of_two(n):
    return n & (n - 1) == 0


def masks_of(n):
    return [n >> (i + 1) for i in range(n.bit_length() - 1)]


def primitive(u):
    inverse = 1.0 / u[0]
    vx, vy, vz = u[1] * inverse, u[2] * inverse, u[3] * inverse
    kinetic = u[1] * (0.5 * vx) + u[2] * (0.5 * vy) + u[3] * (0.5 * vz)
    pressure = (heat_ratio - 1.0) * (u[4] - kinetic)
    sound = jnp.sqrt(heat_ratio * pressure * inverse)
    return vx, vy, pressure, sound


def half_flux(u, moving, pressure, sound, normal):
    half = 0.5 * moving
    flux = [u[f] * half for f in range(FIELDS)]
    flux[normal] = flux[normal] + 0.5 * pressure
    flux[4] = flux[4] + pressure * half
    return flux + [0.5 * (jnp.abs(moving) + sound)]


def face_flux(low_u, low_aux, u, aux):
    wave = jnp.maximum(low_aux[FIELDS], aux[FIELDS])
    return [low_aux[f] + aux[f] - wave * (u[f] - low_u[f]) for f in range(FIELDS)]


def lane_of():
    return lax.broadcasted_iota(jnp.int32, (SUB, LANE), 1)


def sub_of():
    return lax.broadcasted_iota(jnp.int32, (SUB, LANE), 0)


def take_lanes(x, lanes):
    return jnp.take_along_axis(x, lanes, axis=1, mode="promise_in_bounds")


def top_speed(u):
    vx, vy, _, sound = primitive(u)
    return jnp.maximum(jnp.abs(vx), jnp.abs(vy)) + sound


def make_lanes(group, count, patches, slots, around_ref, owner_ref, lanes_ref, table, slot_ref):
    me = lax.axis_index("gy")
    capacity = slots // group
    sets = patches // PX
    lane = lane_of()
    block, in_block = lane // PX, lane & (PX - 1)
    turn = me * count

    for i in range(slots):
        slot_ref[i] = -1

    def rank_source(source, carry):
        rank = jnp.int32(0)
        for i in range(count):
            p = source * count + i
            hit = owner_ref[0, 0, 0, p] == me
            slot_ref[jnp.where(hit, source * capacity + rank, slots)] = p
            rank = rank + jnp.where(hit, 1, 0)
        return carry

    lax.fori_loop(0, group, rank_source, 0)
    held = jnp.full((SUB, LANE), -1, jnp.int32)
    for j in range(slots):
        held = jnp.where(in_block == j, slot_ref[j], held)
    lanes_ref[sets * 4 * 3 * SUB :, :] = held

    table[0:4, 0:patches] = around_ref[0, 0]
    for g in range(sets):
        patch = (g * PX + in_block) ^ turn
        for side in range(4):
            near = take_lanes(jnp.broadcast_to(table[side : side + 1, :], (SUB, LANE)), patch)
            place = jnp.maximum(near, 0) ^ turn
            pick, origin = place & (PX - 1), lax.shift_right_logical(place, 5)
            lacking = jnp.where(near < 0, 1, 0)
            if side in (WEST, EAST):
                pick = pick + PX * block
            else:
                edge, step = (0, -PX) if side == SOUTH else (BLOCKS - 1, PX)
                across = pick + (LANE - PX if side == SOUTH else 0)
                pick = jnp.where(block == edge, across, lane + step)
                origin = jnp.where(block == edge, origin, g)
                lacking = jnp.where(block == edge, lacking, 0)
            for kind, x in enumerate((pick, origin, lacking)):
                at = ((g * 4 + side) * 3 + kind) * SUB
                lanes_ref[at : at + SUB, :] = x


def place_of(me, other, n):
    if power_of_two(n):
        return me ^ other
    behind = me - other
    return jnp.where(behind < 0, behind + n, behind)


def pack_kernel(tiles, rows, group, count, patches, slots, mesh_sizes, *refs):
    owner_ref, around_ref, which_ref, start_ref, patch_ref, box_ref = refs[:6]
    n_gx, n_gz = mesh_sizes
    pay_ref, raw_ref, lanes_ref = refs[6:9]
    cut_refs, (table, slot_ref) = refs[9 : 9 + n_gz], refs[9 + n_gz :]
    raw_ref[...] = patch_ref[...]
    me = lax.axis_index("gy")
    top = None
    for s in range(SUB):
        wave = top_speed([patch_ref[0, 0, f, :, s * LANE : (s + 1) * LANE] for f in range(FIELDS)])
        top = wave if top is None else jnp.maximum(top, wave)
    for f in range(FIELDS):
        pay_ref[f * tiles : (f + 1) * tiles, :] = box_ref[pl.ds(f * BOX_ROWS + me * tiles, tiles), :]
    pay_ref[rows - SUB : rows, :] = top

    start, which = start_ref[0, 0], which_ref[0, 0]
    row = lax.shift_right_logical(start * 2675, 17)
    offset = BOX * (row & 1) + start - row * STRIDE
    near = lax.shift_right_logical(row, 1) - me * tiles
    place = place_of(lax.axis_index("gx"), lax.shift_right_logical(which, n_gz.bit_length() - 1), n_gx)
    apart = (which & (n_gz - 1)) ^ lax.axis_index("gz")
    patch = lax.broadcasted_iota(jnp.int32, start.shape, 1)
    for k in range(n_gz):
        mine = (near >= 0) & (near < tiles) & (apart == k)
        cut_refs[k][0:4, 0:patches] = jnp.where(mine, place * rows + near, n_gx * rows)
        cut_refs[k][4:8, 0:patches] = (HALF * (patch & (SUB - 1)) - offset) & (LANE - 1)
    make_lanes(group, count, patches, slots, around_ref, owner_ref, lanes_ref, table, slot_ref)


def strip_kernel(parts, groups, rows, tiles, patches, *refs):
    cut_refs, pay_ref, out_refs = refs[:groups], refs[groups], refs[groups + 1 :]
    top = pay_ref[rows - SUB : rows, :]
    for k in range(1, parts):
        top = jnp.maximum(top, pay_ref[(k + 1) * rows - SUB : (k + 1) * rows, :])
    block = lane_of() // HALF
    lines = 4 * patches // SUB
    for cut_ref, out_ref in zip(cut_refs, out_refs):
        out_ref[FIELDS * lines :, :] = top
        for v in range(lines):
            side, first = v // (patches // SUB), v % (patches // SUB) * SUB
            acc = None
            for m in range(SUB):
                strip = pay_ref[pl.ds(cut_ref[side, first + m], SUB, stride=tiles), :]
                strip = pltpu.roll(strip, cut_ref[4 + side, first + m], 1)
                acc = strip if acc is None else jnp.where(block == m, strip, acc)
            out_ref[pl.ds(v, FIELDS, stride=lines), :] = acc[:FIELDS, :]


def lanes_at(lanes_ref, g, side, kind):
    at = ((g * 4 + side) * 3 + kind) * SUB
    return lanes_ref[at : at + SUB, :]


def held_at(lanes_ref, sets):
    return lanes_ref[sets * 4 * 3 * SUB : (sets * 4 * 3 + 1) * SUB, :]


def fill_ghosts(u_ref, lanes_ref, coarse_ref, sets):
    for f in range(FIELDS):
        for g in range(sets):

            def ghost(side, at, kept):
                x = None
                for o in range(sets):
                    start = (o * FIELDS + f) * PLANE + at
                    edge = pl.ds(start, DEEP, stride=SPAN) if side in (WEST, EAST) else pl.ds(start, SUB)
                    moved = take_lanes(u_ref[edge, :], lanes_at(lanes_ref, g, side, 0))
                    x = moved if x is None else jnp.where(lanes_at(lanes_ref, g, side, 1) == o, moved, x)
                if coarse_ref is None:
                    return x
                start = ((g * FIELDS + f) * 10 + kept) * SUB
                return jnp.where(lanes_at(lanes_ref, g, side, 2) != 0, coarse_ref[start : start + SUB, :], x)

            base = (g * FIELDS + f) * PLANE
            for side, column, to in ((WEST, PX - 1, -1), (EAST, 0, PX)):
                u_ref[pl.ds(base + spot(0, to), DEEP, stride=SPAN), :] = ghost(side, spot(0, column), side)
            for side, row, to in ((SOUTH, DEEP - 1, -1), (NORTH, 0, DEEP)):
                for i in range(BLOCKS):
                    kept = 2 + (side - SOUTH) * BLOCKS + i
                    u_ref[pl.ds(base + spot(to, SUB * i), SUB), :] = ghost(side, spot(row, SUB * i), kept)


def halves_of(u, axis):
    vx, vy, pressure, sound = primitive(u)
    return half_flux(u, (vx, vy)[axis], pressure, sound, axis + 1)


def fill_halves(u_ref, aux_ref, sets):
    def fill(g, rows, axes):
        u = [u_ref[rows((g * FIELDS + f) * PLANE), :] for f in range(FIELDS)]
        vx, vy, pressure, sound = primitive(u)
        for axis in axes:
            for n, x in enumerate(half_flux(u, (vx, vy)[axis], pressure, sound, axis + 1)):
                aux_ref[rows((g * AUX + axis * (FIELDS + 1) + n) * PLANE), :] = x

    for g in range(sets):

        def cells(r, carry):
            for half in range(2):
                for i in range(BLOCKS):
                    at = spot(2 * r + half, SUB * i)
                    fill(g, lambda b, at=at: pl.ds(pl.multiple_of(b + at, SUB), SUB), (0, 1))
            return carry

        lax.fori_loop(0, DEEP // 2, cells, 0)
        for r in (-1, DEEP):
            for i in range(BLOCKS):
                fill(g, lambda b, at=spot(r, SUB * i): pl.ds(b + at, SUB), (1,))
        for c in (-1, PX):
            fill(g, lambda b, at=spot(0, c): pl.ds(b + at, DEEP, stride=SPAN), (0,))


def load_cells(u_ref, aux_ref, g, axis, rows):
    u = [u_ref[rows((g * FIELDS + f) * PLANE), :] for f in range(FIELDS)]
    start = g * AUX + axis * (FIELDS + 1)
    return u, [aux_ref[rows((start + n) * PLANE), :] for n in range(FIELDS + 1)]


def at_row(at):
    return lambda b: pl.ds(b + at, SUB)


def fill_x_faces(u_ref, aux_ref, dx_ref, g, base):
    def across(r, carry):
        for half in range(2):
            row = 2 * r + half
            for i in range(BLOCKS + 1):
                at = pl.multiple_of(spot(row, SUB * i), SUB)
                low = load_cells(u_ref, aux_ref, g, 0, at_row(at - 1))
                faces = face_flux(*low, *load_cells(u_ref, aux_ref, g, 0, at_row(at)))
                for f in range(FIELDS):
                    to = pl.multiple_of(base + (f * DEEP + row) * FACES + SUB * i, SUB)
                    dx_ref[pl.ds(to, SUB), :] = faces[f]
        return carry

    lax.fori_loop(0, DEEP // 2, across, 0)


def x_change(dx_ref, base, f, row, i):
    west = pl.multiple_of(base + (f * DEEP + row) * FACES + SUB * i, SUB)
    return dx_ref[pl.ds(west, SUB), :] - dx_ref[pl.ds(west + 1, SUB), :]


def prepare_kernel(group, count, patches, lanes_ref, *refs):
    raw_refs = refs[:group]
    u_ref, edge_ref, dx_ref, dy_ref, aux_ref = refs[group:]
    sets = patches // PX

    for f in range(FIELDS):
        for g in range(sets):
            for h in range(2):
                tiles = []
                for q in range(BLOCKS):
                    at = (q * 2 + h) * LANE
                    for k in range(PX // count):
                        tiles.append(raw_refs[g * (PX // count) + k][0, 0, f, :, at : at + LANE])
                cells = jnp.concatenate(tiles, axis=0).T
                for i in range(BLOCKS):
                    to = (g * FIELDS + f) * PLANE + spot(h * BLOCKS + i, 0)
                    u_ref[to : to + PX, :] = cells[i * PX : (i + 1) * PX, :]

    fill_ghosts(u_ref, lanes_ref, None, sets)
    fill_halves(u_ref, aux_ref, sets)
    for g in range(sets):
        fill_x_faces(u_ref, aux_ref, dx_ref, g, g * FIELDS * DEEP * FACES)

        def along(i, carry):
            low = load_cells(u_ref, aux_ref, g, 1, at_row(pl.multiple_of(spot(-1, SUB * i), SUB)))
            for r in range(DEEP + 1):
                cell = load_cells(u_ref, aux_ref, g, 1, at_row(pl.multiple_of(spot(r, SUB * i), SUB)))
                for f, face in enumerate(face_flux(*low, *cell)):
                    to = pl.multiple_of(((g * FIELDS + f) * (DEEP + 1) + r) * PX + SUB * i, SUB)
                    dy_ref[pl.ds(to, SUB), :] = face
                low = cell
            return carry

        lax.fori_loop(0, BLOCKS, along, 0)
        for side in range(4):
            for i, rows in enumerate(edge_rows(side)):
                for n in range(FIELDS + 1):
                    start = g * AUX + (0 if side in (WEST, EAST) else FIELDS + 1) + n
                    to = edge_place(g, side, i, n)
                    edge_ref[to : to + SUB, :] = aux_ref[rows(start * PLANE), :]


def edge_rows(side):
    if side in (WEST, EAST):
        at = spot(0, 0 if side == WEST else PX - 1)
        return [lambda b: pl.ds(b + at, DEEP, stride=SPAN)]
    return [at_row(spot(0 if side == SOUTH else DEEP - 1, SUB * i)) for i in range(BLOCKS)]


def edge_place(g, side, i, n):
    kept = side if side in (WEST, EAST) else 2 + (side - SOUTH) * BLOCKS + i
    return ((g * 10 + kept) * (FIELDS + 1) + n) * SUB


def step_kernel(count, patches, slots, *refs):
    u_ref, edge_ref, dx_ref, dy_ref, lanes_ref = refs[:5]
    strip_refs, out_ref = refs[5:7], refs[7]
    next_u, next_aux, next_dx, strips, doubled, coarse_ref, border_ref = refs[8:]
    lines = 4 * patches // SUB
    sets = patches // PX
    lane, sub = lane_of(), sub_of()
    block, in_block = lane // PX, lane & (PX - 1)
    turn = lax.axis_index("gy") * count

    def joined(at, join):
        return functools.reduce(join, [ref[at : at + SUB, :] for ref in strip_refs])

    for at in range(0, FIELDS * lines, SUB):
        strips[at : at + SUB, :] = joined(at, jnp.add)
    time_step = courant / jnp.max(joined(FIELDS * lines, jnp.maximum))
    part = HALF * sub + (lane & (HALF - 1))
    for t in range(4 * patches // LANE):
        tiles = []
        for v in range(t * HALF, (t + 1) * HALF):
            tile = None
            for f in range(FIELDS):
                row = jnp.broadcast_to(strips[f * lines + v : f * lines + v + 1, :], (SUB, LANE))
                wide = take_lanes(row, part)
                tile = wide if tile is None else jnp.where(lane // HALF == f, wide, tile)
            tiles.append(tile)
        cells = jnp.concatenate(tiles, axis=0).T
        for n in range(FIELDS * 2):
            for twice in range(2):
                at = t * FIELDS * PX + n * HALF + twice
                doubled[pl.ds(at, SUB, stride=2), :] = cells[n * SUB : (n + 1) * SUB, :]

    for g in range(sets):
        patch = (g * PX + in_block) ^ turn
        for side in range(4):
            t, shift = side * patches // LANE, side * patches % LANE
            for f in range(FIELDS):
                pieces = []
                for i in range(BLOCKS):
                    at = t * FIELDS * PX + f * PX + SUB * i
                    pieces.append(take_lanes(doubled[at : at + SUB, :], patch + shift))
                base = (g * FIELDS + f) * 10
                if side in (WEST, EAST):
                    x = pieces[0]
                    for q in range(1, BLOCKS):
                        x = jnp.where(block == q, pieces[q], x)
                    coarse_ref[(base + side) * SUB : (base + side + 1) * SUB, :] = x
                else:
                    for i in range(BLOCKS):
                        at = (base + 2 + (side - SOUTH) * BLOCKS + i) * SUB
                        coarse_ref[at : at + SUB, :] = pieces[i]

    size = FIELDS * DEEP * FACES
    for g in range(sets):
        for at in range(0, size, SUB):
            next_dx[g * size + at : g * size + at + SUB, :] = dx_ref[g * size + at : g * size + at + SUB, :]

        def coarse_cells(kept, axis):
            at = [((g * FIELDS + f) * 10 + kept) * SUB for f in range(FIELDS)]
            u = [coarse_ref[a : a + SUB, :] for a in at]
            return u, halves_of(u, axis)

        def own_cells(side, i):
            rows = edge_rows(side)[i]
            places = [edge_place(g, side, i, n) for n in range(FIELDS + 1)]
            u = [u_ref[rows((g * FIELDS + f) * PLANE), :] for f in range(FIELDS)]
            return u, [edge_ref[at : at + SUB, :] for at in places]

        for side, face in ((WEST, 0), (EAST, PX)):
            beyond, own = coarse_cells(side, 0), own_cells(side, 0)
            faces = face_flux(*beyond, *own) if side == WEST else face_flux(*own, *beyond)
            lacking = lanes_at(lanes_ref, g, side, 2) != 0
            for f in range(FIELDS):
                rows = pl.ds(g * size + f * DEEP * FACES + face, DEEP, stride=FACES)
                next_dx[rows, :] = jnp.where(lacking, faces[f], dx_ref[rows, :])
        for side, face in ((SOUTH, 0), (NORTH, DEEP)):
            lacking = lanes_at(lanes_ref, g, side, 2) != 0
            for i in range(BLOCKS):
                kept = (side - SOUTH) * BLOCKS + i
                beyond, own = coarse_cells(2 + kept, 1), own_cells(side, i)
                faces = face_flux(*beyond, *own) if side == SOUTH else face_flux(*own, *beyond)
                for f in range(FIELDS):
                    fine = ((g * FIELDS + f) * (DEEP + 1) + face) * PX + SUB * i
                    to = ((g * FIELDS + f) * 8 + kept) * SUB
                    border_ref[to : to + SUB, :] = jnp.where(lacking, faces[f], dy_ref[fine : fine + SUB, :])

        def update(f, carry):
            for i in range(BLOCKS):
                for r in range(DEEP):
                    faces = []
                    for n in (r, r + 1):
                        if n in (0, DEEP):
                            at = ((g * FIELDS + f) * 8 + (BLOCKS if n else 0) + i) * SUB
                            faces.append(border_ref[pl.ds(pl.multiple_of(at, SUB), SUB), :])
                        else:
                            at = ((g * FIELDS + f) * (DEEP + 1) + n) * PX + SUB * i
                            faces.append(dy_ref[pl.ds(pl.multiple_of(at, SUB), SUB), :])
                    change = x_change(next_dx, g * size, f, r, i) + (faces[0] - faces[1])
                    at = pl.ds(pl.multiple_of((g * FIELDS + f) * PLANE + spot(r, SUB * i), SUB), SUB)
                    next_u[at, :] = u_ref[at, :] + time_step * change
            return carry

        lax.fori_loop(0, FIELDS, update, 0)

    fill_ghosts(next_u, lanes_ref, coarse_ref, sets)
    fill_halves(next_u, next_aux, sets)
    for g in range(sets):
        fill_x_faces(next_u, next_aux, next_dx, g, g * size)

        def along(half, carry):
            for i in (2 * half, 2 * half + 1):
                low = load_cells(next_u, next_aux, g, 1, at_row(pl.multiple_of(spot(-1, SUB * i), SUB)))
                low_faces = None
                for r in range(DEEP + 1):
                    cell = load_cells(next_u, next_aux, g, 1, at_row(pl.multiple_of(spot(r, SUB * i), SUB)))
                    faces = face_flux(*low, *cell)
                    for f in range(FIELDS):
                        if r == 0:
                            continue
                        change = x_change(next_dx, g * size, f, r - 1, i) + (low_faces[f] - faces[f])
                        new = low[0][f] + time_step * change
                        at = pl.ds(pl.multiple_of((g * FIELDS + f) * PLANE + spot(r - 1, SUB * i), SUB), SUB)
                        next_u[at, :] = 0.5 * u_ref[at, :] + 0.5 * new
                    low, low_faces = cell, faces
            return carry

        lax.fori_loop(0, BLOCKS // 2, along, 0)

    held = held_at(lanes_ref, sets)
    place = jnp.maximum(held, 0) ^ turn
    pick, origin = PX * block + (place & (PX - 1)), lax.shift_right_logical(place, 5)
    for f in range(FIELDS):
        for h in range(2):
            tiles = []
            for i in range(LANE // SUB):
                at = spot(h * BLOCKS + i // BLOCKS, SUB * (i % BLOCKS))
                x = None
                for g in range(sets):
                    start = (g * FIELDS + f) * PLANE + at
                    moved = take_lanes(next_u[start : start + SUB, :], pick)
                    x = moved if x is None else jnp.where(origin == g, moved, x)
                tiles.append(jnp.where(held >= 0, x, 0.0))
            cells = jnp.concatenate(tiles, axis=0).T
            for q in range(BLOCKS):
                at = (q * 2 + h) * LANE
                out_ref[0, 0, f, :, at : at + LANE] = cells[q * PX : q * PX + slots, :]


def limit(*row_counts):
    return pltpu.CompilerParams(vmem_limit_bytes=(sum(row_counts) * LANE * 4 * 5 // 4) + (1 << 20))


def per_device(patch_state, coarse_boxes, new_owner, neighbors, coarse_box, coarse_start):
    count = patch_state.shape[2]
    n_gx, n_gz, group = lax.axis_size("gx"), lax.axis_size("gz"), lax.axis_size("gy")
    parts = n_gx * n_gz
    patches = count * group
    lines = 4 * patches // SUB
    slots = group * max(2, 2 * count // group)
    tiles = BOX_ROWS // group
    rows = -(-tiles * FIELDS // SUB) * SUB + SUB
    strip_rows = FIELDS * lines + SUB
    vmem = pl.BlockSpec(memory_space=pltpu.VMEM)
    smem = pl.BlockSpec(memory_space=pltpu.SMEM)
    f32 = jnp.float32

    def sides_first(x):
        return jnp.swapaxes(x, 2, 3)

    sets = patches // PX
    payload, raw, lanes, *cuts = pl.pallas_call(
        functools.partial(pack_kernel, tiles, rows, group, count, patches, slots, (n_gx, n_gz)),
        out_shape=(
            pltpu.VMEM((rows, LANE), f32),
            pltpu.VMEM((1, 1, FIELDS, count, SUB * LANE), f32),
            pltpu.VMEM(((sets * 4 * 3 + 1) * SUB, LANE), jnp.int32),
        )
        + (pltpu.VMEM((SUB, max(LANE, patches)), jnp.int32),) * n_gz,
        in_specs=[smem] + [vmem] * 5,
        out_specs=(vmem,) * (3 + n_gz),
        scratch_shapes=[pltpu.VMEM((SUB, LANE), jnp.int32), pltpu.SMEM((slots + 1,), jnp.int32)],
        name="pack",
    )(
        sides_first(new_owner),
        sides_first(neighbors),
        sides_first(coarse_box),
        sides_first(coarse_start),
        sides_first(patch_state),
        coarse_boxes.reshape(FIELDS * BOX_ROWS, LANE),
    )

    if power_of_two(n_gx):
        perms = [[(i, i ^ k) for i in range(n_gx)] for k in range(1, n_gx)]
    else:
        perms = [[(i, (i + k) % n_gx) for i in range(n_gx)] for k in range(1, n_gx)]
    boxes = [payload] + [lax.ppermute(payload, "gx", perm) for perm in perms]
    boxes = jnp.concatenate(boxes + [jnp.zeros((SUB * tiles, LANE), f32)], axis=0)
    cuts = cuts[:1] + [lax.ppermute(cuts[k], "gz", [(i, i ^ k) for i in range(n_gz)]) for k in range(1, n_gz)]

    def cut_strips(cuts, boxes, name):
        return pl.pallas_call(
            functools.partial(strip_kernel, n_gx, len(cuts), rows, tiles, patches),
            out_shape=[pltpu.VMEM((strip_rows, LANE), f32)] * len(cuts),
            in_specs=[smem] * len(cuts) + [vmem],
            out_specs=[vmem] * len(cuts),
            compiler_params=limit(n_gx * rows + SUB * tiles, len(cuts) * strip_rows),
            name=name,
        )(*cuts, boxes)

    strips = cut_strips(cuts[:1], boxes, "own_strips")
    boxes, _ = lax.optimization_barrier((boxes, strips[0]))
    strips = strips + cut_strips(cuts[1:], boxes, "other_strips")

    def to_group(x, after=None):
        blocks, have = [x] + [None] * (group - 1), [0]
        masks = masks_of(group)
        for mask in masks:
            perm = [(i, i ^ mask) for i in range(group)]
            for k in have:
                block = blocks[k]
                if after is not None and mask == masks[-1] and k:
                    block, _ = lax.optimization_barrier((block, after))
                blocks[k ^ mask] = lax.ppermute(block, "gy", perm)
            have = have + [k ^ mask for k in have]
        return blocks

    raws = to_group(raw, strips[0])

    shares = [strips[0]]
    for k in range(1, n_gz * group):
        if k // n_gz % 2 == 0:
            perm = [(i, i ^ k) for i in range(n_gz * group)]
            shares.append(lax.ppermute(strips[k % n_gz], ("gy", "gz"), perm))

    made_rows = [
        sets * FIELDS * PLANE,
        sets * 10 * (FIELDS + 1) * SUB,
        sets * FIELDS * DEEP * FACES,
        sets * FIELDS * (DEEP + 1) * PX,
    ]
    made = pl.pallas_call(
        functools.partial(prepare_kernel, group, count, patches),
        out_shape=[pltpu.VMEM((n, LANE), f32) for n in made_rows],
        in_specs=[vmem] * (1 + group),
        out_specs=[vmem] * 4,
        scratch_shapes=[pltpu.VMEM((sets * AUX * PLANE, LANE), f32)],
        compiler_params=limit(*made_rows, sets * AUX * PLANE, lanes.shape[0], patches * FIELDS * SUB),
        cost_estimate=pl.CostEstimate(flops=patches * 1024 * 300, bytes_accessed=patches * 40000, transcendentals=0),
        name="prepare",
    )(lanes, *raws)

    shares = lax.optimization_barrier(shares + [made[0]])[:-1]
    row = lax.broadcasted_iota(jnp.int32, (strip_rows, LANE), 0)
    joined = jnp.where(row < FIELDS * lines, functools.reduce(jnp.add, shares), functools.reduce(jnp.maximum, shares))

    strips = [joined, lax.ppermute(joined, "gy", [(i, i ^ 1) for i in range(group)])]
    scratch_rows = [sets * FIELDS * PLANE, sets * AUX * PLANE, sets * FIELDS * DEEP * FACES] + [
        FIELDS * lines,
        4 * patches // LANE * FIELDS * PX,
        sets * FIELDS * 10 * SUB,
        sets * FIELDS * 8 * SUB,
    ]
    out = pl.pallas_call(
        functools.partial(step_kernel, count, patches, slots),
        out_shape=jax.ShapeDtypeStruct((1, 1, FIELDS, slots, SUB * LANE), f32),
        in_specs=[vmem] * 7,
        out_specs=vmem,
        scratch_shapes=[pltpu.VMEM((n, LANE), f32) for n in scratch_rows],
        compiler_params=limit(*scratch_rows, *made_rows, lanes.shape[0], 2 * strip_rows, FIELDS * slots * SUB),
        name="step",
    )(*made, lanes, *strips)
    return sides_first(out)


def solution(mesh):
    in_specs = (
        P("gx", "gz", "gy", None, None),
        P(("gx", "gz"), None, None),
        P("gx", "gz", None, None),
        P("gx", "gz", None, None),
        P("gx", "gz", None, None),
        P("gx", "gz", None, None),
    )
    out_specs = P("gx", "gz", "gy", None, None)
    return jax.shard_map(
        per_device, mesh=mesh, in_specs=in_specs, out_specs=out_specs, check_vma=False
    )
```

```python
import functools

import jax
import jax.numpy as jnp
from jax import lax
from jax.experimental import pallas as pl
from jax.experimental.pallas import tpu as pltpu
from jax.sharding import PartitionSpec as P

FIELDS = 5
PX = 32
BOX = 64
SUB = 8
LANE = 128
HALF = PX // 2
STRIDE = BOX - HALF + 1
BOX_ROWS = BOX * BOX // LANE
heat_ratio = 1.4
courant = 0.3
WEST, EAST, SOUTH, NORTH = range(4)
BLOCKS = LANE // PX
DEEP = PX // BLOCKS
SPAN = PX + 2 * SUB
PLANE = (DEEP + 2) * SPAN
FACES = PX + SUB
AUX = 2 * (FIELDS + 1)


def spot(row, column):
    return (row + 1) * SPAN + SUB + column


def power_of_two(n):
    return n & (n - 1) == 0


def masks_of(n):
    return [n >> (i + 1) for i in range(n.bit_length() - 1)]


def primitive(u):
    inverse = 1.0 / u[0]
    vx, vy, vz = u[1] * inverse, u[2] * inverse, u[3] * inverse
    kinetic = u[1] * (0.5 * vx) + u[2] * (0.5 * vy) + u[3] * (0.5 * vz)
    pressure = (heat_ratio - 1.0) * (u[4] - kinetic)
    sound = jnp.sqrt(heat_ratio * pressure * inverse)
    return vx, vy, pressure, sound


def half_flux(u, moving, pressure, sound, normal):
    half = 0.5 * moving
    flux = [u[f] * half for f in range(FIELDS)]
    flux[normal] = flux[normal] + 0.5 * pressure
    flux[4] = flux[4] + pressure * half
    return flux + [0.5 * (jnp.abs(moving) + sound)]


def face_flux(low_u, low_aux, u, aux):
    wave = jnp.maximum(low_aux[FIELDS], aux[FIELDS])
    return [low_aux[f] + aux[f] - wave * (u[f] - low_u[f]) for f in range(FIELDS)]


def lane_of():
    return lax.broadcasted_iota(jnp.int32, (SUB, LANE), 1)


def sub_of():
    return lax.broadcasted_iota(jnp.int32, (SUB, LANE), 0)


def take_lanes(x, lanes):
    return jnp.take_along_axis(x, lanes, axis=1, mode="promise_in_bounds")


def top_speed(u):
    vx, vy, _, sound = primitive(u)
    return jnp.maximum(jnp.abs(vx), jnp.abs(vy)) + sound


def make_lanes(group, count, patches, slots, around_ref, owner_ref, lanes_ref, table, slot_ref):
    me = lax.axis_index("gy")
    capacity = slots // group
    sets = patches // PX
    lane = lane_of()
    block, in_block = lane // PX, lane & (PX - 1)
    turn = me * count

    for i in range(slots):
        slot_ref[i] = -1

    def rank_source(source, carry):
        rank = jnp.int32(0)
        for i in range(count):
            p = source * count + i
            hit = owner_ref[0, 0, 0, p] == me
            slot_ref[jnp.where(hit, source * capacity + rank, slots)] = p
            rank = rank + jnp.where(hit, 1, 0)
        return carry

    lax.fori_loop(0, group, rank_source, 0)
    held = jnp.full((SUB, LANE), -1, jnp.int32)
    for j in range(slots):
        held = jnp.where(in_block == j, slot_ref[j], held)
    lanes_ref[sets * 4 * 3 * SUB :, :] = held

    table[0:4, 0:patches] = around_ref[0, 0]
    for g in range(sets):
        patch = (g * PX + in_block) ^ turn
        for side in range(4):
            near = take_lanes(jnp.broadcast_to(table[side : side + 1, :], (SUB, LANE)), patch)
            place = jnp.maximum(near, 0) ^ turn
            pick, origin = place & (PX - 1), lax.shift_right_logical(place, 5)
            lacking = jnp.where(near < 0, 1, 0)
            if side in (WEST, EAST):
                pick = pick + PX * block
            else:
                edge, step = (0, -PX) if side == SOUTH else (BLOCKS - 1, PX)
                across = pick + (LANE - PX if side == SOUTH else 0)
                pick = jnp.where(block == edge, across, lane + step)
                origin = jnp.where(block == edge, origin, g)
                lacking = jnp.where(block == edge, lacking, 0)
            for kind, x in enumerate((pick, origin, lacking)):
                at = ((g * 4 + side) * 3 + kind) * SUB
                lanes_ref[at : at + SUB, :] = x


def place_of(me, other, n):
    if power_of_two(n):
        return me ^ other
    behind = me - other
    return jnp.where(behind < 0, behind + n, behind)


def pack_kernel(tiles, rows, group, count, patches, slots, mesh_sizes, *refs):
    owner_ref, around_ref, which_ref, start_ref, patch_ref, box_ref = refs[:6]
    n_gx, n_gz = mesh_sizes
    pay_ref, raw_ref, lanes_ref = refs[6:9]
    cut_refs, (table, slot_ref) = refs[9 : 9 + n_gz], refs[9 + n_gz :]
    raw_ref[...] = patch_ref[...]
    me = lax.axis_index("gy")
    top = None
    for s in range(SUB):
        wave = top_speed([patch_ref[0, 0, f, :, s * LANE : (s + 1) * LANE] for f in range(FIELDS)])
        top = wave if top is None else jnp.maximum(top, wave)
    for f in range(FIELDS):
        pay_ref[f * tiles : (f + 1) * tiles, :] = box_ref[pl.ds(f * BOX_ROWS + me * tiles, tiles), :]
    pay_ref[rows - SUB : rows, :] = top

    start, which = start_ref[0, 0], which_ref[0, 0]
    row = lax.shift_right_logical(start * 2675, 17)
    offset = BOX * (row & 1) + start - row * STRIDE
    near = lax.shift_right_logical(row, 1) - me * tiles
    place = place_of(lax.axis_index("gx"), lax.shift_right_logical(which, n_gz.bit_length() - 1), n_gx)
    apart = (which & (n_gz - 1)) ^ lax.axis_index("gz")
    patch = lax.broadcasted_iota(jnp.int32, start.shape, 1)
    for k in range(n_gz):
        mine = (near >= 0) & (near < tiles) & (apart == k)
        cut_refs[k][0:4, 0:patches] = jnp.where(mine, place * rows + near, n_gx * rows)
        cut_refs[k][4:8, 0:patches] = (HALF * (patch & (SUB - 1)) - offset) & (LANE - 1)
    make_lanes(group, count, patches, slots, around_ref, owner_ref, lanes_ref, table, slot_ref)


def strip_kernel(parts, groups, rows, tiles, patches, *refs):
    cut_refs, pay_ref, out_refs = refs[:groups], refs[groups], refs[groups + 1 :]
    top = pay_ref[rows - SUB : rows, :]
    for k in range(1, parts):
        top = jnp.maximum(top, pay_ref[(k + 1) * rows - SUB : (k + 1) * rows, :])
    block = lane_of() // HALF
    lines = 4 * patches // SUB
    for cut_ref, out_ref in zip(cut_refs, out_refs):
        out_ref[FIELDS * lines :, :] = top
        for v in range(lines):
            side, first = v // (patches // SUB), v % (patches // SUB) * SUB
            acc = None
            for m in range(SUB):
                strip = pay_ref[pl.ds(cut_ref[side, first + m], SUB, stride=tiles), :]
                strip = pltpu.roll(strip, cut_ref[4 + side, first + m], 1)
                acc = strip if acc is None else jnp.where(block == m, strip, acc)
            out_ref[pl.ds(v, FIELDS, stride=lines), :] = acc[:FIELDS, :]


def lanes_at(lanes_ref, g, side, kind):
    at = ((g * 4 + side) * 3 + kind) * SUB
    return lanes_ref[at : at + SUB, :]


def held_at(lanes_ref, sets):
    return lanes_ref[sets * 4 * 3 * SUB : (sets * 4 * 3 + 1) * SUB, :]


def fill_ghosts(u_ref, lanes_ref, coarse_ref, sets):
    for f in range(FIELDS):
        for g in range(sets):

            def ghost(side, at, kept):
                x = None
                for o in range(sets):
                    start = (o * FIELDS + f) * PLANE + at
                    edge = pl.ds(start, DEEP, stride=SPAN) if side in (WEST, EAST) else pl.ds(start, SUB)
                    moved = take_lanes(u_ref[edge, :], lanes_at(lanes_ref, g, side, 0))
                    x = moved if x is None else jnp.where(lanes_at(lanes_ref, g, side, 1) == o, moved, x)
                if coarse_ref is None:
                    return x
                start = ((g * FIELDS + f) * 10 + kept) * SUB
                return jnp.where(lanes_at(lanes_ref, g, side, 2) != 0, coarse_ref[start : start + SUB, :], x)

            base = (g * FIELDS + f) * PLANE
            for side, column, to in ((WEST, PX - 1, -1), (EAST, 0, PX)):
                u_ref[pl.ds(base + spot(0, to), DEEP, stride=SPAN), :] = ghost(side, spot(0, column), side)
            for side, row, to in ((SOUTH, DEEP - 1, -1), (NORTH, 0, DEEP)):
                for i in range(BLOCKS):
                    kept = 2 + (side - SOUTH) * BLOCKS + i
                    u_ref[pl.ds(base + spot(to, SUB * i), SUB), :] = ghost(side, spot(row, SUB * i), kept)


def halves_of(u, axis):
    vx, vy, pressure, sound = primitive(u)
    return half_flux(u, (vx, vy)[axis], pressure, sound, axis + 1)


def fill_halves(u_ref, aux_ref, sets):
    def fill(g, rows, axes):
        u = [u_ref[rows((g * FIELDS + f) * PLANE), :] for f in range(FIELDS)]
        vx, vy, pressure, sound = primitive(u)
        for axis in axes:
            for n, x in enumerate(half_flux(u, (vx, vy)[axis], pressure, sound, axis + 1)):
                aux_ref[rows((g * AUX + axis * (FIELDS + 1) + n) * PLANE), :] = x

    for g in range(sets):

        def cells(r, carry):
            for part in range(BLOCKS):
                for i in range(BLOCKS):
                    at = spot(BLOCKS * r + part, SUB * i)
                    fill(g, lambda b, at=at: pl.ds(pl.multiple_of(b + at, SUB), SUB), (0, 1))
            return carry

        lax.fori_loop(0, DEEP // BLOCKS, cells, 0)
        for r in (-1, DEEP):
            for i in range(BLOCKS):
                fill(g, lambda b, at=spot(r, SUB * i): pl.ds(b + at, SUB), (1,))
        for c in (-1, PX):
            fill(g, lambda b, at=spot(0, c): pl.ds(b + at, DEEP, stride=SPAN), (0,))


def load_cells(u_ref, aux_ref, g, axis, rows):
    u = [u_ref[rows((g * FIELDS + f) * PLANE), :] for f in range(FIELDS)]
    start = g * AUX + axis * (FIELDS + 1)
    return u, [aux_ref[rows((start + n) * PLANE), :] for n in range(FIELDS + 1)]


def at_row(at):
    return lambda b: pl.ds(b + at, SUB)


def fill_x_faces(u_ref, aux_ref, dx_ref, g, base):
    def across(r, carry):
        for part in range(BLOCKS):
            row = BLOCKS * r + part
            for i in range(BLOCKS + 1):
                at = pl.multiple_of(spot(row, SUB * i), SUB)
                low = load_cells(u_ref, aux_ref, g, 0, at_row(at - 1))
                faces = face_flux(*low, *load_cells(u_ref, aux_ref, g, 0, at_row(at)))
                for f in range(FIELDS):
                    to = pl.multiple_of(base + (f * DEEP + row) * FACES + SUB * i, SUB)
                    dx_ref[pl.ds(to, SUB), :] = faces[f]
        return carry

    lax.fori_loop(0, DEEP // BLOCKS, across, 0)


def x_change(dx_ref, base, f, row, i):
    west = pl.multiple_of(base + (f * DEEP + row) * FACES + SUB * i, SUB)
    return dx_ref[pl.ds(west, SUB), :] - dx_ref[pl.ds(west + 1, SUB), :]


def prepare_kernel(group, count, patches, lanes_ref, *refs):
    raw_refs = refs[:group]
    u_ref, edge_ref, dx_ref, dy_ref, aux_ref = refs[group:]
    sets = patches // PX

    for f in range(FIELDS):
        for g in range(sets):
            for h in range(2):
                tiles = []
                for q in range(BLOCKS):
                    at = (q * 2 + h) * LANE
                    for k in range(PX // count):
                        tiles.append(raw_refs[g * (PX // count) + k][0, 0, f, :, at : at + LANE])
                cells = jnp.concatenate(tiles, axis=0).T
                for i in range(BLOCKS):
                    to = (g * FIELDS + f) * PLANE + spot(h * BLOCKS + i, 0)
                    u_ref[to : to + PX, :] = cells[i * PX : (i + 1) * PX, :]

    fill_ghosts(u_ref, lanes_ref, None, sets)
    fill_halves(u_ref, aux_ref, sets)
    for g in range(sets):
        fill_x_faces(u_ref, aux_ref, dx_ref, g, g * FIELDS * DEEP * FACES)

        def along(i, carry):
            low = load_cells(u_ref, aux_ref, g, 1, at_row(pl.multiple_of(spot(-1, SUB * i), SUB)))
            for r in range(DEEP + 1):
                cell = load_cells(u_ref, aux_ref, g, 1, at_row(pl.multiple_of(spot(r, SUB * i), SUB)))
                for f, face in enumerate(face_flux(*low, *cell)):
                    to = pl.multiple_of(((g * FIELDS + f) * (DEEP + 1) + r) * PX + SUB * i, SUB)
                    dy_ref[pl.ds(to, SUB), :] = face
                low = cell
            return carry

        lax.fori_loop(0, BLOCKS, along, 0)
        for side in range(4):
            for i, rows in enumerate(edge_rows(side)):
                for n in range(FIELDS + 1):
                    start = g * AUX + (0 if side in (WEST, EAST) else FIELDS + 1) + n
                    to = edge_place(g, side, i, n)
                    edge_ref[to : to + SUB, :] = aux_ref[rows(start * PLANE), :]


def edge_rows(side):
    if side in (WEST, EAST):
        at = spot(0, 0 if side == WEST else PX - 1)
        return [lambda b: pl.ds(b + at, DEEP, stride=SPAN)]
    return [at_row(spot(0 if side == SOUTH else DEEP - 1, SUB * i)) for i in range(BLOCKS)]


def edge_place(g, side, i, n):
    kept = side if side in (WEST, EAST) else 2 + (side - SOUTH) * BLOCKS + i
    return ((g * 10 + kept) * (FIELDS + 1) + n) * SUB


def step_kernel(count, patches, slots, *refs):
    u_ref, edge_ref, dx_ref, dy_ref, lanes_ref = refs[:5]
    strip_refs, out_ref = refs[5:7], refs[7]
    next_u, next_aux, next_dx, strips, doubled, coarse_ref, border_ref = refs[8:]
    lines = 4 * patches // SUB
    sets = patches // PX
    lane, sub = lane_of(), sub_of()
    block, in_block = lane // PX, lane & (PX - 1)
    turn = lax.axis_index("gy") * count

    def joined(at, join):
        return functools.reduce(join, [ref[at : at + SUB, :] for ref in strip_refs])

    for at in range(0, FIELDS * lines, SUB):
        strips[at : at + SUB, :] = joined(at, jnp.add)
    time_step = courant / jnp.max(joined(FIELDS * lines, jnp.maximum))
    part = HALF * sub + (lane & (HALF - 1))
    for t in range(4 * patches // LANE):
        tiles = []
        for v in range(t * HALF, (t + 1) * HALF):
            tile = None
            for f in range(FIELDS):
                row = jnp.broadcast_to(strips[f * lines + v : f * lines + v + 1, :], (SUB, LANE))
                wide = take_lanes(row, part)
                tile = wide if tile is None else jnp.where(lane // HALF == f, wide, tile)
            tiles.append(tile)
        cells = jnp.concatenate(tiles, axis=0).T
        for n in range(FIELDS * 2):
            for twice in range(2):
                at = t * FIELDS * PX + n * HALF + twice
                doubled[pl.ds(at, SUB, stride=2), :] = cells[n * SUB : (n + 1) * SUB, :]

    for g in range(sets):
        patch = (g * PX + in_block) ^ turn
        for side in range(4):
            t, shift = side * patches // LANE, side * patches % LANE
            for f in range(FIELDS):
                pieces = []
                for i in range(BLOCKS):
                    at = t * FIELDS * PX + f * PX + SUB * i
                    pieces.append(take_lanes(doubled[at : at + SUB, :], patch + shift))
                base = (g * FIELDS + f) * 10
                if side in (WEST, EAST):
                    x = pieces[0]
                    for q in range(1, BLOCKS):
                        x = jnp.where(block == q, pieces[q], x)
                    coarse_ref[(base + side) * SUB : (base + side + 1) * SUB, :] = x
                else:
                    for i in range(BLOCKS):
                        at = (base + 2 + (side - SOUTH) * BLOCKS + i) * SUB
                        coarse_ref[at : at + SUB, :] = pieces[i]

    size = FIELDS * DEEP * FACES
    for g in range(sets):
        for at in range(0, size, SUB):
            next_dx[g * size + at : g * size + at + SUB, :] = dx_ref[g * size + at : g * size + at + SUB, :]

        def coarse_cells(kept, axis):
            at = [((g * FIELDS + f) * 10 + kept) * SUB for f in range(FIELDS)]
            u = [coarse_ref[a : a + SUB, :] for a in at]
            return u, halves_of(u, axis)

        def own_cells(side, i):
            rows = edge_rows(side)[i]
            places = [edge_place(g, side, i, n) for n in range(FIELDS + 1)]
            u = [u_ref[rows((g * FIELDS + f) * PLANE), :] for f in range(FIELDS)]
            return u, [edge_ref[at : at + SUB, :] for at in places]

        for side, face in ((WEST, 0), (EAST, PX)):
            beyond, own = coarse_cells(side, 0), own_cells(side, 0)
            faces = face_flux(*beyond, *own) if side == WEST else face_flux(*own, *beyond)
            lacking = lanes_at(lanes_ref, g, side, 2) != 0
            for f in range(FIELDS):
                rows = pl.ds(g * size + f * DEEP * FACES + face, DEEP, stride=FACES)
                next_dx[rows, :] = jnp.where(lacking, faces[f], dx_ref[rows, :])
        for side, face in ((SOUTH, 0), (NORTH, DEEP)):
            lacking = lanes_at(lanes_ref, g, side, 2) != 0
            for i in range(BLOCKS):
                kept = (side - SOUTH) * BLOCKS + i
                beyond, own = coarse_cells(2 + kept, 1), own_cells(side, i)
                faces = face_flux(*beyond, *own) if side == SOUTH else face_flux(*own, *beyond)
                for f in range(FIELDS):
                    fine = ((g * FIELDS + f) * (DEEP + 1) + face) * PX + SUB * i
                    to = ((g * FIELDS + f) * 8 + kept) * SUB
                    border_ref[to : to + SUB, :] = jnp.where(lacking, faces[f], dy_ref[fine : fine + SUB, :])

        for f in range(FIELDS):
            for i in range(BLOCKS):
                for r in range(DEEP):
                    faces = []
                    for n in (r, r + 1):
                        if n in (0, DEEP):
                            at = ((g * FIELDS + f) * 8 + (BLOCKS if n else 0) + i) * SUB
                            faces.append(border_ref[pl.ds(pl.multiple_of(at, SUB), SUB), :])
                        else:
                            at = ((g * FIELDS + f) * (DEEP + 1) + n) * PX + SUB * i
                            faces.append(dy_ref[pl.ds(pl.multiple_of(at, SUB), SUB), :])
                    change = x_change(next_dx, g * size, f, r, i) + (faces[0] - faces[1])
                    at = pl.ds(pl.multiple_of((g * FIELDS + f) * PLANE + spot(r, SUB * i), SUB), SUB)
                    next_u[at, :] = u_ref[at, :] + time_step * change

    fill_ghosts(next_u, lanes_ref, coarse_ref, sets)
    fill_halves(next_u, next_aux, sets)
    for g in range(sets):
        fill_x_faces(next_u, next_aux, next_dx, g, g * size)

        def along(half, carry):
            for i in (2 * half, 2 * half + 1):
                low = load_cells(next_u, next_aux, g, 1, at_row(pl.multiple_of(spot(-1, SUB * i), SUB)))
                low_faces = None
                for r in range(DEEP + 1):
                    cell = load_cells(next_u, next_aux, g, 1, at_row(pl.multiple_of(spot(r, SUB * i), SUB)))
                    faces = face_flux(*low, *cell)
                    for f in range(FIELDS):
                        if r == 0:
                            continue
                        change = x_change(next_dx, g * size, f, r - 1, i) + (low_faces[f] - faces[f])
                        new = low[0][f] + time_step * change
                        at = pl.ds(pl.multiple_of((g * FIELDS + f) * PLANE + spot(r - 1, SUB * i), SUB), SUB)
                        next_u[at, :] = 0.5 * u_ref[at, :] + 0.5 * new
                    low, low_faces = cell, faces
            return carry

        lax.fori_loop(0, BLOCKS // 2, along, 0)

    held = held_at(lanes_ref, sets)
    place = jnp.maximum(held, 0) ^ turn
    pick, origin = PX * block + (place & (PX - 1)), lax.shift_right_logical(place, 5)
    for f in range(FIELDS):
        for h in range(2):
            tiles = []
            for i in range(LANE // SUB):
                at = spot(h * BLOCKS + i // BLOCKS, SUB * (i % BLOCKS))
                x = None
                for g in range(sets):
                    start = (g * FIELDS + f) * PLANE + at
                    moved = take_lanes(next_u[start : start + SUB, :], pick)
                    x = moved if x is None else jnp.where(origin == g, moved, x)
                tiles.append(jnp.where(held >= 0, x, 0.0))
            cells = jnp.concatenate(tiles, axis=0).T
            for q in range(BLOCKS):
                at = (q * 2 + h) * LANE
                out_ref[0, 0, f, :, at : at + LANE] = cells[q * PX : q * PX + slots, :]


def limit(*row_counts):
    return pltpu.CompilerParams(vmem_limit_bytes=(sum(row_counts) * LANE * 4 * 5 // 4) + (1 << 20))


def per_device(patch_state, coarse_boxes, new_owner, neighbors, coarse_box, coarse_start):
    count = patch_state.shape[2]
    n_gx, n_gz, group = lax.axis_size("gx"), lax.axis_size("gz"), lax.axis_size("gy")
    parts = n_gx * n_gz
    patches = count * group
    lines = 4 * patches // SUB
    slots = group * max(2, 2 * count // group)
    tiles = BOX_ROWS // group
    rows = -(-tiles * FIELDS // SUB) * SUB + SUB
    strip_rows = FIELDS * lines + SUB
    vmem = pl.BlockSpec(memory_space=pltpu.VMEM)
    smem = pl.BlockSpec(memory_space=pltpu.SMEM)
    f32 = jnp.float32

    def sides_first(x):
        return jnp.swapaxes(x, 2, 3)

    sets = patches // PX
    payload, raw, lanes, *cuts = pl.pallas_call(
        functools.partial(pack_kernel, tiles, rows, group, count, patches, slots, (n_gx, n_gz)),
        out_shape=(
            pltpu.VMEM((rows, LANE), f32),
            pltpu.VMEM((1, 1, FIELDS, count, SUB * LANE), f32),
            pltpu.VMEM(((sets * 4 * 3 + 1) * SUB, LANE), jnp.int32),
        )
        + (pltpu.VMEM((SUB, max(LANE, patches)), jnp.int32),) * n_gz,
        in_specs=[smem] + [vmem] * 5,
        out_specs=(vmem,) * (3 + n_gz),
        scratch_shapes=[pltpu.VMEM((SUB, LANE), jnp.int32), pltpu.SMEM((slots + 1,), jnp.int32)],
        name="pack",
    )(
        sides_first(new_owner),
        sides_first(neighbors),
        sides_first(coarse_box),
        sides_first(coarse_start),
        sides_first(patch_state),
        coarse_boxes.reshape(FIELDS * BOX_ROWS, LANE),
    )

    if power_of_two(n_gx):
        perms = [[(i, i ^ k) for i in range(n_gx)] for k in range(1, n_gx)]
    else:
        perms = [[(i, (i + k) % n_gx) for i in range(n_gx)] for k in range(1, n_gx)]
    boxes = [payload] + [lax.ppermute(payload, "gx", perm) for perm in perms]
    boxes = jnp.concatenate(boxes + [jnp.zeros((SUB * tiles, LANE), f32)], axis=0)
    cuts = cuts[:1] + [lax.ppermute(cuts[k], "gz", [(i, i ^ k) for i in range(n_gz)]) for k in range(1, n_gz)]

    strips = pl.pallas_call(
        functools.partial(strip_kernel, n_gx, n_gz, rows, tiles, patches),
        out_shape=[pltpu.VMEM((strip_rows, LANE), f32)] * n_gz,
        in_specs=[smem] * n_gz + [vmem],
        out_specs=[vmem] * n_gz,
        compiler_params=limit(n_gx * rows + SUB * tiles, n_gz * strip_rows),
        name="strips",
    )(*cuts, boxes)

    def to_group(x, after=None):
        blocks, have = [x] + [None] * (group - 1), [0]
        masks = masks_of(group)
        for mask in masks:
            perm = [(i, i ^ mask) for i in range(group)]
            for k in have:
                block = blocks[k]
                if after is not None and mask == masks[-1] and k:
                    block, _ = lax.optimization_barrier((block, after))
                blocks[k ^ mask] = lax.ppermute(block, "gy", perm)
            have = have + [k ^ mask for k in have]
        return blocks

    raws = to_group(raw, strips[0])

    shares = [strips[0]]
    for k in reversed(range(1, n_gz * group)):
        if k // n_gz % 2 == 0:
            perm = [(i, i ^ k) for i in range(n_gz * group)]
            shares.append(lax.ppermute(strips[k % n_gz], ("gy", "gz"), perm))

    made_rows = [
        sets * FIELDS * PLANE,
        sets * 10 * (FIELDS + 1) * SUB,
        sets * FIELDS * DEEP * FACES,
        sets * FIELDS * (DEEP + 1) * PX,
    ]
    made = pl.pallas_call(
        functools.partial(prepare_kernel, group, count, patches),
        out_shape=[pltpu.VMEM((n, LANE), f32) for n in made_rows],
        in_specs=[vmem] * (1 + group),
        out_specs=[vmem] * 4,
        scratch_shapes=[pltpu.VMEM((sets * AUX * PLANE, LANE), f32)],
        compiler_params=limit(*made_rows, sets * AUX * PLANE, lanes.shape[0], patches * FIELDS * SUB),
        cost_estimate=pl.CostEstimate(flops=patches * 1024 * 300, bytes_accessed=patches * 40000, transcendentals=0),
        name="prepare",
    )(lanes, *raws)

    shares = lax.optimization_barrier(shares + [made[0]])[:-1]
    row = lax.broadcasted_iota(jnp.int32, (strip_rows, LANE), 0)
    joined = jnp.where(row < FIELDS * lines, functools.reduce(jnp.add, shares), functools.reduce(jnp.maximum, shares))

    strips = [joined, lax.ppermute(joined, "gy", [(i, i ^ 1) for i in range(group)])]
    scratch_rows = [sets * FIELDS * PLANE, sets * AUX * PLANE, sets * FIELDS * DEEP * FACES] + [
        FIELDS * lines,
        4 * patches // LANE * FIELDS * PX,
        sets * FIELDS * 10 * SUB,
        sets * FIELDS * 8 * SUB,
    ]
    out = pl.pallas_call(
        functools.partial(step_kernel, count, patches, slots),
        out_shape=jax.ShapeDtypeStruct((1, 1, FIELDS, slots, SUB * LANE), f32),
        in_specs=[vmem] * 7,
        out_specs=vmem,
        scratch_shapes=[pltpu.VMEM((n, LANE), f32) for n in scratch_rows],
        compiler_params=limit(*scratch_rows, *made_rows, lanes.shape[0], 2 * strip_rows, FIELDS * slots * SUB),
        name="step",
    )(*made, lanes, *strips)
    return sides_first(out)


def solution(mesh):
    in_specs = (
        P("gx", "gz", "gy", None, None),
        P(("gx", "gz"), None, None),
        P("gx", "gz", None, None),
        P("gx", "gz", None, None),
        P("gx", "gz", None, None),
        P("gx", "gz", None, None),
    )
    out_specs = P("gx", "gz", "gy", None, None)
    return jax.shard_map(
        per_device, mesh=mesh, in_specs=in_specs, out_specs=out_specs, check_vma=False
    )
```

```python
import functools

import jax
import jax.numpy as jnp
from jax import lax
from jax.experimental import pallas as pl
from jax.experimental.pallas import tpu as pltpu
from jax.sharding import PartitionSpec as P

FIELDS = 5
PX = 32
BOX = 64
SUB = 8
LANE = 128
HALF = PX // 2
STRIDE = BOX - HALF + 1
BOX_ROWS = BOX * BOX // LANE
heat_ratio = 1.4
courant = 0.3
WEST, EAST, SOUTH, NORTH = range(4)
BLOCKS = LANE // PX
DEEP = PX // BLOCKS
SPAN = PX + 2 * SUB
PLANE = (DEEP + 2) * SPAN
FACES = PX + SUB
AUX = 2 * (FIELDS + 1)


def spot(row, column):
    return (row + 1) * SPAN + SUB + column


def power_of_two(n):
    return n & (n - 1) == 0


def masks_of(n):
    return [n >> (i + 1) for i in range(n.bit_length() - 1)]


def primitive(u):
    inverse = 1.0 / u[0]
    vx, vy, vz = u[1] * inverse, u[2] * inverse, u[3] * inverse
    kinetic = u[1] * (0.5 * vx) + u[2] * (0.5 * vy) + u[3] * (0.5 * vz)
    pressure = (heat_ratio - 1.0) * (u[4] - kinetic)
    sound = jnp.sqrt(heat_ratio * pressure * inverse)
    return vx, vy, pressure, sound


def half_flux(u, moving, pressure, sound, normal):
    half = 0.5 * moving
    flux = [u[f] * half for f in range(FIELDS)]
    flux[normal] = flux[normal] + 0.5 * pressure
    flux[4] = flux[4] + pressure * half
    return flux + [0.5 * (jnp.abs(moving) + sound)]


def face_flux(low_u, low_aux, u, aux):
    wave = jnp.maximum(low_aux[FIELDS], aux[FIELDS])
    return [low_aux[f] + aux[f] - wave * (u[f] - low_u[f]) for f in range(FIELDS)]


def lane_of():
    return lax.broadcasted_iota(jnp.int32, (SUB, LANE), 1)


def sub_of():
    return lax.broadcasted_iota(jnp.int32, (SUB, LANE), 0)


def take_lanes(x, lanes):
    return jnp.take_along_axis(x, lanes, axis=1, mode="promise_in_bounds")


def top_speed(u):
    vx, vy, _, sound = primitive(u)
    return jnp.maximum(jnp.abs(vx), jnp.abs(vy)) + sound


def make_lanes(group, count, patches, slots, around_ref, owner_ref, lanes_ref, table, slot_ref):
    me = lax.axis_index("gy")
    capacity = slots // group
    sets = patches // PX
    lane = lane_of()
    block, in_block = lane // PX, lane & (PX - 1)
    turn = me * count

    for i in range(slots):
        slot_ref[i] = -1

    def rank_source(source, carry):
        rank = jnp.int32(0)
        for i in range(count):
            p = source * count + i
            hit = owner_ref[0, 0, 0, p] == me
            slot_ref[jnp.where(hit, source * capacity + rank, slots)] = p
            rank = rank + jnp.where(hit, 1, 0)
        return carry

    lax.fori_loop(0, group, rank_source, 0)
    held = jnp.full((SUB, LANE), -1, jnp.int32)
    for j in range(slots):
        held = jnp.where(in_block == j, slot_ref[j], held)
    lanes_ref[sets * 4 * 3 * SUB :, :] = held

    table[0:4, 0:patches] = around_ref[0, 0]
    for g in range(sets):
        patch = (g * PX + in_block) ^ turn
        for side in range(4):
            near = take_lanes(jnp.broadcast_to(table[side : side + 1, :], (SUB, LANE)), patch)
            place = jnp.maximum(near, 0) ^ turn
            pick, origin = place & (PX - 1), lax.shift_right_logical(place, 5)
            lacking = jnp.where(near < 0, 1, 0)
            if side in (WEST, EAST):
                pick = pick + PX * block
            else:
                edge, step = (0, -PX) if side == SOUTH else (BLOCKS - 1, PX)
                across = pick + (LANE - PX if side == SOUTH else 0)
                pick = jnp.where(block == edge, across, lane + step)
                origin = jnp.where(block == edge, origin, g)
                lacking = jnp.where(block == edge, lacking, 0)
            for kind, x in enumerate((pick, origin, lacking)):
                at = ((g * 4 + side) * 3 + kind) * SUB
                lanes_ref[at : at + SUB, :] = x


def place_of(me, other, n):
    if power_of_two(n):
        apart = me ^ other
        return jnp.where(apart == 0, 0, n - apart)
    ahead = other - me
    return jnp.where(ahead < 0, ahead + n, ahead)


def pack_kernel(tiles, rows, group, count, patches, slots, mesh_sizes, *refs):
    owner_ref, around_ref, which_ref, start_ref, patch_ref, box_ref = refs[:6]
    n_gx, n_gz = mesh_sizes
    pay_ref, raw_ref, lanes_ref = refs[6:9]
    cut_refs, (table, slot_ref) = refs[9 : 9 + n_gz], refs[9 + n_gz :]
    raw_ref[...] = patch_ref[...]
    me = lax.axis_index("gy")
    top = None
    for s in range(SUB):
        wave = top_speed([patch_ref[0, 0, f, :, s * LANE : (s + 1) * LANE] for f in range(FIELDS)])
        top = wave if top is None else jnp.maximum(top, wave)
    for f in range(FIELDS):
        pay_ref[f * tiles : (f + 1) * tiles, :] = box_ref[pl.ds(f * BOX_ROWS + me * tiles, tiles), :]
    pay_ref[rows - SUB : rows, :] = top

    start, which = start_ref[0, 0], which_ref[0, 0]
    row = lax.shift_right_logical(start * 2675, 17)
    offset = BOX * (row & 1) + start - row * STRIDE
    near = lax.shift_right_logical(row, 1) - me * tiles
    place = place_of(lax.axis_index("gx"), lax.shift_right_logical(which, n_gz.bit_length() - 1), n_gx)
    apart = (which & (n_gz - 1)) ^ lax.axis_index("gz")
    patch = lax.broadcasted_iota(jnp.int32, start.shape, 1)
    for k in range(n_gz):
        mine = (near >= 0) & (near < tiles) & (apart == k)
        cut_refs[k][0:4, 0:patches] = jnp.where(mine, place * rows + near, n_gx * rows)
        cut_refs[k][4:8, 0:patches] = (HALF * (patch & (SUB - 1)) - offset) & (LANE - 1)
    make_lanes(group, count, patches, slots, around_ref, owner_ref, lanes_ref, table, slot_ref)


def strip_kernel(parts, groups, rows, tiles, patches, *refs):
    cut_refs, pay_ref, out_refs = refs[:groups], refs[groups], refs[groups + 1 :]
    top = pay_ref[rows - SUB : rows, :]
    for k in range(1, parts):
        top = jnp.maximum(top, pay_ref[(k + 1) * rows - SUB : (k + 1) * rows, :])
    block = lane_of() // HALF
    lines = 4 * patches // SUB
    for cut_ref, out_ref in zip(cut_refs, out_refs):
        out_ref[FIELDS * lines :, :] = top
        for v in range(lines):
            side, first = v // (patches // SUB), v % (patches // SUB) * SUB
            acc = None
            for m in range(SUB):
                strip = pay_ref[pl.ds(cut_ref[side, first + m], SUB, stride=tiles), :]
                strip = pltpu.roll(strip, cut_ref[4 + side, first + m], 1)
                acc = strip if acc is None else jnp.where(block == m, strip, acc)
            out_ref[pl.ds(v, FIELDS, stride=lines), :] = acc[:FIELDS, :]


def lanes_at(lanes_ref, g, side, kind):
    at = ((g * 4 + side) * 3 + kind) * SUB
    return lanes_ref[at : at + SUB, :]


def held_at(lanes_ref, sets):
    return lanes_ref[sets * 4 * 3 * SUB : (sets * 4 * 3 + 1) * SUB, :]


def fill_ghosts(u_ref, lanes_ref, coarse_ref, sets):
    for f in range(FIELDS):
        for g in range(sets):

            def ghost(side, at, kept):
                x = None
                for o in range(sets):
                    start = (o * FIELDS + f) * PLANE + at
                    edge = pl.ds(start, DEEP, stride=SPAN) if side in (WEST, EAST) else pl.ds(start, SUB)
                    moved = take_lanes(u_ref[edge, :], lanes_at(lanes_ref, g, side, 0))
                    x = moved if x is None else jnp.where(lanes_at(lanes_ref, g, side, 1) == o, moved, x)
                if coarse_ref is None:
                    return x
                start = ((g * FIELDS + f) * 10 + kept) * SUB
                return jnp.where(lanes_at(lanes_ref, g, side, 2) != 0, coarse_ref[start : start + SUB, :], x)

            base = (g * FIELDS + f) * PLANE
            for side, column, to in ((WEST, PX - 1, -1), (EAST, 0, PX)):
                u_ref[pl.ds(base + spot(0, to), DEEP, stride=SPAN), :] = ghost(side, spot(0, column), side)
            for side, row, to in ((SOUTH, DEEP - 1, -1), (NORTH, 0, DEEP)):
                for i in range(BLOCKS):
                    kept = 2 + (side - SOUTH) * BLOCKS + i
                    u_ref[pl.ds(base + spot(to, SUB * i), SUB), :] = ghost(side, spot(row, SUB * i), kept)


def halves_of(u, axis):
    vx, vy, pressure, sound = primitive(u)
    return half_flux(u, (vx, vy)[axis], pressure, sound, axis + 1)


def fill_halves(u_ref, aux_ref, sets):
    def fill(g, rows, axes):
        u = [u_ref[rows((g * FIELDS + f) * PLANE), :] for f in range(FIELDS)]
        vx, vy, pressure, sound = primitive(u)
        for axis in axes:
            for n, x in enumerate(half_flux(u, (vx, vy)[axis], pressure, sound, axis + 1)):
                aux_ref[rows((g * AUX + axis * (FIELDS + 1) + n) * PLANE), :] = x

    for g in range(sets):

        def cells(r, carry):
            for part in range(BLOCKS):
                for i in range(BLOCKS):
                    at = spot(BLOCKS * r + part, SUB * i)
                    fill(g, lambda b, at=at: pl.ds(pl.multiple_of(b + at, SUB), SUB), (0, 1))
            return carry

        lax.fori_loop(0, DEEP // BLOCKS, cells, 0)
        for r in (-1, DEEP):
            for i in range(BLOCKS):
                fill(g, lambda b, at=spot(r, SUB * i): pl.ds(b + at, SUB), (1,))
        for c in (-1, PX):
            fill(g, lambda b, at=spot(0, c): pl.ds(b + at, DEEP, stride=SPAN), (0,))


def load_cells(u_ref, aux_ref, g, axis, rows):
    u = [u_ref[rows((g * FIELDS + f) * PLANE), :] for f in range(FIELDS)]
    start = g * AUX + axis * (FIELDS + 1)
    return u, [aux_ref[rows((start + n) * PLANE), :] for n in range(FIELDS + 1)]


def at_row(at):
    return lambda b: pl.ds(b + at, SUB)


def fill_x_faces(u_ref, aux_ref, dx_ref, g, base):
    def across(r, carry):
        for part in range(BLOCKS):
            row = BLOCKS * r + part
            for i in range(BLOCKS + 1):
                at = pl.multiple_of(spot(row, SUB * i), SUB)
                low = load_cells(u_ref, aux_ref, g, 0, at_row(at - 1))
                faces = face_flux(*low, *load_cells(u_ref, aux_ref, g, 0, at_row(at)))
                for f in range(FIELDS):
                    to = pl.multiple_of(base + (f * DEEP + row) * FACES + SUB * i, SUB)
                    dx_ref[pl.ds(to, SUB), :] = faces[f]
        return carry

    lax.fori_loop(0, DEEP // BLOCKS, across, 0)


def x_change(dx_ref, base, f, row, i):
    west = pl.multiple_of(base + (f * DEEP + row) * FACES + SUB * i, SUB)
    return dx_ref[pl.ds(west, SUB), :] - dx_ref[pl.ds(west + 1, SUB), :]


def prepare_kernel(group, count, patches, lanes_ref, *refs):
    raw_refs = refs[:group]
    u_ref, edge_ref, dx_ref, dy_ref, aux_ref = refs[group:]
    sets = patches // PX

    for f in range(FIELDS):
        for g in range(sets):
            for h in range(2):
                tiles = []
                for q in range(BLOCKS):
                    at = (q * 2 + h) * LANE
                    for k in range(PX // count):
                        tiles.append(raw_refs[g * (PX // count) + k][0, 0, f, :, at : at + LANE])
                cells = jnp.concatenate(tiles, axis=0).T
                for i in range(BLOCKS):
                    to = (g * FIELDS + f) * PLANE + spot(h * BLOCKS + i, 0)
                    u_ref[to : to + PX, :] = cells[i * PX : (i + 1) * PX, :]

    fill_ghosts(u_ref, lanes_ref, None, sets)
    fill_halves(u_ref, aux_ref, sets)
    for g in range(sets):
        fill_x_faces(u_ref, aux_ref, dx_ref, g, g * FIELDS * DEEP * FACES)

        def along(i, carry):
            low = load_cells(u_ref, aux_ref, g, 1, at_row(pl.multiple_of(spot(-1, SUB * i), SUB)))
            for r in range(DEEP + 1):
                cell = load_cells(u_ref, aux_ref, g, 1, at_row(pl.multiple_of(spot(r, SUB * i), SUB)))
                for f, face in enumerate(face_flux(*low, *cell)):
                    to = pl.multiple_of(((g * FIELDS + f) * (DEEP + 1) + r) * PX + SUB * i, SUB)
                    dy_ref[pl.ds(to, SUB), :] = face
                low = cell
            return carry

        lax.fori_loop(0, BLOCKS, along, 0)
        for side in range(4):
            for i, rows in enumerate(edge_rows(side)):
                for n in range(FIELDS + 1):
                    start = g * AUX + (0 if side in (WEST, EAST) else FIELDS + 1) + n
                    to = edge_place(g, side, i, n)
                    edge_ref[to : to + SUB, :] = aux_ref[rows(start * PLANE), :]


def edge_rows(side):
    if side in (WEST, EAST):
        at = spot(0, 0 if side == WEST else PX - 1)
        return [lambda b: pl.ds(b + at, DEEP, stride=SPAN)]
    return [at_row(spot(0 if side == SOUTH else DEEP - 1, SUB * i)) for i in range(BLOCKS)]


def edge_place(g, side, i, n):
    kept = side if side in (WEST, EAST) else 2 + (side - SOUTH) * BLOCKS + i
    return ((g * 10 + kept) * (FIELDS + 1) + n) * SUB


def step_kernel(count, patches, slots, *refs):
    u_ref, edge_ref, dx_ref, dy_ref, lanes_ref = refs[:5]
    strip_refs, out_ref = refs[5:7], refs[7]
    next_u, next_aux, next_dx, strips, doubled, coarse_ref, border_ref = refs[8:]
    lines = 4 * patches // SUB
    sets = patches // PX
    lane, sub = lane_of(), sub_of()
    block, in_block = lane // PX, lane & (PX - 1)
    turn = lax.axis_index("gy") * count

    def joined(at, join):
        return functools.reduce(join, [ref[at : at + SUB, :] for ref in strip_refs])

    for at in range(0, FIELDS * lines, SUB):
        strips[at : at + SUB, :] = joined(at, jnp.add)
    time_step = courant / jnp.max(joined(FIELDS * lines, jnp.maximum))
    part = HALF * sub + (lane & (HALF - 1))
    for t in range(4 * patches // LANE):
        tiles = []
        for v in range(t * HALF, (t + 1) * HALF):
            tile = None
            for f in range(FIELDS):
                row = jnp.broadcast_to(strips[f * lines + v : f * lines + v + 1, :], (SUB, LANE))
                wide = take_lanes(row, part)
                tile = wide if tile is None else jnp.where(lane // HALF == f, wide, tile)
            tiles.append(tile)
        cells = jnp.concatenate(tiles, axis=0).T
        for n in range(FIELDS * 2):
            for twice in range(2):
                at = t * FIELDS * PX + n * HALF + twice
                doubled[pl.ds(at, SUB, stride=2), :] = cells[n * SUB : (n + 1) * SUB, :]

    for g in range(sets):
        patch = (g * PX + in_block) ^ turn
        for side in range(4):
            t, shift = side * patches // LANE, side * patches % LANE
            for f in range(FIELDS):
                pieces = []
                for i in range(BLOCKS):
                    at = t * FIELDS * PX + f * PX + SUB * i
                    pieces.append(take_lanes(doubled[at : at + SUB, :], patch + shift))
                base = (g * FIELDS + f) * 10
                if side in (WEST, EAST):
                    x = pieces[0]
                    for q in range(1, BLOCKS):
                        x = jnp.where(block == q, pieces[q], x)
                    coarse_ref[(base + side) * SUB : (base + side + 1) * SUB, :] = x
                else:
                    for i in range(BLOCKS):
                        at = (base + 2 + (side - SOUTH) * BLOCKS + i) * SUB
                        coarse_ref[at : at + SUB, :] = pieces[i]

    size = FIELDS * DEEP * FACES
    for g in range(sets):
        for at in range(0, size, SUB):
            next_dx[g * size + at : g * size + at + SUB, :] = dx_ref[g * size + at : g * size + at + SUB, :]

        def coarse_cells(kept, axis):
            at = [((g * FIELDS + f) * 10 + kept) * SUB for f in range(FIELDS)]
            u = [coarse_ref[a : a + SUB, :] for a in at]
            return u, halves_of(u, axis)

        def own_cells(side, i):
            rows = edge_rows(side)[i]
            places = [edge_place(g, side, i, n) for n in range(FIELDS + 1)]
            u = [u_ref[rows((g * FIELDS + f) * PLANE), :] for f in range(FIELDS)]
            return u, [edge_ref[at : at + SUB, :] for at in places]

        for side, face in ((WEST, 0), (EAST, PX)):
            beyond, own = coarse_cells(side, 0), own_cells(side, 0)
            faces = face_flux(*beyond, *own) if side == WEST else face_flux(*own, *beyond)
            lacking = lanes_at(lanes_ref, g, side, 2) != 0
            for f in range(FIELDS):
                rows = pl.ds(g * size + f * DEEP * FACES + face, DEEP, stride=FACES)
                next_dx[rows, :] = jnp.where(lacking, faces[f], dx_ref[rows, :])
        for side, face in ((SOUTH, 0), (NORTH, DEEP)):
            lacking = lanes_at(lanes_ref, g, side, 2) != 0
            for i in range(BLOCKS):
                kept = (side - SOUTH) * BLOCKS + i
                beyond, own = coarse_cells(2 + kept, 1), own_cells(side, i)
                faces = face_flux(*beyond, *own) if side == SOUTH else face_flux(*own, *beyond)
                for f in range(FIELDS):
                    fine = ((g * FIELDS + f) * (DEEP + 1) + face) * PX + SUB * i
                    to = ((g * FIELDS + f) * 8 + kept) * SUB
                    border_ref[to : to + SUB, :] = jnp.where(lacking, faces[f], dy_ref[fine : fine + SUB, :])

        for f in range(FIELDS):
            for i in range(BLOCKS):
                for r in range(DEEP):
                    faces = []
                    for n in (r, r + 1):
                        if n in (0, DEEP):
                            at = ((g * FIELDS + f) * 8 + (BLOCKS if n else 0) + i) * SUB
                            faces.append(border_ref[pl.ds(pl.multiple_of(at, SUB), SUB), :])
                        else:
                            at = ((g * FIELDS + f) * (DEEP + 1) + n) * PX + SUB * i
                            faces.append(dy_ref[pl.ds(pl.multiple_of(at, SUB), SUB), :])
                    change = x_change(next_dx, g * size, f, r, i) + (faces[0] - faces[1])
                    at = pl.ds(pl.multiple_of((g * FIELDS + f) * PLANE + spot(r, SUB * i), SUB), SUB)
                    next_u[at, :] = u_ref[at, :] + time_step * change

    fill_ghosts(next_u, lanes_ref, coarse_ref, sets)
    fill_halves(next_u, next_aux, sets)
    for g in range(sets):
        fill_x_faces(next_u, next_aux, next_dx, g, g * size)

        def along(half, carry):
            for i in (2 * half, 2 * half + 1):
                low = load_cells(next_u, next_aux, g, 1, at_row(pl.multiple_of(spot(-1, SUB * i), SUB)))
                low_faces = None
                for r in range(DEEP + 1):
                    cell = load_cells(next_u, next_aux, g, 1, at_row(pl.multiple_of(spot(r, SUB * i), SUB)))
                    faces = face_flux(*low, *cell)
                    for f in range(FIELDS):
                        if r == 0:
                            continue
                        change = x_change(next_dx, g * size, f, r - 1, i) + (low_faces[f] - faces[f])
                        new = low[0][f] + time_step * change
                        at = pl.ds(pl.multiple_of((g * FIELDS + f) * PLANE + spot(r - 1, SUB * i), SUB), SUB)
                        next_u[at, :] = 0.5 * u_ref[at, :] + 0.5 * new
                    low, low_faces = cell, faces
            return carry

        lax.fori_loop(0, BLOCKS // 2, along, 0)

    held = held_at(lanes_ref, sets)
    place = jnp.maximum(held, 0) ^ turn
    pick, origin = PX * block + (place & (PX - 1)), lax.shift_right_logical(place, 5)
    for f in range(FIELDS):
        for h in range(2):
            tiles = []
            for i in range(LANE // SUB):
                at = spot(h * BLOCKS + i // BLOCKS, SUB * (i % BLOCKS))
                x = None
                for g in range(sets):
                    start = (g * FIELDS + f) * PLANE + at
                    moved = take_lanes(next_u[start : start + SUB, :], pick)
                    x = moved if x is None else jnp.where(origin == g, moved, x)
                tiles.append(jnp.where(held >= 0, x, 0.0))
            cells = jnp.concatenate(tiles, axis=0).T
            for q in range(BLOCKS):
                at = (q * 2 + h) * LANE
                out_ref[0, 0, f, :, at : at + LANE] = cells[q * PX : q * PX + slots, :]


def limit(*row_counts):
    return pltpu.CompilerParams(vmem_limit_bytes=(sum(row_counts) * LANE * 4 * 5 // 4) + (1 << 20))


def per_device(patch_state, coarse_boxes, new_owner, neighbors, coarse_box, coarse_start):
    count = patch_state.shape[2]
    n_gx, n_gz, group = lax.axis_size("gx"), lax.axis_size("gz"), lax.axis_size("gy")
    parts = n_gx * n_gz
    patches = count * group
    lines = 4 * patches // SUB
    slots = group * max(2, 2 * count // group)
    tiles = BOX_ROWS // group
    rows = -(-tiles * FIELDS // SUB) * SUB + SUB
    strip_rows = FIELDS * lines + SUB
    vmem = pl.BlockSpec(memory_space=pltpu.VMEM)
    smem = pl.BlockSpec(memory_space=pltpu.SMEM)
    f32 = jnp.float32

    def sides_first(x):
        return jnp.swapaxes(x, 2, 3)

    sets = patches // PX
    payload, raw, lanes, *cuts = pl.pallas_call(
        functools.partial(pack_kernel, tiles, rows, group, count, patches, slots, (n_gx, n_gz)),
        out_shape=(
            pltpu.VMEM((rows, LANE), f32),
            pltpu.VMEM((1, 1, FIELDS, count, SUB * LANE), f32),
            pltpu.VMEM(((sets * 4 * 3 + 1) * SUB, LANE), jnp.int32),
        )
        + (pltpu.VMEM((SUB, max(LANE, patches)), jnp.int32),) * n_gz,
        in_specs=[smem] + [vmem] * 5,
        out_specs=(vmem,) * (3 + n_gz),
        scratch_shapes=[pltpu.VMEM((SUB, LANE), jnp.int32), pltpu.SMEM((slots + 1,), jnp.int32)],
        name="pack",
    )(
        sides_first(new_owner),
        sides_first(neighbors),
        sides_first(coarse_box),
        sides_first(coarse_start),
        sides_first(patch_state),
        coarse_boxes.reshape(FIELDS * BOX_ROWS, LANE),
    )

    if power_of_two(n_gx):
        perms = [[(i, i ^ k) for i in range(n_gx)] for k in range(1, n_gx)]
    else:
        perms = [[(i, (i + k) % n_gx) for i in range(n_gx)] for k in range(1, n_gx)]
    boxes = [payload] + [lax.ppermute(payload, "gx", perm) for perm in perms[::-1]]
    cuts = cuts[:1] + [lax.ppermute(cuts[k], "gz", [(i, i ^ k) for i in range(n_gz)]) for k in range(1, n_gz)]
    *boxes, last = lax.optimization_barrier(boxes + cuts[1:2])
    cuts = cuts[:1] + [last] + cuts[2:]
    boxes = jnp.concatenate(boxes + [jnp.zeros((SUB * tiles, LANE), f32)], axis=0)

    strips = pl.pallas_call(
        functools.partial(strip_kernel, n_gx, n_gz, rows, tiles, patches),
        out_shape=[pltpu.VMEM((strip_rows, LANE), f32)] * n_gz,
        in_specs=[smem] * n_gz + [vmem],
        out_specs=[vmem] * n_gz,
        compiler_params=limit(n_gx * rows + SUB * tiles, n_gz * strip_rows),
        name="strips",
    )(*cuts, boxes)

    def to_group(x, after=None):
        blocks, have = [x] + [None] * (group - 1), [0]
        masks = masks_of(group)
        for mask in masks:
            perm = [(i, i ^ mask) for i in range(group)]
            for k in have:
                block = blocks[k]
                if after is not None and mask == masks[-1] and k:
                    block, _ = lax.optimization_barrier((block, after))
                blocks[k ^ mask] = lax.ppermute(block, "gy", perm)
            have = have + [k ^ mask for k in have]
        return blocks

    raws = to_group(raw, strips[0])

    shares = [strips[0]]
    for k in reversed(range(1, n_gz * group)):
        if k // n_gz % 2 == 0:
            perm = [(i, i ^ k) for i in range(n_gz * group)]
            shares.append(lax.ppermute(strips[k % n_gz], ("gy", "gz"), perm))

    made_rows = [
        sets * FIELDS * PLANE,
        sets * 10 * (FIELDS + 1) * SUB,
        sets * FIELDS * DEEP * FACES,
        sets * FIELDS * (DEEP + 1) * PX,
    ]
    made = pl.pallas_call(
        functools.partial(prepare_kernel, group, count, patches),
        out_shape=[pltpu.VMEM((n, LANE), f32) for n in made_rows],
        in_specs=[vmem] * (1 + group),
        out_specs=[vmem] * 4,
        scratch_shapes=[pltpu.VMEM((sets * AUX * PLANE, LANE), f32)],
        compiler_params=limit(*made_rows, sets * AUX * PLANE, lanes.shape[0], patches * FIELDS * SUB),
        cost_estimate=pl.CostEstimate(flops=patches * 1024 * 300, bytes_accessed=patches * 40000, transcendentals=0),
        name="prepare",
    )(lanes, *raws)

    shares = lax.optimization_barrier(shares + [made[0]])[:-1]
    row = lax.broadcasted_iota(jnp.int32, (strip_rows, LANE), 0)
    joined = jnp.where(row < FIELDS * lines, functools.reduce(jnp.add, shares), functools.reduce(jnp.maximum, shares))

    strips = [joined, lax.ppermute(joined, "gy", [(i, i ^ 1) for i in range(group)])]
    scratch_rows = [sets * FIELDS * PLANE, sets * AUX * PLANE, sets * FIELDS * DEEP * FACES] + [
        FIELDS * lines,
        4 * patches // LANE * FIELDS * PX,
        sets * FIELDS * 10 * SUB,
        sets * FIELDS * 8 * SUB,
    ]
    out = pl.pallas_call(
        functools.partial(step_kernel, count, patches, slots),
        out_shape=jax.ShapeDtypeStruct((1, 1, FIELDS, slots, SUB * LANE), f32),
        in_specs=[vmem] * 7,
        out_specs=vmem,
        scratch_shapes=[pltpu.VMEM((n, LANE), f32) for n in scratch_rows],
        compiler_params=limit(*scratch_rows, *made_rows, lanes.shape[0], 2 * strip_rows, FIELDS * slots * SUB),
        name="step",
    )(*made, lanes, *strips)
    return sides_first(out)


def solution(mesh):
    in_specs = (
        P("gx", "gz", "gy", None, None),
        P(("gx", "gz"), None, None),
        P("gx", "gz", None, None),
        P("gx", "gz", None, None),
        P("gx", "gz", None, None),
        P("gx", "gz", None, None),
    )
    out_specs = P("gx", "gz", "gy", None, None)
    return jax.shard_map(
        per_device, mesh=mesh, in_specs=in_specs, out_specs=out_specs, check_vma=False
    )
```

```python
import functools

import jax
import jax.numpy as jnp
from jax import lax
from jax.experimental import pallas as pl
from jax.experimental.pallas import tpu as pltpu
from jax.sharding import PartitionSpec as P

FIELDS = 5
PX = 32
BOX = 64
SUB = 8
LANE = 128
HALF = PX // 2
STRIDE = BOX - HALF + 1
BOX_ROWS = BOX * BOX // LANE
heat_ratio = 1.4
courant = 0.3
WEST, EAST, SOUTH, NORTH = range(4)
BLOCKS = LANE // PX
DEEP = PX // BLOCKS
SPAN = PX + 2 * SUB
PLANE = (DEEP + 2) * SPAN
FACES = PX + SUB
AUX = 2 * (FIELDS + 1)


def spot(row, column):
    return (row + 1) * SPAN + SUB + column


def power_of_two(n):
    return n & (n - 1) == 0


def masks_of(n):
    return [n >> (i + 1) for i in range(n.bit_length() - 1)]


def primitive(u):
    inverse = 1.0 / u[0]
    vx, vy, vz = u[1] * inverse, u[2] * inverse, u[3] * inverse
    kinetic = u[1] * (0.5 * vx) + u[2] * (0.5 * vy) + u[3] * (0.5 * vz)
    pressure = (heat_ratio - 1.0) * (u[4] - kinetic)
    sound = jnp.sqrt(heat_ratio * pressure * inverse)
    return vx, vy, pressure, sound


def half_flux(u, moving, pressure, sound, normal):
    half = 0.5 * moving
    flux = [u[f] * half for f in range(FIELDS)]
    flux[normal] = flux[normal] + 0.5 * pressure
    flux[4] = flux[4] + pressure * half
    return flux + [0.5 * (jnp.abs(moving) + sound)]


def face_flux(low_u, low_aux, u, aux):
    wave = jnp.maximum(low_aux[FIELDS], aux[FIELDS])
    return [low_aux[f] + aux[f] - wave * (u[f] - low_u[f]) for f in range(FIELDS)]


def lane_of():
    return lax.broadcasted_iota(jnp.int32, (SUB, LANE), 1)


def sub_of():
    return lax.broadcasted_iota(jnp.int32, (SUB, LANE), 0)


def take_lanes(x, lanes):
    return jnp.take_along_axis(x, lanes, axis=1, mode="promise_in_bounds")


def top_speed(u):
    vx, vy, _, sound = primitive(u)
    return jnp.maximum(jnp.abs(vx), jnp.abs(vy)) + sound


def make_lanes(group, count, patches, slots, around_ref, owner_ref, lanes_ref, table, slot_ref):
    me = lax.axis_index("gy")
    capacity = slots // group
    sets = patches // PX
    lane = lane_of()
    block, in_block = lane // PX, lane & (PX - 1)
    turn = me * count

    for i in range(slots):
        slot_ref[i] = -1

    def rank_source(source, carry):
        rank = jnp.int32(0)
        for i in range(count):
            p = source * count + i
            hit = owner_ref[0, 0, 0, p] == me
            slot_ref[jnp.where(hit, source * capacity + rank, slots)] = p
            rank = rank + jnp.where(hit, 1, 0)
        return carry

    lax.fori_loop(0, group, rank_source, 0)
    held = jnp.full((SUB, LANE), -1, jnp.int32)
    for j in range(slots):
        held = jnp.where(in_block == j, slot_ref[j], held)
    lanes_ref[sets * 4 * 3 * SUB :, :] = held

    table[0:4, 0:patches] = around_ref[0, 0]
    for g in range(sets):
        patch = (g * PX + in_block) ^ turn
        for side in range(4):
            near = take_lanes(jnp.broadcast_to(table[side : side + 1, :], (SUB, LANE)), patch)
            place = jnp.maximum(near, 0) ^ turn
            pick, origin = place & (PX - 1), lax.shift_right_logical(place, 5)
            lacking = jnp.where(near < 0, 1, 0)
            if side in (WEST, EAST):
                pick = pick + PX * block
            else:
                edge, step = (0, -PX) if side == SOUTH else (BLOCKS - 1, PX)
                across = pick + (LANE - PX if side == SOUTH else 0)
                pick = jnp.where(block == edge, across, lane + step)
                origin = jnp.where(block == edge, origin, g)
                lacking = jnp.where(block == edge, lacking, 0)
            for kind, x in enumerate((pick, origin, lacking)):
                at = ((g * 4 + side) * 3 + kind) * SUB
                lanes_ref[at : at + SUB, :] = x


def place_of(me, other, n):
    if power_of_two(n):
        apart = me ^ other
        return jnp.where(apart == 0, 0, n - apart)
    ahead = other - me
    return jnp.where(ahead < 0, ahead + n, ahead)


def pack_kernel(tiles, rows, group, count, patches, slots, mesh_sizes, *refs):
    owner_ref, around_ref, which_ref, start_ref, patch_ref, box_ref = refs[:6]
    n_gx, n_gz = mesh_sizes
    pay_ref, raw_ref, lanes_ref = refs[6:9]
    cut_refs, (table, slot_ref) = refs[9 : 9 + n_gz], refs[9 + n_gz :]
    raw_ref[...] = patch_ref[...]
    me = lax.axis_index("gy")
    top = None
    for s in range(SUB):
        wave = top_speed([patch_ref[0, 0, f, :, s * LANE : (s + 1) * LANE] for f in range(FIELDS)])
        top = wave if top is None else jnp.maximum(top, wave)
    for f in range(FIELDS):
        pay_ref[f * tiles : (f + 1) * tiles, :] = box_ref[pl.ds(f * BOX_ROWS + me * tiles, tiles), :]
    pay_ref[rows - SUB : rows, :] = top

    start, which = start_ref[0, 0], which_ref[0, 0]
    row = lax.shift_right_logical(start * 2675, 17)
    offset = BOX * (row & 1) + start - row * STRIDE
    near = lax.shift_right_logical(row, 1) - me * tiles
    place = place_of(lax.axis_index("gx"), lax.shift_right_logical(which, n_gz.bit_length() - 1), n_gx)
    apart = (which & (n_gz - 1)) ^ lax.axis_index("gz")
    patch = lax.broadcasted_iota(jnp.int32, start.shape, 1)
    for k in range(n_gz):
        mine = (near >= 0) & (near < tiles) & (apart == k)
        cut_refs[k][0:4, 0:patches] = jnp.where(mine, place * rows + near, n_gx * rows)
        cut_refs[k][4:8, 0:patches] = (HALF * (patch & (SUB - 1)) - offset) & (LANE - 1)
    make_lanes(group, count, patches, slots, around_ref, owner_ref, lanes_ref, table, slot_ref)


def strip_kernel(parts, groups, rows, tiles, patches, *refs):
    cut_refs, pay_ref, out_refs = refs[:groups], refs[groups], refs[groups + 1 :]
    top = pay_ref[rows - SUB : rows, :]
    for k in range(1, parts):
        top = jnp.maximum(top, pay_ref[(k + 1) * rows - SUB : (k + 1) * rows, :])
    block = lane_of() // HALF
    lines = 4 * patches // SUB
    for cut_ref, out_ref in zip(cut_refs, out_refs):
        out_ref[FIELDS * lines :, :] = top
        for v in range(lines):
            side, first = v // (patches // SUB), v % (patches // SUB) * SUB
            acc = None
            for m in range(SUB):
                strip = pay_ref[pl.ds(cut_ref[side, first + m], SUB, stride=tiles), :]
                strip = pltpu.roll(strip, cut_ref[4 + side, first + m], 1)
                acc = strip if acc is None else jnp.where(block == m, strip, acc)
            out_ref[pl.ds(v, FIELDS, stride=lines), :] = acc[:FIELDS, :]


def lanes_at(lanes_ref, g, side, kind):
    at = ((g * 4 + side) * 3 + kind) * SUB
    return lanes_ref[at : at + SUB, :]


def held_at(lanes_ref, sets):
    return lanes_ref[sets * 4 * 3 * SUB : (sets * 4 * 3 + 1) * SUB, :]


def fill_ghosts(u_ref, lanes_ref, coarse_ref, sets):
    for f in range(FIELDS):
        for g in range(sets):

            def ghost(side, at, kept):
                x = None
                for o in range(sets):
                    start = (o * FIELDS + f) * PLANE + at
                    edge = pl.ds(start, DEEP, stride=SPAN) if side in (WEST, EAST) else pl.ds(start, SUB)
                    moved = take_lanes(u_ref[edge, :], lanes_at(lanes_ref, g, side, 0))
                    x = moved if x is None else jnp.where(lanes_at(lanes_ref, g, side, 1) == o, moved, x)
                if coarse_ref is None:
                    return x
                start = ((g * FIELDS + f) * 10 + kept) * SUB
                return jnp.where(lanes_at(lanes_ref, g, side, 2) != 0, coarse_ref[start : start + SUB, :], x)

            base = (g * FIELDS + f) * PLANE
            for side, column, to in ((WEST, PX - 1, -1), (EAST, 0, PX)):
                u_ref[pl.ds(base + spot(0, to), DEEP, stride=SPAN), :] = ghost(side, spot(0, column), side)
            for side, row, to in ((SOUTH, DEEP - 1, -1), (NORTH, 0, DEEP)):
                for i in range(BLOCKS):
                    kept = 2 + (side - SOUTH) * BLOCKS + i
                    u_ref[pl.ds(base + spot(to, SUB * i), SUB), :] = ghost(side, spot(row, SUB * i), kept)


def halves_of(u, axis):
    vx, vy, pressure, sound = primitive(u)
    return half_flux(u, (vx, vy)[axis], pressure, sound, axis + 1)


def fill_halves(u_ref, aux_ref, sets):
    def fill(g, rows, axes):
        u = [u_ref[rows((g * FIELDS + f) * PLANE), :] for f in range(FIELDS)]
        vx, vy, pressure, sound = primitive(u)
        for axis in axes:
            for n, x in enumerate(half_flux(u, (vx, vy)[axis], pressure, sound, axis + 1)):
                aux_ref[rows((g * AUX + axis * (FIELDS + 1) + n) * PLANE), :] = x

    for g in range(sets):

        def cells(r, carry):
            for part in range(BLOCKS):
                for i in range(BLOCKS):
                    at = spot(BLOCKS * r + part, SUB * i)
                    fill(g, lambda b, at=at: pl.ds(pl.multiple_of(b + at, SUB), SUB), (0, 1))
            return carry

        lax.fori_loop(0, DEEP // BLOCKS, cells, 0)
        for r in (-1, DEEP):
            for i in range(BLOCKS):
                fill(g, lambda b, at=spot(r, SUB * i): pl.ds(b + at, SUB), (1,))
        for c in (-1, PX):
            fill(g, lambda b, at=spot(0, c): pl.ds(b + at, DEEP, stride=SPAN), (0,))


def load_cells(u_ref, aux_ref, g, axis, rows):
    u = [u_ref[rows((g * FIELDS + f) * PLANE), :] for f in range(FIELDS)]
    start = g * AUX + axis * (FIELDS + 1)
    return u, [aux_ref[rows((start + n) * PLANE), :] for n in range(FIELDS + 1)]


def at_row(at):
    return lambda b: pl.ds(b + at, SUB)


def fill_x_faces(u_ref, aux_ref, dx_ref, g, base):
    def across(r, carry):
        for part in range(BLOCKS):
            row = BLOCKS * r + part
            for i in range(BLOCKS + 1):
                at = pl.multiple_of(spot(row, SUB * i), SUB)
                low = load_cells(u_ref, aux_ref, g, 0, at_row(at - 1))
                faces = face_flux(*low, *load_cells(u_ref, aux_ref, g, 0, at_row(at)))
                for f in range(FIELDS):
                    to = pl.multiple_of(base + (f * DEEP + row) * FACES + SUB * i, SUB)
                    dx_ref[pl.ds(to, SUB), :] = faces[f]
        return carry

    lax.fori_loop(0, DEEP // BLOCKS, across, 0)


def x_change(dx_ref, base, f, row, i):
    west = pl.multiple_of(base + (f * DEEP + row) * FACES + SUB * i, SUB)
    return dx_ref[pl.ds(west, SUB), :] - dx_ref[pl.ds(west + 1, SUB), :]


def prepare_kernel(group, count, patches, lanes_ref, *refs):
    raw_refs = refs[:group]
    u_ref, edge_ref, dx_ref, dy_ref, aux_ref = refs[group:]
    sets = patches // PX

    for f in range(FIELDS):
        for g in range(sets):
            for h in range(2):
                tiles = []
                for q in range(BLOCKS):
                    at = (q * 2 + h) * LANE
                    for k in range(PX // count):
                        tiles.append(raw_refs[g * (PX // count) + k][0, 0, f, :, at : at + LANE])
                cells = jnp.concatenate(tiles, axis=0).T
                for i in range(BLOCKS):
                    to = (g * FIELDS + f) * PLANE + spot(h * BLOCKS + i, 0)
                    u_ref[to : to + PX, :] = cells[i * PX : (i + 1) * PX, :]

    fill_ghosts(u_ref, lanes_ref, None, sets)
    fill_halves(u_ref, aux_ref, sets)
    for g in range(sets):
        fill_x_faces(u_ref, aux_ref, dx_ref, g, g * FIELDS * DEEP * FACES)

        def along(i, carry):
            low = load_cells(u_ref, aux_ref, g, 1, at_row(pl.multiple_of(spot(-1, SUB * i), SUB)))
            for r in range(DEEP + 1):
                cell = load_cells(u_ref, aux_ref, g, 1, at_row(pl.multiple_of(spot(r, SUB * i), SUB)))
                for f, face in enumerate(face_flux(*low, *cell)):
                    to = pl.multiple_of(((g * FIELDS + f) * (DEEP + 1) + r) * PX + SUB * i, SUB)
                    dy_ref[pl.ds(to, SUB), :] = face
                low = cell
            return carry

        lax.fori_loop(0, BLOCKS, along, 0)
        for side in range(4):
            for i, rows in enumerate(edge_rows(side)):
                for n in range(FIELDS + 1):
                    start = g * AUX + (0 if side in (WEST, EAST) else FIELDS + 1) + n
                    to = edge_place(g, side, i, n)
                    edge_ref[to : to + SUB, :] = aux_ref[rows(start * PLANE), :]


def edge_rows(side):
    if side in (WEST, EAST):
        at = spot(0, 0 if side == WEST else PX - 1)
        return [lambda b: pl.ds(b + at, DEEP, stride=SPAN)]
    return [at_row(spot(0 if side == SOUTH else DEEP - 1, SUB * i)) for i in range(BLOCKS)]


def edge_place(g, side, i, n):
    kept = side if side in (WEST, EAST) else 2 + (side - SOUTH) * BLOCKS + i
    return ((g * 10 + kept) * (FIELDS + 1) + n) * SUB


def step_kernel(count, patches, slots, *refs):
    u_ref, edge_ref, dx_ref, dy_ref, lanes_ref = refs[:5]
    strip_refs, out_ref = refs[5:7], refs[7]
    next_u, next_aux, next_dx, strips, doubled, coarse_ref, border_ref = refs[8:]
    lines = 4 * patches // SUB
    sets = patches // PX
    lane, sub = lane_of(), sub_of()
    block, in_block = lane // PX, lane & (PX - 1)
    turn = lax.axis_index("gy") * count

    def joined(at, join):
        return functools.reduce(join, [ref[at : at + SUB, :] for ref in strip_refs])

    for at in range(0, FIELDS * lines, SUB):
        strips[at : at + SUB, :] = joined(at, jnp.add)
    time_step = courant / jnp.max(joined(FIELDS * lines, jnp.maximum))
    part = HALF * sub + (lane & (HALF - 1))
    for t in range(4 * patches // LANE):
        tiles = []
        for v in range(t * HALF, (t + 1) * HALF):
            tile = None
            for f in range(FIELDS):
                row = jnp.broadcast_to(strips[f * lines + v : f * lines + v + 1, :], (SUB, LANE))
                wide = take_lanes(row, part)
                tile = wide if tile is None else jnp.where(lane // HALF == f, wide, tile)
            tiles.append(tile)
        cells = jnp.concatenate(tiles, axis=0).T
        for n in range(FIELDS * 2):
            for twice in range(2):
                at = t * FIELDS * PX + n * HALF + twice
                doubled[pl.ds(at, SUB, stride=2), :] = cells[n * SUB : (n + 1) * SUB, :]

    for g in range(sets):
        patch = (g * PX + in_block) ^ turn
        for side in range(4):
            t, shift = side * patches // LANE, side * patches % LANE
            for f in range(FIELDS):
                pieces = []
                for i in range(BLOCKS):
                    at = t * FIELDS * PX + f * PX + SUB * i
                    pieces.append(take_lanes(doubled[at : at + SUB, :], patch + shift))
                base = (g * FIELDS + f) * 10
                if side in (WEST, EAST):
                    x = pieces[0]
                    for q in range(1, BLOCKS):
                        x = jnp.where(block == q, pieces[q], x)
                    coarse_ref[(base + side) * SUB : (base + side + 1) * SUB, :] = x
                else:
                    for i in range(BLOCKS):
                        at = (base + 2 + (side - SOUTH) * BLOCKS + i) * SUB
                        coarse_ref[at : at + SUB, :] = pieces[i]

    size = FIELDS * DEEP * FACES
    for g in range(sets):
        for at in range(0, size, SUB):
            next_dx[g * size + at : g * size + at + SUB, :] = dx_ref[g * size + at : g * size + at + SUB, :]

        def coarse_cells(kept, axis):
            at = [((g * FIELDS + f) * 10 + kept) * SUB for f in range(FIELDS)]
            u = [coarse_ref[a : a + SUB, :] for a in at]
            return u, halves_of(u, axis)

        def own_cells(side, i):
            rows = edge_rows(side)[i]
            places = [edge_place(g, side, i, n) for n in range(FIELDS + 1)]
            u = [u_ref[rows((g * FIELDS + f) * PLANE), :] for f in range(FIELDS)]
            return u, [edge_ref[at : at + SUB, :] for at in places]

        for side, face in ((WEST, 0), (EAST, PX)):
            beyond, own = coarse_cells(side, 0), own_cells(side, 0)
            faces = face_flux(*beyond, *own) if side == WEST else face_flux(*own, *beyond)
            lacking = lanes_at(lanes_ref, g, side, 2) != 0
            for f in range(FIELDS):
                rows = pl.ds(g * size + f * DEEP * FACES + face, DEEP, stride=FACES)
                next_dx[rows, :] = jnp.where(lacking, faces[f], dx_ref[rows, :])
        for side, face in ((SOUTH, 0), (NORTH, DEEP)):
            lacking = lanes_at(lanes_ref, g, side, 2) != 0
            for i in range(BLOCKS):
                kept = (side - SOUTH) * BLOCKS + i
                beyond, own = coarse_cells(2 + kept, 1), own_cells(side, i)
                faces = face_flux(*beyond, *own) if side == SOUTH else face_flux(*own, *beyond)
                for f in range(FIELDS):
                    fine = ((g * FIELDS + f) * (DEEP + 1) + face) * PX + SUB * i
                    to = ((g * FIELDS + f) * 8 + kept) * SUB
                    border_ref[to : to + SUB, :] = jnp.where(lacking, faces[f], dy_ref[fine : fine + SUB, :])

        for f in range(FIELDS):
            for i in range(BLOCKS):
                for r in range(DEEP):
                    faces = []
                    for n in (r, r + 1):
                        if n in (0, DEEP):
                            at = ((g * FIELDS + f) * 8 + (BLOCKS if n else 0) + i) * SUB
                            faces.append(border_ref[pl.ds(pl.multiple_of(at, SUB), SUB), :])
                        else:
                            at = ((g * FIELDS + f) * (DEEP + 1) + n) * PX + SUB * i
                            faces.append(dy_ref[pl.ds(pl.multiple_of(at, SUB), SUB), :])
                    change = x_change(next_dx, g * size, f, r, i) + (faces[0] - faces[1])
                    at = pl.ds(pl.multiple_of((g * FIELDS + f) * PLANE + spot(r, SUB * i), SUB), SUB)
                    next_u[at, :] = u_ref[at, :] + time_step * change

    fill_ghosts(next_u, lanes_ref, coarse_ref, sets)
    fill_halves(next_u, next_aux, sets)
    for g in range(sets):
        fill_x_faces(next_u, next_aux, next_dx, g, g * size)

        def along(half, carry):
            for i in (2 * half, 2 * half + 1):
                low = load_cells(next_u, next_aux, g, 1, at_row(pl.multiple_of(spot(-1, SUB * i), SUB)))
                low_faces = None
                for r in range(DEEP + 1):
                    cell = load_cells(next_u, next_aux, g, 1, at_row(pl.multiple_of(spot(r, SUB * i), SUB)))
                    faces = face_flux(*low, *cell)
                    for f in range(FIELDS):
                        if r == 0:
                            continue
                        change = x_change(next_dx, g * size, f, r - 1, i) + (low_faces[f] - faces[f])
                        new = low[0][f] + time_step * change
                        at = pl.ds(pl.multiple_of((g * FIELDS + f) * PLANE + spot(r - 1, SUB * i), SUB), SUB)
                        next_u[at, :] = 0.5 * u_ref[at, :] + 0.5 * new
                    low, low_faces = cell, faces
            return carry

        lax.fori_loop(0, BLOCKS // 2, along, 0)

    held = held_at(lanes_ref, sets)
    place = jnp.maximum(held, 0) ^ turn
    pick, origin = PX * block + (place & (PX - 1)), lax.shift_right_logical(place, 5)
    for f in range(FIELDS):
        for h in range(2):
            tiles = []
            for i in range(LANE // SUB):
                at = spot(h * BLOCKS + i // BLOCKS, SUB * (i % BLOCKS))
                x = None
                for g in range(sets):
                    start = (g * FIELDS + f) * PLANE + at
                    moved = take_lanes(next_u[start : start + SUB, :], pick)
                    x = moved if x is None else jnp.where(origin == g, moved, x)
                tiles.append(jnp.where(held >= 0, x, 0.0))
            cells = jnp.concatenate(tiles, axis=0).T
            for q in range(BLOCKS):
                at = (q * 2 + h) * LANE
                out_ref[0, 0, f, :, at : at + LANE] = cells[q * PX : q * PX + slots, :]


def limit(*row_counts):
    return pltpu.CompilerParams(vmem_limit_bytes=(sum(row_counts) * LANE * 4 * 5 // 4) + (1 << 20))


def per_device(patch_state, coarse_boxes, new_owner, neighbors, coarse_box, coarse_start):
    count = patch_state.shape[2]
    n_gx, n_gz, group = lax.axis_size("gx"), lax.axis_size("gz"), lax.axis_size("gy")
    parts = n_gx * n_gz
    patches = count * group
    lines = 4 * patches // SUB
    slots = group * max(2, 2 * count // group)
    tiles = BOX_ROWS // group
    rows = -(-tiles * FIELDS // SUB) * SUB + SUB
    strip_rows = FIELDS * lines + SUB
    vmem = pl.BlockSpec(memory_space=pltpu.VMEM)
    smem = pl.BlockSpec(memory_space=pltpu.SMEM)
    f32 = jnp.float32

    def sides_first(x):
        return jnp.swapaxes(x, 2, 3)

    sets = patches // PX
    payload, raw, lanes, *cuts = pl.pallas_call(
        functools.partial(pack_kernel, tiles, rows, group, count, patches, slots, (n_gx, n_gz)),
        out_shape=(
            pltpu.VMEM((rows, LANE), f32),
            pltpu.VMEM((1, 1, FIELDS, count, SUB * LANE), f32),
            pltpu.VMEM(((sets * 4 * 3 + 1) * SUB, LANE), jnp.int32),
        )
        + (pltpu.VMEM((SUB, max(LANE, patches)), jnp.int32),) * n_gz,
        in_specs=[smem] + [vmem] * 5,
        out_specs=(vmem,) * (3 + n_gz),
        scratch_shapes=[pltpu.VMEM((SUB, LANE), jnp.int32), pltpu.SMEM((slots + 1,), jnp.int32)],
        name="pack",
    )(
        sides_first(new_owner),
        sides_first(neighbors),
        sides_first(coarse_box),
        sides_first(coarse_start),
        sides_first(patch_state),
        coarse_boxes.reshape(FIELDS * BOX_ROWS, LANE),
    )

    if power_of_two(n_gx):
        perms = [[(i, i ^ k) for i in range(n_gx)] for k in range(1, n_gx)]
    else:
        perms = [[(i, (i + k) % n_gx) for i in range(n_gx)] for k in range(1, n_gx)]
    boxes = [payload] + [lax.ppermute(payload, "gx", perm) for perm in perms[::-1]]
    cuts = cuts[:1] + [lax.ppermute(cuts[k], "gz", [(i, i ^ k) for i in range(n_gz)]) for k in range(1, n_gz)]
    far = masks_of(group)[0]
    raw_far = lax.ppermute(raw, "gy", [(i, i ^ far) for i in range(group)])
    raw_far, *boxes, last = lax.optimization_barrier([raw_far] + boxes + cuts[1:2])
    cuts = cuts[:1] + [last] + cuts[2:]
    boxes = jnp.concatenate(boxes + [jnp.zeros((SUB * tiles, LANE), f32)], axis=0)

    strips = pl.pallas_call(
        functools.partial(strip_kernel, n_gx, n_gz, rows, tiles, patches),
        out_shape=[pltpu.VMEM((strip_rows, LANE), f32)] * n_gz,
        in_specs=[smem] * n_gz + [vmem],
        out_specs=[vmem] * n_gz,
        compiler_params=limit(n_gx * rows + SUB * tiles, n_gz * strip_rows),
        name="strips",
    )(*cuts, boxes)

    raws, have = [raw] + [None] * (group - 1), [0]
    raws[far] = raw_far
    for mask in masks_of(group):
        perm = [(i, i ^ mask) for i in range(group)]
        for k in have:
            block = raws[k]
            if mask == 1 and k:
                block, _ = lax.optimization_barrier((block, strips[0]))
            if raws[k ^ mask] is None:
                raws[k ^ mask] = lax.ppermute(block, "gy", perm)
        have = have + [k ^ mask for k in have]

    shares = [strips[0]]
    for k in reversed(range(1, n_gz * group)):
        if k // n_gz % 2 == 0:
            perm = [(i, i ^ k) for i in range(n_gz * group)]
            shares.append(lax.ppermute(strips[k % n_gz], ("gy", "gz"), perm))

    made_rows = [
        sets * FIELDS * PLANE,
        sets * 10 * (FIELDS + 1) * SUB,
        sets * FIELDS * DEEP * FACES,
        sets * FIELDS * (DEEP + 1) * PX,
    ]
    made = pl.pallas_call(
        functools.partial(prepare_kernel, group, count, patches),
        out_shape=[pltpu.VMEM((n, LANE), f32) for n in made_rows],
        in_specs=[vmem] * (1 + group),
        out_specs=[vmem] * 4,
        scratch_shapes=[pltpu.VMEM((sets * AUX * PLANE, LANE), f32)],
        compiler_params=limit(*made_rows, sets * AUX * PLANE, lanes.shape[0], patches * FIELDS * SUB),
        cost_estimate=pl.CostEstimate(flops=patches * 1024 * 300, bytes_accessed=patches * 40000, transcendentals=0),
        name="prepare",
    )(lanes, *raws)

    shares = lax.optimization_barrier(shares + [made[0]])[:-1]
    row = lax.broadcasted_iota(jnp.int32, (strip_rows, LANE), 0)
    joined = jnp.where(row < FIELDS * lines, functools.reduce(jnp.add, shares), functools.reduce(jnp.maximum, shares))

    strips = [joined, lax.ppermute(joined, "gy", [(i, i ^ 1) for i in range(group)])]
    scratch_rows = [sets * FIELDS * PLANE, sets * AUX * PLANE, sets * FIELDS * DEEP * FACES] + [
        FIELDS * lines,
        4 * patches // LANE * FIELDS * PX,
        sets * FIELDS * 10 * SUB,
        sets * FIELDS * 8 * SUB,
    ]
    out = pl.pallas_call(
        functools.partial(step_kernel, count, patches, slots),
        out_shape=jax.ShapeDtypeStruct((1, 1, FIELDS, slots, SUB * LANE), f32),
        in_specs=[vmem] * 7,
        out_specs=vmem,
        scratch_shapes=[pltpu.VMEM((n, LANE), f32) for n in scratch_rows],
        compiler_params=limit(*scratch_rows, *made_rows, lanes.shape[0], 2 * strip_rows, FIELDS * slots * SUB),
        name="step",
    )(*made, lanes, *strips)
    return sides_first(out)


def solution(mesh):
    in_specs = (
        P("gx", "gz", "gy", None, None),
        P(("gx", "gz"), None, None),
        P("gx", "gz", None, None),
        P("gx", "gz", None, None),
        P("gx", "gz", None, None),
        P("gx", "gz", None, None),
    )
    out_specs = P("gx", "gz", "gy", None, None)
    return jax.shard_map(
        per_device, mesh=mesh, in_specs=in_specs, out_specs=out_specs, check_vma=False
    )
```

```python
import functools

import jax
import jax.numpy as jnp
from jax import lax
from jax.experimental import pallas as pl
from jax.experimental.pallas import tpu as pltpu
from jax.sharding import PartitionSpec as P

FIELDS = 5
PX = 32
BOX = 64
SUB = 8
LANE = 128
HALF = PX // 2
STRIDE = BOX - HALF + 1
BOX_ROWS = BOX * BOX // LANE
heat_ratio = 1.4
courant = 0.3
WEST, EAST, SOUTH, NORTH = range(4)
BLOCKS = LANE // PX
DEEP = PX // BLOCKS
SPAN = PX + 2 * SUB
PLANE = (DEEP + 2) * SPAN
FACES = PX + SUB
AUX = 2 * (FIELDS + 1)


def spot(row, column):
    return (row + 1) * SPAN + SUB + column


def power_of_two(n):
    return n & (n - 1) == 0


def masks_of(n):
    return [n >> (i + 1) for i in range(n.bit_length() - 1)]


def primitive(u):
    inverse = 1.0 / u[0]
    vx, vy, vz = u[1] * inverse, u[2] * inverse, u[3] * inverse
    kinetic = u[1] * (0.5 * vx) + u[2] * (0.5 * vy) + u[3] * (0.5 * vz)
    pressure = (heat_ratio - 1.0) * (u[4] - kinetic)
    sound = jnp.sqrt(heat_ratio * pressure * inverse)
    return vx, vy, pressure, sound


def half_flux(u, moving, pressure, sound, normal):
    half = 0.5 * moving
    flux = [u[f] * half for f in range(FIELDS)]
    flux[normal] = flux[normal] + 0.5 * pressure
    flux[4] = flux[4] + pressure * half
    return flux + [0.5 * (jnp.abs(moving) + sound)]


def face_flux(low_u, low_aux, u, aux):
    wave = jnp.maximum(low_aux[FIELDS], aux[FIELDS])
    return [low_aux[f] + aux[f] - wave * (u[f] - low_u[f]) for f in range(FIELDS)]


def lane_of():
    return lax.broadcasted_iota(jnp.int32, (SUB, LANE), 1)


def sub_of():
    return lax.broadcasted_iota(jnp.int32, (SUB, LANE), 0)


def take_lanes(x, lanes):
    return jnp.take_along_axis(x, lanes, axis=1, mode="promise_in_bounds")


def top_speed(u):
    vx, vy, _, sound = primitive(u)
    return jnp.maximum(jnp.abs(vx), jnp.abs(vy)) + sound


def make_lanes(group, count, patches, slots, around_ref, owner_ref, lanes_ref, table, slot_ref):
    me = lax.axis_index("gy")
    capacity = slots // group
    sets = patches // PX
    lane = lane_of()
    block, in_block = lane // PX, lane & (PX - 1)
    turn = me * count

    for i in range(slots):
        slot_ref[i] = -1

    def rank_source(source, carry):
        rank = jnp.int32(0)
        for i in range(count):
            p = source * count + i
            hit = owner_ref[0, 0, 0, p] == me
            slot_ref[jnp.where(hit, source * capacity + rank, slots)] = p
            rank = rank + jnp.where(hit, 1, 0)
        return carry

    lax.fori_loop(0, group, rank_source, 0)
    held = jnp.full((SUB, LANE), -1, jnp.int32)
    for j in range(slots):
        held = jnp.where(in_block == j, slot_ref[j], held)
    lanes_ref[sets * 4 * 3 * SUB :, :] = held

    table[0:4, 0:patches] = around_ref[0, 0]
    for g in range(sets):
        patch = (g * PX + in_block) ^ turn
        for side in range(4):
            near = take_lanes(jnp.broadcast_to(table[side : side + 1, :], (SUB, LANE)), patch)
            place = jnp.maximum(near, 0) ^ turn
            pick, origin = place & (PX - 1), lax.shift_right_logical(place, 5)
            lacking = jnp.where(near < 0, 1, 0)
            if side in (WEST, EAST):
                pick = pick + PX * block
            else:
                edge, step = (0, -PX) if side == SOUTH else (BLOCKS - 1, PX)
                across = pick + (LANE - PX if side == SOUTH else 0)
                pick = jnp.where(block == edge, across, lane + step)
                origin = jnp.where(block == edge, origin, g)
                lacking = jnp.where(block == edge, lacking, 0)
            for kind, x in enumerate((pick, origin, lacking)):
                at = ((g * 4 + side) * 3 + kind) * SUB
                lanes_ref[at : at + SUB, :] = x


def place_of(me, other, n):
    if power_of_two(n):
        return me ^ other
    behind = me - other
    return jnp.where(behind < 0, behind + n, behind)


def pack_kernel(tiles, rows, group, count, patches, slots, mesh_sizes, *refs):
    owner_ref, around_ref, which_ref, start_ref, patch_ref, box_ref = refs[:6]
    n_gx, n_gz = mesh_sizes
    pay_ref, raw_ref, lanes_ref = refs[6:9]
    cut_refs, (table, slot_ref) = refs[9 : 9 + n_gz], refs[9 + n_gz :]
    raw_ref[...] = patch_ref[...]
    me = lax.axis_index("gy")
    top = None
    for s in range(SUB):
        wave = top_speed([patch_ref[0, 0, f, :, s * LANE : (s + 1) * LANE] for f in range(FIELDS)])
        top = wave if top is None else jnp.maximum(top, wave)
    for f in range(FIELDS):
        pay_ref[f * tiles : (f + 1) * tiles, :] = box_ref[pl.ds(f * BOX_ROWS + me * tiles, tiles), :]
    pay_ref[rows - SUB : rows, :] = top

    start, which = start_ref[0, 0], which_ref[0, 0]
    row = lax.shift_right_logical(start * 2675, 17)
    offset = BOX * (row & 1) + start - row * STRIDE
    near = lax.shift_right_logical(row, 1) - me * tiles
    place = place_of(lax.axis_index("gx"), lax.shift_right_logical(which, n_gz.bit_length() - 1), n_gx)
    apart = (which & (n_gz - 1)) ^ lax.axis_index("gz")
    patch = lax.broadcasted_iota(jnp.int32, start.shape, 1)
    for k in range(n_gz):
        mine = (near >= 0) & (near < tiles) & (apart == k)
        cut_refs[k][0:4, 0:patches] = jnp.where(mine, place * rows + near, n_gx * rows)
        cut_refs[k][4:8, 0:patches] = (HALF * (patch & (SUB - 1)) - offset) & (LANE - 1)
    make_lanes(group, count, patches, slots, around_ref, owner_ref, lanes_ref, table, slot_ref)


def strip_kernel(parts, groups, rows, tiles, patches, *refs):
    cut_refs, pay_ref, out_refs = refs[:groups], refs[groups], refs[groups + 1 :]
    top = pay_ref[rows - SUB : rows, :]
    for k in range(1, parts):
        top = jnp.maximum(top, pay_ref[(k + 1) * rows - SUB : (k + 1) * rows, :])
    block = lane_of() // HALF
    lines = 4 * patches // SUB
    for cut_ref, out_ref in zip(cut_refs, out_refs):
        out_ref[FIELDS * lines :, :] = top
        for v in range(lines):
            side, first = v // (patches // SUB), v % (patches // SUB) * SUB
            acc = None
            for m in range(SUB):
                strip = pay_ref[pl.ds(cut_ref[side, first + m], SUB, stride=tiles), :]
                strip = pltpu.roll(strip, cut_ref[4 + side, first + m], 1)
                acc = strip if acc is None else jnp.where(block == m, strip, acc)
            out_ref[pl.ds(v, FIELDS, stride=lines), :] = acc[:FIELDS, :]


def lanes_at(lanes_ref, g, side, kind):
    at = ((g * 4 + side) * 3 + kind) * SUB
    return lanes_ref[at : at + SUB, :]


def held_at(lanes_ref, sets):
    return lanes_ref[sets * 4 * 3 * SUB : (sets * 4 * 3 + 1) * SUB, :]


def fill_ghosts(u_ref, lanes_ref, coarse_ref, sets):
    for f in range(FIELDS):
        for g in range(sets):

            def ghost(side, at, kept):
                x = None
                for o in range(sets):
                    start = (o * FIELDS + f) * PLANE + at
                    edge = pl.ds(start, DEEP, stride=SPAN) if side in (WEST, EAST) else pl.ds(start, SUB)
                    moved = take_lanes(u_ref[edge, :], lanes_at(lanes_ref, g, side, 0))
                    x = moved if x is None else jnp.where(lanes_at(lanes_ref, g, side, 1) == o, moved, x)
                if coarse_ref is None:
                    return x
                start = ((g * FIELDS + f) * 10 + kept) * SUB
                return jnp.where(lanes_at(lanes_ref, g, side, 2) != 0, coarse_ref[start : start + SUB, :], x)

            base = (g * FIELDS + f) * PLANE
            for side, column, to in ((WEST, PX - 1, -1), (EAST, 0, PX)):
                u_ref[pl.ds(base + spot(0, to), DEEP, stride=SPAN), :] = ghost(side, spot(0, column), side)
            for side, row, to in ((SOUTH, DEEP - 1, -1), (NORTH, 0, DEEP)):
                for i in range(BLOCKS):
                    kept = 2 + (side - SOUTH) * BLOCKS + i
                    u_ref[pl.ds(base + spot(to, SUB * i), SUB), :] = ghost(side, spot(row, SUB * i), kept)


def halves_of(u, axis):
    vx, vy, pressure, sound = primitive(u)
    return half_flux(u, (vx, vy)[axis], pressure, sound, axis + 1)


def fill_halves(u_ref, aux_ref, sets):
    def fill(g, rows, axes):
        u = [u_ref[rows((g * FIELDS + f) * PLANE), :] for f in range(FIELDS)]
        vx, vy, pressure, sound = primitive(u)
        for axis in axes:
            for n, x in enumerate(half_flux(u, (vx, vy)[axis], pressure, sound, axis + 1)):
                aux_ref[rows((g * AUX + axis * (FIELDS + 1) + n) * PLANE), :] = x

    for g in range(sets):

        def cells(r, carry):
            for part in range(BLOCKS):
                for i in range(BLOCKS):
                    at = spot(BLOCKS * r + part, SUB * i)
                    fill(g, lambda b, at=at: pl.ds(pl.multiple_of(b + at, SUB), SUB), (0, 1))
            return carry

        lax.fori_loop(0, DEEP // BLOCKS, cells, 0)
        for r in (-1, DEEP):
            for i in range(BLOCKS):
                fill(g, lambda b, at=spot(r, SUB * i): pl.ds(b + at, SUB), (1,))
        for c in (-1, PX):
            fill(g, lambda b, at=spot(0, c): pl.ds(b + at, DEEP, stride=SPAN), (0,))


def load_cells(u_ref, aux_ref, g, axis, rows):
    u = [u_ref[rows((g * FIELDS + f) * PLANE), :] for f in range(FIELDS)]
    start = g * AUX + axis * (FIELDS + 1)
    return u, [aux_ref[rows((start + n) * PLANE), :] for n in range(FIELDS + 1)]


def at_row(at):
    return lambda b: pl.ds(b + at, SUB)


def fill_x_faces(u_ref, aux_ref, dx_ref, g, base):
    def across(r, carry):
        for part in range(BLOCKS):
            row = BLOCKS * r + part
            for i in range(BLOCKS + 1):
                at = pl.multiple_of(spot(row, SUB * i), SUB)
                low = load_cells(u_ref, aux_ref, g, 0, at_row(at - 1))
                faces = face_flux(*low, *load_cells(u_ref, aux_ref, g, 0, at_row(at)))
                for f in range(FIELDS):
                    to = pl.multiple_of(base + (f * DEEP + row) * FACES + SUB * i, SUB)
                    dx_ref[pl.ds(to, SUB), :] = faces[f]
        return carry

    lax.fori_loop(0, DEEP // BLOCKS, across, 0)


def x_change(dx_ref, base, f, row, i):
    west = pl.multiple_of(base + (f * DEEP + row) * FACES + SUB * i, SUB)
    return dx_ref[pl.ds(west, SUB), :] - dx_ref[pl.ds(west + 1, SUB), :]


def prepare_kernel(group, count, patches, lanes_ref, *refs):
    raw_refs = refs[:group]
    u_ref, edge_ref, dx_ref, dy_ref, aux_ref = refs[group:]
    sets = patches // PX

    for f in range(FIELDS):
        for g in range(sets):
            for h in range(2):
                tiles = []
                for q in range(BLOCKS):
                    at = (q * 2 + h) * LANE
                    for k in range(PX // count):
                        tiles.append(raw_refs[g * (PX // count) + k][0, 0, f, :, at : at + LANE])
                cells = jnp.concatenate(tiles, axis=0).T
                for i in range(BLOCKS):
                    to = (g * FIELDS + f) * PLANE + spot(h * BLOCKS + i, 0)
                    u_ref[to : to + PX, :] = cells[i * PX : (i + 1) * PX, :]

    fill_ghosts(u_ref, lanes_ref, None, sets)
    fill_halves(u_ref, aux_ref, sets)
    for g in range(sets):
        fill_x_faces(u_ref, aux_ref, dx_ref, g, g * FIELDS * DEEP * FACES)

        def along(i, carry):
            low = load_cells(u_ref, aux_ref, g, 1, at_row(pl.multiple_of(spot(-1, SUB * i), SUB)))
            for r in range(DEEP + 1):
                cell = load_cells(u_ref, aux_ref, g, 1, at_row(pl.multiple_of(spot(r, SUB * i), SUB)))
                for f, face in enumerate(face_flux(*low, *cell)):
                    to = pl.multiple_of(((g * FIELDS + f) * (DEEP + 1) + r) * PX + SUB * i, SUB)
                    dy_ref[pl.ds(to, SUB), :] = face
                low = cell
            return carry

        lax.fori_loop(0, BLOCKS, along, 0)
        for side in range(4):
            for i, rows in enumerate(edge_rows(side)):
                for n in range(FIELDS + 1):
                    start = g * AUX + (0 if side in (WEST, EAST) else FIELDS + 1) + n
                    to = edge_place(g, side, i, n)
                    edge_ref[to : to + SUB, :] = aux_ref[rows(start * PLANE), :]


def edge_rows(side):
    if side in (WEST, EAST):
        at = spot(0, 0 if side == WEST else PX - 1)
        return [lambda b: pl.ds(b + at, DEEP, stride=SPAN)]
    return [at_row(spot(0 if side == SOUTH else DEEP - 1, SUB * i)) for i in range(BLOCKS)]


def edge_place(g, side, i, n):
    kept = side if side in (WEST, EAST) else 2 + (side - SOUTH) * BLOCKS + i
    return ((g * 10 + kept) * (FIELDS + 1) + n) * SUB


def step_kernel(count, patches, slots, *refs):
    u_ref, edge_ref, dx_ref, dy_ref, lanes_ref = refs[:5]
    strip_refs, out_ref = refs[5:7], refs[7]
    next_u, next_aux, next_dx, strips, doubled, coarse_ref, border_ref = refs[8:]
    lines = 4 * patches // SUB
    sets = patches // PX
    lane, sub = lane_of(), sub_of()
    block, in_block = lane // PX, lane & (PX - 1)
    turn = lax.axis_index("gy") * count

    def joined(at, join):
        return functools.reduce(join, [ref[at : at + SUB, :] for ref in strip_refs])

    for at in range(0, FIELDS * lines, SUB):
        strips[at : at + SUB, :] = joined(at, jnp.add)
    time_step = courant / jnp.max(joined(FIELDS * lines, jnp.maximum))
    part = HALF * sub + (lane & (HALF - 1))
    for t in range(4 * patches // LANE):
        tiles = []
        for v in range(t * HALF, (t + 1) * HALF):
            tile = None
            for f in range(FIELDS):
                row = jnp.broadcast_to(strips[f * lines + v : f * lines + v + 1, :], (SUB, LANE))
                wide = take_lanes(row, part)
                tile = wide if tile is None else jnp.where(lane // HALF == f, wide, tile)
            tiles.append(tile)
        cells = jnp.concatenate(tiles, axis=0).T
        for n in range(FIELDS * 2):
            for twice in range(2):
                at = t * FIELDS * PX + n * HALF + twice
                doubled[pl.ds(at, SUB, stride=2), :] = cells[n * SUB : (n + 1) * SUB, :]

    for g in range(sets):
        patch = (g * PX + in_block) ^ turn
        for side in range(4):
            t, shift = side * patches // LANE, side * patches % LANE
            for f in range(FIELDS):
                pieces = []
                for i in range(BLOCKS):
                    at = t * FIELDS * PX + f * PX + SUB * i
                    pieces.append(take_lanes(doubled[at : at + SUB, :], patch + shift))
                base = (g * FIELDS + f) * 10
                if side in (WEST, EAST):
                    x = pieces[0]
                    for q in range(1, BLOCKS):
                        x = jnp.where(block == q, pieces[q], x)
                    coarse_ref[(base + side) * SUB : (base + side + 1) * SUB, :] = x
                else:
                    for i in range(BLOCKS):
                        at = (base + 2 + (side - SOUTH) * BLOCKS + i) * SUB
                        coarse_ref[at : at + SUB, :] = pieces[i]

    size = FIELDS * DEEP * FACES
    for g in range(sets):
        for at in range(0, size, SUB):
            next_dx[g * size + at : g * size + at + SUB, :] = dx_ref[g * size + at : g * size + at + SUB, :]

        def coarse_cells(kept, axis):
            at = [((g * FIELDS + f) * 10 + kept) * SUB for f in range(FIELDS)]
            u = [coarse_ref[a : a + SUB, :] for a in at]
            return u, halves_of(u, axis)

        def own_cells(side, i):
            rows = edge_rows(side)[i]
            places = [edge_place(g, side, i, n) for n in range(FIELDS + 1)]
            u = [u_ref[rows((g * FIELDS + f) * PLANE), :] for f in range(FIELDS)]
            return u, [edge_ref[at : at + SUB, :] for at in places]

        for side, face in ((WEST, 0), (EAST, PX)):
            beyond, own = coarse_cells(side, 0), own_cells(side, 0)
            faces = face_flux(*beyond, *own) if side == WEST else face_flux(*own, *beyond)
            lacking = lanes_at(lanes_ref, g, side, 2) != 0
            for f in range(FIELDS):
                rows = pl.ds(g * size + f * DEEP * FACES + face, DEEP, stride=FACES)
                next_dx[rows, :] = jnp.where(lacking, faces[f], dx_ref[rows, :])
        for side, face in ((SOUTH, 0), (NORTH, DEEP)):
            lacking = lanes_at(lanes_ref, g, side, 2) != 0
            for i in range(BLOCKS):
                kept = (side - SOUTH) * BLOCKS + i
                beyond, own = coarse_cells(2 + kept, 1), own_cells(side, i)
                faces = face_flux(*beyond, *own) if side == SOUTH else face_flux(*own, *beyond)
                for f in range(FIELDS):
                    fine = ((g * FIELDS + f) * (DEEP + 1) + face) * PX + SUB * i
                    to = ((g * FIELDS + f) * 8 + kept) * SUB
                    border_ref[to : to + SUB, :] = jnp.where(lacking, faces[f], dy_ref[fine : fine + SUB, :])

        for f in range(FIELDS):
            for i in range(BLOCKS):
                for r in range(DEEP):
                    faces = []
                    for n in (r, r + 1):
                        if n in (0, DEEP):
                            at = ((g * FIELDS + f) * 8 + (BLOCKS if n else 0) + i) * SUB
                            faces.append(border_ref[pl.ds(pl.multiple_of(at, SUB), SUB), :])
                        else:
                            at = ((g * FIELDS + f) * (DEEP + 1) + n) * PX + SUB * i
                            faces.append(dy_ref[pl.ds(pl.multiple_of(at, SUB), SUB), :])
                    change = x_change(next_dx, g * size, f, r, i) + (faces[0] - faces[1])
                    at = pl.ds(pl.multiple_of((g * FIELDS + f) * PLANE + spot(r, SUB * i), SUB), SUB)
                    next_u[at, :] = u_ref[at, :] + time_step * change

    fill_ghosts(next_u, lanes_ref, coarse_ref, sets)
    fill_halves(next_u, next_aux, sets)
    for g in range(sets):
        fill_x_faces(next_u, next_aux, next_dx, g, g * size)

        def along(half, carry):
            for i in (2 * half, 2 * half + 1):
                low = load_cells(next_u, next_aux, g, 1, at_row(pl.multiple_of(spot(-1, SUB * i), SUB)))
                low_faces = None
                for r in range(DEEP + 1):
                    cell = load_cells(next_u, next_aux, g, 1, at_row(pl.multiple_of(spot(r, SUB * i), SUB)))
                    faces = face_flux(*low, *cell)
                    for f in range(FIELDS):
                        if r == 0:
                            continue
                        change = x_change(next_dx, g * size, f, r - 1, i) + (low_faces[f] - faces[f])
                        new = low[0][f] + time_step * change
                        at = pl.ds(pl.multiple_of((g * FIELDS + f) * PLANE + spot(r - 1, SUB * i), SUB), SUB)
                        next_u[at, :] = 0.5 * u_ref[at, :] + 0.5 * new
                    low, low_faces = cell, faces
            return carry

        lax.fori_loop(0, BLOCKS // 2, along, 0)

    held = held_at(lanes_ref, sets)
    place = jnp.maximum(held, 0) ^ turn
    pick, origin = PX * block + (place & (PX - 1)), lax.shift_right_logical(place, 5)
    for f in range(FIELDS):
        for h in range(2):
            tiles = []
            for i in range(LANE // SUB):
                at = spot(h * BLOCKS + i // BLOCKS, SUB * (i % BLOCKS))
                x = None
                for g in range(sets):
                    start = (g * FIELDS + f) * PLANE + at
                    moved = take_lanes(next_u[start : start + SUB, :], pick)
                    x = moved if x is None else jnp.where(origin == g, moved, x)
                tiles.append(jnp.where(held >= 0, x, 0.0))
            cells = jnp.concatenate(tiles, axis=0).T
            for q in range(BLOCKS):
                at = (q * 2 + h) * LANE
                out_ref[0, 0, f, :, at : at + LANE] = cells[q * PX : q * PX + slots, :]


def limit(*row_counts):
    return pltpu.CompilerParams(vmem_limit_bytes=(sum(row_counts) * LANE * 4 * 5 // 4) + (1 << 20))


def per_device(patch_state, coarse_boxes, new_owner, neighbors, coarse_box, coarse_start):
    count = patch_state.shape[2]
    n_gx, n_gz, group = lax.axis_size("gx"), lax.axis_size("gz"), lax.axis_size("gy")
    parts = n_gx * n_gz
    patches = count * group
    lines = 4 * patches // SUB
    slots = group * max(2, 2 * count // group)
    tiles = BOX_ROWS // group
    rows = -(-tiles * FIELDS // SUB) * SUB + SUB
    strip_rows = FIELDS * lines + SUB
    vmem = pl.BlockSpec(memory_space=pltpu.VMEM)
    smem = pl.BlockSpec(memory_space=pltpu.SMEM)
    f32 = jnp.float32

    def sides_first(x):
        return jnp.swapaxes(x, 2, 3)

    sets = patches // PX
    payload, raw, lanes, *cuts = pl.pallas_call(
        functools.partial(pack_kernel, tiles, rows, group, count, patches, slots, (n_gx, n_gz)),
        out_shape=(
            pltpu.VMEM((rows, LANE), f32),
            pltpu.VMEM((1, 1, FIELDS, count, SUB * LANE), f32),
            pltpu.VMEM(((sets * 4 * 3 + 1) * SUB, LANE), jnp.int32),
        )
        + (pltpu.VMEM((SUB, max(LANE, patches)), jnp.int32),) * n_gz,
        in_specs=[smem] + [vmem] * 5,
        out_specs=(vmem,) * (3 + n_gz),
        scratch_shapes=[pltpu.VMEM((SUB, LANE), jnp.int32), pltpu.SMEM((slots + 1,), jnp.int32)],
        name="pack",
    )(
        sides_first(new_owner),
        sides_first(neighbors),
        sides_first(coarse_box),
        sides_first(coarse_start),
        sides_first(patch_state),
        coarse_boxes.reshape(FIELDS * BOX_ROWS, LANE),
    )

    if power_of_two(n_gx):
        perms = [[(i, i ^ k) for i in range(n_gx)] for k in range(1, n_gx)]
    else:
        perms = [[(i, (i + k) % n_gx) for i in range(n_gx)] for k in range(1, n_gx)]
    boxes = [payload] + [lax.ppermute(payload, "gx", perm) for perm in perms]
    boxes = jnp.concatenate(boxes + [jnp.zeros((SUB * tiles, LANE), f32)], axis=0)
    cuts = cuts[:1] + [lax.ppermute(cuts[k], "gz", [(i, i ^ k) for i in range(n_gz)]) for k in range(1, n_gz)]

    strips = pl.pallas_call(
        functools.partial(strip_kernel, n_gx, n_gz, rows, tiles, patches),
        out_shape=[pltpu.VMEM((strip_rows, LANE), f32)] * n_gz,
        in_specs=[smem] * n_gz + [vmem],
        out_specs=[vmem] * n_gz,
        compiler_params=limit(n_gx * rows + SUB * tiles, n_gz * strip_rows),
        name="strips",
    )(*cuts, boxes)

    def to_group(x, after=None):
        blocks, have = [x] + [None] * (group - 1), [0]
        masks = masks_of(group)
        for mask in masks:
            perm = [(i, i ^ mask) for i in range(group)]
            for k in have:
                block = blocks[k]
                if after is not None and mask == masks[-1] and k:
                    block, _ = lax.optimization_barrier((block, after))
                blocks[k ^ mask] = lax.ppermute(block, "gy", perm)
            have = have + [k ^ mask for k in have]
        return blocks

    raws = to_group(raw, strips[-1])

    shares = [strips[0]]
    for k in reversed(range(1, n_gz * group)):
        if k // n_gz % 2 == 0:
            perm = [(i, i ^ k) for i in range(n_gz * group)]
            shares.append(lax.ppermute(strips[k % n_gz], ("gy", "gz"), perm))

    made_rows = [
        sets * FIELDS * PLANE,
        sets * 10 * (FIELDS + 1) * SUB,
        sets * FIELDS * DEEP * FACES,
        sets * FIELDS * (DEEP + 1) * PX,
    ]
    made = pl.pallas_call(
        functools.partial(prepare_kernel, group, count, patches),
        out_shape=[pltpu.VMEM((n, LANE), f32) for n in made_rows],
        in_specs=[vmem] * (1 + group),
        out_specs=[vmem] * 4,
        scratch_shapes=[pltpu.VMEM((sets * AUX * PLANE, LANE), f32)],
        compiler_params=limit(*made_rows, sets * AUX * PLANE, lanes.shape[0], patches * FIELDS * SUB),
        cost_estimate=pl.CostEstimate(flops=patches * 1024 * 300, bytes_accessed=patches * 40000, transcendentals=0),
        name="prepare",
    )(lanes, *raws)

    shares = lax.optimization_barrier(shares + [made[0]])[:-1]
    row = lax.broadcasted_iota(jnp.int32, (strip_rows, LANE), 0)
    joined = jnp.where(row < FIELDS * lines, functools.reduce(jnp.add, shares), functools.reduce(jnp.maximum, shares))

    strips = [joined, lax.ppermute(joined, "gy", [(i, i ^ 1) for i in range(group)])]
    scratch_rows = [sets * FIELDS * PLANE, sets * AUX * PLANE, sets * FIELDS * DEEP * FACES] + [
        FIELDS * lines,
        4 * patches // LANE * FIELDS * PX,
        sets * FIELDS * 10 * SUB,
        sets * FIELDS * 8 * SUB,
    ]
    out = pl.pallas_call(
        functools.partial(step_kernel, count, patches, slots),
        out_shape=jax.ShapeDtypeStruct((1, 1, FIELDS, slots, SUB * LANE), f32),
        in_specs=[vmem] * 7,
        out_specs=vmem,
        scratch_shapes=[pltpu.VMEM((n, LANE), f32) for n in scratch_rows],
        compiler_params=limit(*scratch_rows, *made_rows, lanes.shape[0], 2 * strip_rows, FIELDS * slots * SUB),
        name="step",
    )(*made, lanes, *strips)
    return sides_first(out)


def solution(mesh):
    in_specs = (
        P("gx", "gz", "gy", None, None),
        P(("gx", "gz"), None, None),
        P("gx", "gz", None, None),
        P("gx", "gz", None, None),
        P("gx", "gz", None, None),
        P("gx", "gz", None, None),
    )
    out_specs = P("gx", "gz", "gy", None, None)
    return jax.shard_map(
        per_device, mesh=mesh, in_specs=in_specs, out_specs=out_specs, check_vma=False
    )
```
